32 devices in a mesh: dp: 8 (over z, x), tensor: 4 (over y, core).
Axes of the slice: x: 2, y: 2, z: 4, core: 2. Of those that a mesh axis runs over, the one named last changes fastest.
Arguments:
- tokens: bfloat16 [16384, 768], P('dp'), may hold values from -6 to 6
- lengths: int32 [16, 8], P('dp'), may hold values from 1 to 512, 1024 in all within a row
- time: int32 [16], P('dp'), may hold values from 0 to 999
- qkv_weight: bfloat16 [768, 3, 768], P(None, None, 'tensor'), may hold values from -0.21875 to 0.21875
- out_weight: bfloat16 [768, 768], P('tensor'), may hold values from -0.625 to 0.625
- up_weight: bfloat16 [768, 3072], P(None, 'tensor'), may hold values from -0.21875 to 0.21875
- up_bias: bfloat16 [3072], P('tensor'), may hold values from -3 to 3
- down_weight: bfloat16 [3072, 768], P('tensor'), may hold values from -0.109375 to 0.109375
- down_bias: bfloat16 [768], replicated, may hold values from -3 to 3
- gain_attn: bfloat16 [768], replicated, may hold values from 0.5 to 1.5
- gain_mlp: bfloat16 [768], replicated, may hold values from 0.5 to 1.5
- ada_weight: bfloat16 [128, 6, 768], replicated, may hold values from -0.5 to 0.5
- ada_bias: bfloat16 [6, 768], replicated, may hold values from -3 to 3
- cotangent: bfloat16 [16384, 768], P('dp'), may hold values from -6 to 6
Outputs:
- output: bfloat16 [16384, 768], P('dp')
- grad_tokens: bfloat16 [16384, 768], P('dp')
- grad_qkv_weight: float32 [768, 3, 768], P(None, None, 'tensor')
- grad_out_weight: float32 [768, 768], P('tensor')
- grad_up_weight: float32 [768, 3072], P(None, 'tensor')
- grad_up_bias: float32 [3072], P('tensor')
- grad_down_weight: float32 [3072, 768], P('tensor')
- grad_down_bias: float32 [768], replicated
- grad_gain_attn: float32 [768], replicated
- grad_gain_mlp: float32 [768], replicated
- grad_ada_weight: float32 [128, 6, 768], replicated
- grad_ada_bias: float32 [6, 768], replicated
The draws below stay inside these ranges and needn't reach their ends.
Inputs may be any that keep to these rules, and one draw needn't show every extreme that they name: `lengths`: in each slot the longest document has exactly 512 tokens.
All inputs are finite; a program needn't handle non-finite values.
Results may differ from the reference program's by a relative error of at most 0.02.
Values may be sent and summed in bfloat16 or wider, within the bound.
A program may use at most 192 MiB of HBM per device.

```python
import math
import jax
import jax.numpy as jnp
import numpy as np
from jax import lax

D = 768
HEADS = 12
HEAD_DIM = 64
FF = 3072
COND = 128
SLOT_LEN = 1024
DOCS = 8
TSTEPS = 1000
SLOTS = 16
TOKENS = 16384
N_TENSOR = 4


def with_ends(values, own_key, smallest, largest):
    longest = values.shape.index(max(values.shape))
    spots = []
    for shift in (0, 1):
        where = [jax.random.randint(jax.random.fold_in(own_key, axis), (), 0, length) for axis, length in enumerate(values.shape)]
        where[longest] = (where[longest] + shift) % values.shape[longest]
        spots.append(tuple(where))
    return values.at[spots[0]].set(smallest).at[spots[1]].set(largest)


def level_of(rng, extent, cuts, smallest, largest):
    def one(dim, shards_of):
        steps = jax.random.uniform(jax.random.fold_in(jax.random.fold_in(rng, 6), dim), (shards_of,), jnp.float32, smallest / len(cuts), largest / len(cuts))
        return jnp.repeat(jnp.exp(steps), extent[dim] // shards_of).reshape((-1,) + (1,) * (len(extent) - dim - 1))

    loudness = one(*cuts[0])
    for cut in cuts[1:]:
        loudness = loudness * one(*cut)
    return loudness


def length_profile(amount, total, most, skew):
    loads = [(1 << 20) // math.isqrt(standing ** skew) + 1 for standing in range(2, amount + 1)]
    spare, holding = total - most - (amount - 1), [1] * (amount - 1)
    while spare > 0:
        candidates = [i for i in range(amount - 1) if holding[i] < most]
        whole, budget = sum([loads[i] for i in candidates]), spare
        for i in candidates:
            extra = min(most - holding[i], max(1, budget * loads[i] // whole), spare)
            holding[i] = holding[i] + extra
            spare = spare - extra
    return np.array([most] + holding)


def uneven_parts(rng, number_of, total, limit, slope):
    if number_of == 2:
        one = jax.random.randint(rng, (), max(1, total - limit), min(limit, total - 1) + 1)
        return jnp.stack([one, total - one])
    tallies = jnp.asarray(length_profile(number_of, total, limit, slope), jnp.int32)
    twos = (number_of - 1) // 2
    donor, taker = tallies[1:1 + 2 * twos:2], tallies[2:2 + 2 * twos:2]
    margin = jnp.minimum(donor - 1, limit - taker)
    moved = jax.random.randint(jax.random.fold_in(rng, 1), (twos,), 0, 1 << 20) % (margin + 1)
    tallies = tallies.at[1:1 + 2 * twos:2].set(donor - moved).at[2:2 + 2 * twos:2].set(taker + moved)
    return tallies[jax.random.permutation(jax.random.fold_in(rng, 2), number_of)]


def noise(rng, dims, scale, reach, split=(), kind=jnp.bfloat16):
    drawn = scale * jax.random.normal(rng, dims, jnp.float32)
    if split:
        drawn = drawn * level_of(rng, dims, split, -0.22, 0.18)
    return jnp.clip(drawn, -reach, reach).astype(kind)


def setup_inputs(seed: int = 0) -> dict:
    arg_keys = jax.random.split(jax.random.key(seed), 15)
    return {
        "tokens": noise(arg_keys[0], (TOKENS, D), 1.0, 6.0, ((0, 8),)),
        "lengths": jax.vmap(lambda own: uneven_parts(own, DOCS, SLOT_LEN, SLOT_LEN // 2, 2))(jax.random.split(arg_keys[1], SLOTS)).reshape((SLOTS, DOCS)).astype(jnp.int32),
        "time": with_ends(jax.random.randint(arg_keys[2], (SLOTS,), 0, TSTEPS), jax.random.fold_in(arg_keys[2], 1), 0, TSTEPS - 1).astype(jnp.int32),
        "qkv_weight": noise(arg_keys[3], (D, 3, D), D ** -0.5, 0.21875, ((2, 4),)),
        "out_weight": noise(arg_keys[4], (D, D), (D // 8) ** -0.5, 0.625, ((0, 4),)),
        "up_weight": noise(arg_keys[5], (D, FF), D ** -0.5, 0.21875, ((1, 4),)),
        "up_bias": noise(arg_keys[6], (FF,), 0.5, 3.0, ((0, 4),)),
        "down_weight": noise(arg_keys[7], (FF, D), FF ** -0.5, 0.109375, ((0, 4),)),
        "down_bias": noise(arg_keys[8], (D,), 0.5, 3.0),
        "gain_attn": jnp.clip(1.0 + 0.1 * jax.random.normal(arg_keys[9], (D,), jnp.float32), 0.5, 1.5).astype(jnp.bfloat16),
        "gain_mlp": jnp.clip(1.0 + 0.1 * jax.random.normal(arg_keys[10], (D,), jnp.float32), 0.5, 1.5).astype(jnp.bfloat16),
        "ada_weight": noise(arg_keys[11], (COND, 6, D), COND ** -0.5, 0.5),
        "ada_bias": noise(arg_keys[12], (6, D), 0.5, 3.0),
        "cotangent": noise(arg_keys[13], (TOKENS, D), 1.0, 6.0, ((0, 8),)),
    }


@jax.custom_vjp
def low(v):
    return lax.optimization_barrier(v.astype(jnp.bfloat16)).astype(jnp.float32)

@jax.custom_vjp
def low_back(v):
    return v

def low_keep(v):
    return (low(v), None)

def low_pass(kept, grad):
    return (grad,)

def back_keep(v):
    return (v, None)

def back_low(kept, grad):
    return (low(grad),)
low.defvjp(low_keep, low_pass)
low_back.defvjp(back_keep, back_low)

def norm_mod(inputs, gain, shift_mod, scale_mod):
    center = lax.optimization_barrier(jnp.mean(inputs, axis=-1, keepdims=True))
    centered = inputs - center
    spread = lax.optimization_barrier(jnp.mean(centered * centered, axis=-1, keepdims=True))
    return centered * lax.rsqrt(spread + 1e-05) * gain * (1.0 + scale_mod) + shift_mod

def rotary_tables(position, head_width):
    half_width = head_width // 2
    inverse = jnp.exp(jnp.arange(half_width, dtype=jnp.float32) * (-2.0 * math.log(10000.0) / head_width))
    angles = position.astype(jnp.float32)[..., None] * inverse
    cosines = jnp.concatenate([jnp.cos(angles), jnp.cos(angles)], axis=-1)[..., None, :]
    sines = jnp.concatenate([jnp.sin(angles), jnp.sin(angles)], axis=-1)[..., None, :]
    return (cosines, sines)

def rotate(values_in, cosines, sines):
    half_width = values_in.shape[-1] // 2
    turned = jnp.concatenate([-values_in[..., half_width:], values_in[..., :half_width]], axis=-1)
    return values_in * cosines + turned * sines

def time_features(steps_in, width):
    half_width = width // 2
    frequency = jnp.exp(jnp.arange(half_width, dtype=jnp.float32) * (-math.log(10000.0) / half_width))
    angles = steps_in.astype(jnp.float32)[:, None] * frequency[None, :]
    return jnp.concatenate([jnp.cos(angles), jnp.sin(angles)], axis=-1)

def doc_layout(lengths_row, count):
    doc_ends = jnp.cumsum(lengths_row).astype(jnp.int32)
    places = jnp.arange(count, dtype=jnp.int32)
    passed = (places[:, None] >= doc_ends[None, :]).astype(jnp.int32)
    segment = lax.optimization_barrier(jnp.sum(passed, axis=1)).astype(jnp.int32)
    starts = lax.optimization_barrier(jnp.sum(passed * lengths_row[None, :], axis=1)).astype(jnp.int32)
    return (segment, places - starts)

def slot_forward(params, inputs, segment, position, features):
    qkv_w, out_w, up_w, up_b, down_w, down_b, gain_one, gain_two, ada_w, ada_b = params
    precise = lax.Precision.HIGHEST
    modulation = jnp.dot(features, ada_w.reshape(COND, 6 * D), precision=precise).reshape(6, D) + ada_b
    normed = low(norm_mod(inputs, gain_one, modulation[0], modulation[1]))
    projected = low_back(jnp.dot(normed, qkv_w.reshape(D, 3 * D), precision=precise))
    projected = projected.reshape(SLOT_LEN, 3, HEADS, HEAD_DIM)
    cosines, sines = rotary_tables(position, HEAD_DIM)
    queries = low(rotate(projected[:, 0], cosines, sines))
    key_heads = low(rotate(projected[:, 1], cosines, sines))
    value_heads = low(projected[:, 2])
    scores = jnp.einsum('qhd,khd->hqk', queries, key_heads, precision=precise) * (1.0 / math.sqrt(HEAD_DIM))
    allowed = segment[:, None] == segment[None, :]
    scores = low_back(jnp.where(allowed[None], scores, -1000000000.0))
    highest = lax.optimization_barrier(jnp.max(scores, axis=-1, keepdims=True))
    exp_terms = jnp.exp(scores - highest)
    attn_weights = exp_terms / lax.optimization_barrier(jnp.sum(exp_terms, axis=-1, keepdims=True))
    attended = jnp.einsum('hqk,khd->qhd', low(attn_weights), value_heads, precision=precise)
    attended = low_back(low(attended)).reshape(SLOT_LEN, N_TENSOR, D // N_TENSOR)
    partial_out = jnp.einsum('lgc,gcd->lgd', attended, out_w.reshape(N_TENSOR, D // N_TENSOR, D), precision=precise)
    branch = low_back(lax.optimization_barrier(jnp.sum(low(partial_out), axis=1)))
    middle = inputs + modulation[2] * branch
    normed_two = low(norm_mod(middle, gain_two, modulation[3], modulation[4]))
    hidden_pre = low_back(jnp.dot(normed_two, up_w, precision=precise) + up_b)
    hidden_act = low(jax.nn.gelu(hidden_pre, approximate=True)).reshape(SLOT_LEN, N_TENSOR, FF // N_TENSOR)
    partial_mlp = jnp.einsum('lgc,gcd->lgd', hidden_act, down_w.reshape(N_TENSOR, FF // N_TENSOR, D), precision=precise)
    mlp_out = low_back(lax.optimization_barrier(jnp.sum(low(partial_mlp), axis=1))) + down_b
    return middle + modulation[5] * mlp_out

def reference(tokens, lengths, time, qkv_weight, out_weight, up_weight, up_bias, down_weight, down_bias, gain_attn, gain_mlp, ada_weight, ada_bias, cotangent):
    params = tuple((weight_in.astype(jnp.float32) for weight_in in (qkv_weight, out_weight, up_weight, up_bias, down_weight, down_bias, gain_attn, gain_mlp, ada_weight, ada_bias)))
    inputs = tokens.astype(jnp.float32).reshape(SLOTS, SLOT_LEN, D)
    segments, positions = jax.vmap(lambda lengths_row: doc_layout(lengths_row, SLOT_LEN))(lengths)
    features = time_features(time, COND)
    slot_step = jax.checkpoint(slot_forward)

    def forward(weights_all, inputs_all):

        def scan_body(carry, pieces):
            return (carry, slot_step(weights_all, pieces[0], pieces[1], pieces[2], pieces[3]))
        unused, outputs = lax.scan(scan_body, jnp.zeros((), jnp.float32), (inputs_all, segments, positions, features))
        return outputs
    outputs, pull_back = jax.vjp(forward, params, inputs)
    weight_grads, input_grads = pull_back(cotangent.astype(jnp.float32).reshape(SLOTS, SLOT_LEN, D))
    grad_qkv, grad_out, grad_up, grad_up_b, grad_down, grad_down_b, grad_gain_one, grad_gain_two, grad_ada_w, grad_ada_b = weight_grads
    return (outputs.reshape(TOKENS, D).astype(jnp.bfloat16), input_grads.reshape(TOKENS, D).astype(jnp.bfloat16), grad_qkv, grad_out, grad_up, grad_up_b, grad_down, grad_down_b, grad_gain_one, grad_gain_two, grad_ada_w, grad_ada_b)
```

```python
import functools
import math

import jax
import jax.numpy as jnp
from jax import lax
from jax.experimental import pallas as pl
from jax.experimental.pallas import tpu as pltpu
from jax.sharding import PartitionSpec as P

HEAD_DIM = 64
HALF = HEAD_DIM // 2
EPS = 1e-05
ROWS = 256
PRECISE = lax.Precision.HIGHEST
VMEM_LIMIT = 60 * 1024 * 1024
F32 = jnp.float32
BF16 = jnp.bfloat16
GELU_A = math.sqrt(2.0 / math.pi)
GELU_B = 0.044715

NN = (((1,), (0,)), ((), ()))
NT = (((1,), (1,)), ((), ()))
TN = (((0,), (0,)), ((), ()))


def mm(left, right, dims=NN):
    return lax.dot_general(left, right, dims, preferred_element_type=F32)


def params(**more):
    return pltpu.CompilerParams(vmem_limit_bytes=VMEM_LIMIT, **more)


def whole(shape):
    zeros = (0,) * len(shape)
    return pl.BlockSpec(shape, lambda *_: zeros)


def norm_parts(v):
    center = jnp.mean(v, axis=-1, keepdims=True)
    centered = v - center
    spread = jnp.mean(centered * centered, axis=-1, keepdims=True)
    rstd = lax.rsqrt(spread + EPS)
    return centered * rstd, rstd


def join_heads(own_ref, par_ref, part, width):
    rows = slice(part * width, (part + 1) * width)
    return jnp.concatenate([own_ref[rows, :], par_ref[rows, :]], axis=0)


def qkv_kernel(core, tok, gain, mod, own, par, cos, sin, normed_o, qt_o, kt_o, vt_o, q_o, k_o, v_o):
    width = own.shape[0] // 3
    xhat, _ = norm_parts(tok[...].astype(F32))
    normed = (xhat * gain[...] * (1.0 + mod[1:2, :]) + mod[0:1, :]).astype(BF16)
    normed_o[...] = normed
    c, s = cos[...], sin[...]
    for part, (t_o, r_o) in enumerate(((qt_o, q_o), (kt_o, k_o), (vt_o, v_o))):
        turned = mm(join_heads(own, par, part, width), normed, NT)
        if part < 2:
            pieces = []
            for h in range(2 * width // HEAD_DIM):
                a = turned[h * HEAD_DIM : h * HEAD_DIM + HALF]
                b = turned[h * HEAD_DIM + HALF : (h + 1) * HEAD_DIM]
                pieces += [a * c - b * s, b * c + a * s]
            turned = jnp.concatenate(pieces, axis=0)
        if part == 0:
            turned = turned * (1.0 / math.sqrt(HEAD_DIM))
        t_o[...] = turned.astype(BF16)
        r_o[...] = turned.T.astype(BF16)


def qkv_call(core, tokens, gain, mod, own, par, cos, sin, length):
    width, model = 2 * own.shape[0] // 3, tokens.shape[1]
    steps = length // ROWS
    col = pl.BlockSpec((width, ROWS), lambda i, c: (0, i))
    row = pl.BlockSpec((ROWS, width), lambda i, c: (i, 0))
    table = pl.BlockSpec((HALF, ROWS), lambda i, c: (0, i))
    return pl.pallas_call(
        qkv_kernel,
        grid_spec=pltpu.PrefetchScalarGridSpec(
            num_scalar_prefetch=1,
            grid=(steps,),
            in_specs=[
                pl.BlockSpec((ROWS, model), lambda i, c: (c[0] * steps + i, 0)),
                whole(gain.shape),
                whole(mod.shape),
                whole(own.shape),
                whole(par.shape),
                table,
                table,
            ],
            out_specs=[pl.BlockSpec((ROWS, model), lambda i, c: (i, 0))] + [col] * 3 + [row] * 3,
        ),
        out_shape=[jax.ShapeDtypeStruct((length, model), BF16)]
        + [jax.ShapeDtypeStruct((width, length), BF16)] * 3
        + [jax.ShapeDtypeStruct((length, width), BF16)] * 3,
        compiler_params=params(),
        name="norm_qkv",
    )(core, tokens, gain, mod, own, par, cos, sin)


def only_half(block, second):
    zero = jnp.zeros_like(block)
    return jnp.concatenate([zero, block] if second else [block, zero], axis=0)


def doc_mask(lo_ref, hi_ref, keys):
    place = lax.broadcasted_iota(jnp.int32, (keys, lo_ref.shape[1]), 0)
    return (place >= lo_ref[...]) & (place < hi_ref[...])


def att_kernel(qt, k, vt, lo, hi, own, par, at_o, stat_o, br_o):
    heads = qt.shape[0] // HEAD_DIM
    allowed = doc_mask(lo, hi, k.shape[0])
    for h in range(heads):
        pair = slice((h // 2) * 2 * HEAD_DIM, (h // 2 + 1) * 2 * HEAD_DIM)
        mine = slice(h * HEAD_DIM, (h + 1) * HEAD_DIM)
        scores = mm(k[:, pair], only_half(qt[mine, :], h % 2))
        scores = jnp.where(allowed, scores, -1000000000.0)
        top = jnp.max(scores, axis=0, keepdims=True)
        terms = jnp.exp(scores - top)
        inv = 1.0 / jnp.sum(terms, axis=0, keepdims=True)
        out = mm(vt[mine, :], (terms * inv).astype(BF16))
        at_o[mine, :] = out.astype(BF16)
        stat_o[h : h + 1, :] = top
        stat_o[8 + h : 9 + h, :] = inv
    weight = jnp.concatenate([own[...], par[...]], axis=0)
    br_o[...] = mm(at_o[...], weight, TN).astype(BF16)


def att_call(qt, k, vt, lo, hi, own, par, half, halves):
    width, length = qt.shape
    model = own.shape[1]
    steps = length // ROWS // halves
    first = half * steps
    col = pl.BlockSpec((width, ROWS), lambda i: (0, first + i))
    bound = pl.BlockSpec((1, ROWS), lambda i: (0, first + i))
    span = steps * ROWS
    return pl.pallas_call(
        att_kernel,
        grid=(steps,),
        in_specs=[col, whole(k.shape), whole(vt.shape), bound, bound, whole(own.shape), whole(par.shape)],
        out_specs=[
            pl.BlockSpec((width, ROWS), lambda i: (0, i)),
            pl.BlockSpec((16, ROWS), lambda i: (0, i)),
            pl.BlockSpec((ROWS, model), lambda i: (i, 0)),
        ],
        out_shape=[
            jax.ShapeDtypeStruct((width, span), BF16),
            jax.ShapeDtypeStruct((16, span), F32),
            jax.ShapeDtypeStruct((span, model), BF16),
        ],
        compiler_params=params(),
        cost_estimate=pl.CostEstimate(flops=10_000_000_000, bytes_accessed=4_000_000, transcendentals=0),
        name="attend",
    )(qt, k, vt, lo, hi, own, par)


def mlp_kernel(
    core, tok, cot, br_own, br_par, gain, mod, up0, up1, bias, down0, down1,
    n2_o, act_o, pre_o, gml_o, out_o, gn_o,
):
    middle = tok[...].astype(F32) + mod[2:3, :] * (br_own[...].astype(F32) + br_par[...].astype(F32))
    xhat, _ = norm_parts(middle)
    normed = (xhat * gain[...] * (1.0 + mod[4:5, :]) + mod[3:4, :]).astype(BF16)
    n2_o[...] = normed
    gml = (mod[5:6, :] * cot[...].astype(F32)).astype(BF16)
    gml_o[...] = gml
    part = jnp.zeros(tok.shape, F32)
    grad = jnp.zeros(tok.shape, F32)
    hidden = up0.shape[1]
    for n, (up, down) in enumerate(((up0, down0), (up1, down1))):
        cols = slice(n * hidden, (n + 1) * hidden)
        v = mm(normed, up[...]) + bias[n : n + 1, :]
        square = v * v
        t = jnp.tanh(GELU_A * v * (1.0 + GELU_B * square))
        act = (0.5 * v * (1.0 + t)).astype(BF16)
        act_o[:, cols] = act
        slope = 0.5 * (1.0 + t) + (0.5 * GELU_A) * v * (1.0 - t * t) * (1.0 + 3.0 * GELU_B * square)
        part = part + mm(act, down[...])
        pre = (mm(gml, down[...], NT) * slope).astype(BF16)
        pre_o[:, cols] = pre
        grad = grad + mm(pre, up[...], NT)
    out_o[...] = part.astype(BF16)
    gn_o[...] = grad.astype(BF16)


def mlp_call(core, tokens, cot, br_own, br_par, gain, mod, up0, up1, bias, down0, down1, half, halves, length):
    model, hidden = up0.shape
    steps = length // ROWS // halves
    span = steps * ROWS
    mine = pl.BlockSpec((ROWS, model), lambda i, c: (c[0] * steps * halves + half * steps + i, 0))
    row = pl.BlockSpec((ROWS, model), lambda i, c: (i, 0))
    wide = pl.BlockSpec((ROWS, 2 * hidden), lambda i, c: (i, 0))
    return pl.pallas_call(
        mlp_kernel,
        grid_spec=pltpu.PrefetchScalarGridSpec(
            num_scalar_prefetch=1,
            grid=(steps,),
            in_specs=[mine, mine, row, row]
            + [whole(a.shape) for a in (gain, mod, up0, up1, bias, down0, down1)],
            out_specs=[row, wide, wide, row, row, row],
        ),
        out_shape=[jax.ShapeDtypeStruct((span, w), BF16) for w in (model, 2 * hidden, 2 * hidden, model, model, model)],
        compiler_params=params(),
        cost_estimate=pl.CostEstimate(flops=6_000_000_000, bytes_accessed=8_000_000, transcendentals=0),
        name="mlp",
    )(core, tokens, cot, br_own, br_par, gain, mod, up0, up1, bias, down0, down1)


def att_back_kernel(
    core, tok, cot, br_own, br_par, gn_own, gn_par, gain, mod, own, par,
    qt, q, k, kt, v, lo, hi, stat, cos, sin, dk_in, dv_in,
    gmid_o, gb_o, sums_o, gq_o, dk_o, dv_o,
):
    heads = qt.shape[0] // HEAD_DIM

    @pl.when(pl.program_id(0) == 0)
    def _():
        sums_o[...] = jnp.zeros_like(sums_o)
        dk_o[...] = dk_in[...]
        dv_o[...] = dv_in[...]

    branch = br_own[...].astype(F32) + br_par[...].astype(F32)
    xhat, rstd = norm_parts(tok[...].astype(F32) + mod[2:3, :] * branch)
    gn = gn_own[...].astype(F32) + gn_par[...].astype(F32)
    y = gn * ((1.0 + mod[4:5, :]) * gain[...])
    gn_x = gn * xhat
    mean_y = jnp.mean(y, axis=-1, keepdims=True)
    mean_yx = jnp.mean(y * xhat, axis=-1, keepdims=True)
    grad_out = cot[...].astype(F32)
    gmid = grad_out + rstd * (y - mean_y - xhat * mean_yx)
    gmid_o[...] = gmid
    sums_o[0:1, :] += jnp.sum(gn, axis=0, keepdims=True)
    sums_o[1:2, :] += jnp.sum(gn_x, axis=0, keepdims=True)
    sums_o[2:3, :] += jnp.sum(gmid * branch, axis=0, keepdims=True)
    sums_o[3:4, :] += jnp.sum(grad_out, axis=0, keepdims=True)
    gb = (mod[2:3, :] * gmid).astype(BF16)
    gb_o[...] = gb
    weight = jnp.concatenate([own[...], par[...]], axis=0)
    do_t = mm(weight, gb, NT).astype(BF16)
    do = mm(gb, weight, NT).astype(BF16)
    allowed = doc_mask(lo, hi, k.shape[0])
    lane = lax.broadcasted_iota(jnp.int32, (ROWS, 2 * HEAD_DIM), 1)
    c, s = cos[...], sin[...]
    for p in range(heads // 2):
        pair = slice(p * 2 * HEAD_DIM, (p + 1) * 2 * HEAD_DIM)
        dk_sum, dv_sum = dk_o[:, pair], dv_o[:, pair]
        for n in range(2):
            h = 2 * p + n
            mine = slice(h * HEAD_DIM, (h + 1) * HEAD_DIM)
            scores = mm(k[:, pair], only_half(qt[mine, :], n))
            probs = jnp.where(allowed, jnp.exp(scores - stat[h : h + 1, :]), 0.0) * stat[8 + h : 9 + h, :]
            grad_p = mm(v[:, pair], only_half(do_t[mine, :], n))
            centre = jnp.sum(probs * grad_p, axis=0, keepdims=True)
            grad_s = (probs * (grad_p - centre)).astype(BF16)
            dq = mm(kt[mine, :], grad_s) * (1.0 / math.sqrt(HEAD_DIM))
            ua, ub = dq[:HALF], dq[HALF:]
            gq_o[h * HEAD_DIM : h * HEAD_DIM + HALF, :] = (ua * c + ub * s).astype(BF16)
            gq_o[h * HEAD_DIM + HALF : (h + 1) * HEAD_DIM, :] = (ub * c - ua * s).astype(BF16)
            here = (lane >= HEAD_DIM) if n else (lane < HEAD_DIM)
            none = jnp.zeros((ROWS, 2 * HEAD_DIM), BF16)
            dk_sum = dk_sum + mm(grad_s, jnp.where(here, q[:, pair], none))
            dv_sum = dv_sum + mm(probs.astype(BF16), jnp.where(here, do[:, pair], none))
        dk_o[:, pair] = dk_sum
        dv_o[:, pair] = dv_sum


def att_back_call(
    core, tokens, cot, br_own, br_par, gn_own, gn_par, gain, mod, own, par,
    qt, q, k, kt, v, lo, hi, stat, cos, sin, dk_in, dv_in, half, halves,
):
    width, length = qt.shape
    model = own.shape[1]
    steps = length // ROWS // halves
    first = half * steps
    span = steps * ROWS
    mine = pl.BlockSpec((ROWS, model), lambda i, c: (c[0] * steps * halves + first + i, 0))
    row = pl.BlockSpec((ROWS, model), lambda i, c: (i, 0))

    def lanes(height, start=first):
        return pl.BlockSpec((height, ROWS), lambda i, c: (0, start + i))

    sums = (8, model)
    return pl.pallas_call(
        att_back_kernel,
        grid_spec=pltpu.PrefetchScalarGridSpec(
            num_scalar_prefetch=1,
            grid=(steps,),
            in_specs=[mine, mine, row, row, row, row]
            + [whole(a.shape) for a in (gain, mod, own, par)]
            + [lanes(width), pl.BlockSpec((ROWS, width), lambda i, c: (first + i, 0))]
            + [whole(a.shape) for a in (k, kt, v)]
            + [lanes(1), lanes(1), lanes(16, 0), lanes(HALF), lanes(HALF)]
            + [whole(dk_in.shape), whole(dv_in.shape)],
            out_specs=[row, row, whole(sums), lanes(width, 0), whole(dk_in.shape), whole(dv_in.shape)],
        ),
        out_shape=[
            jax.ShapeDtypeStruct((span, model), F32),
            jax.ShapeDtypeStruct((span, model), BF16),
            jax.ShapeDtypeStruct(sums, F32),
            jax.ShapeDtypeStruct((width, span), BF16),
            jax.ShapeDtypeStruct(dk_in.shape, F32),
            jax.ShapeDtypeStruct(dv_in.shape, F32),
        ],
        compiler_params=params(),
        cost_estimate=pl.CostEstimate(flops=20_000_000_000, bytes_accessed=8_000_000, transcendentals=0),
        name="attend_back",
    )(core, tokens, cot, br_own, br_par, gn_own, gn_par, gain, mod, own, par,
      qt, q, k, kt, v, lo, hi, stat, cos, sin, dk_in, dv_in)


def qkv_back_kernel(core, tok, gq, dk, dv, own, par, cos, sin, g_o, gn_o, sums_o):
    width = own.shape[0] // 3

    @pl.when(pl.program_id(0) == 0)
    def _():
        sums_o[...] = jnp.zeros_like(sums_o)

    c, s = cos[...], sin[...]
    turned = dk[...].T
    pieces = []
    for h in range(2 * width // HEAD_DIM):
        ua = turned[h * HEAD_DIM : h * HEAD_DIM + HALF]
        ub = turned[h * HEAD_DIM + HALF : (h + 1) * HEAD_DIM]
        pieces += [ua * c + ub * s, ub * c - ua * s]
    gk = jnp.concatenate(pieces, axis=0).astype(BF16)
    gv = dv[...].T.astype(BF16)
    grads = (gq[...], gk, gv)
    gn = jnp.zeros(tok.shape, F32)
    for part in range(3):
        g_o[part * 2 * width : (part + 1) * 2 * width, :] = grads[part]
        gn = gn + mm(grads[part], join_heads(own, par, part, width), TN)
    gn_o[...] = gn.astype(BF16)
    xhat, _ = norm_parts(tok[...].astype(F32))
    sums_o[0:1, :] += jnp.sum(gn, axis=0, keepdims=True)
    sums_o[1:2, :] += jnp.sum(gn * xhat, axis=0, keepdims=True)


def qkv_back_call(core, tokens, gq, dk, dv, own, par, cos, sin):
    length, width = dk.shape
    model = tokens.shape[1]
    steps = length // ROWS

    def lanes(height):
        return pl.BlockSpec((height, ROWS), lambda i, c: (0, i))

    rows = pl.BlockSpec((ROWS, width), lambda i, c: (i, 0))
    sums = (8, model)
    return pl.pallas_call(
        qkv_back_kernel,
        grid_spec=pltpu.PrefetchScalarGridSpec(
            num_scalar_prefetch=1,
            grid=(steps,),
            in_specs=[
                pl.BlockSpec((ROWS, model), lambda i, c: (c[0] * steps + i, 0)),
                lanes(width), rows, rows, whole(own.shape), whole(par.shape), lanes(HALF), lanes(HALF),
            ],
            out_specs=[lanes(3 * width), pl.BlockSpec((ROWS, model), lambda i, c: (i, 0)), whole(sums)],
        ),
        out_shape=[
            jax.ShapeDtypeStruct((3 * width, length), BF16),
            jax.ShapeDtypeStruct((length, model), BF16),
            jax.ShapeDtypeStruct(sums, F32),
        ],
        compiler_params=params(),
        name="qkv_back",
    )(core, tokens, gq, dk, dv, own, par, cos, sin)


def tokens_kernel(core, tok, gn_own, gn_par, gmid, gain, mod, out_o):
    xhat, rstd = norm_parts(tok[...].astype(F32))
    gn = gn_own[...].astype(F32) + gn_par[...].astype(F32)
    y = gn * ((1.0 + mod[1:2, :]) * gain[...])
    mean_y = jnp.mean(y, axis=-1, keepdims=True)
    mean_yx = jnp.mean(y * xhat, axis=-1, keepdims=True)
    out_o[...] = (gmid[...] + rstd * (y - mean_y - xhat * mean_yx)).astype(BF16)


def tokens_call(core, tokens, gn_own, gn_par, gmid, gain, mod):
    length, model = gn_own.shape
    steps = length // ROWS
    row = pl.BlockSpec((ROWS, model), lambda i, c: (i, 0))
    return pl.pallas_call(
        tokens_kernel,
        grid_spec=pltpu.PrefetchScalarGridSpec(
            num_scalar_prefetch=1,
            grid=(steps,),
            in_specs=[
                pl.BlockSpec((ROWS, model), lambda i, c: (c[0] * steps + i, 0)),
                row, row, row, whole(gain.shape), whole(mod.shape),
            ],
            out_specs=row,
        ),
        out_shape=jax.ShapeDtypeStruct((length, model), BF16),
        compiler_params=params(),
        name="grad_tokens",
    )(core, tokens, gn_own, gn_par, gmid, gain, mod)


def output_kernel(core, tok, cot, br_own, br_par, ml_own, ml_par, mod, bias, out_o, sums_o):
    @pl.when(pl.program_id(0) == 0)
    def _():
        sums_o[...] = jnp.zeros_like(sums_o)

    middle = tok[...].astype(F32) + mod[2:3, :] * (br_own[...].astype(F32) + br_par[...].astype(F32))
    mlp_out = ml_own[...].astype(F32) + ml_par[...].astype(F32) + bias[...]
    out_o[...] = (middle + mod[5:6, :] * mlp_out).astype(BF16)
    sums_o[0:1, :] += jnp.sum(cot[...].astype(F32) * mlp_out, axis=0, keepdims=True)


def output_call(core, tokens, cot, br_own, br_par, ml_own, ml_par, mod, bias, half, halves):
    span, model = br_own.shape
    steps = span // ROWS
    row = pl.BlockSpec((ROWS, model), lambda i, c: (i, 0))
    mine = pl.BlockSpec((ROWS, model), lambda i, c: (c[0] * steps * halves + half * steps + i, 0))
    sums = (8, model)
    return pl.pallas_call(
        output_kernel,
        grid_spec=pltpu.PrefetchScalarGridSpec(
            num_scalar_prefetch=1,
            grid=(steps,),
            in_specs=[mine, mine, row, row, row, row, whole(mod.shape), whole(bias.shape)],
            out_specs=[row, whole(sums)],
        ),
        out_shape=[jax.ShapeDtypeStruct((span, model), BF16), jax.ShapeDtypeStruct(sums, F32)],
        compiler_params=params(),
        name="block_output",
    )(core, tokens, cot, br_own, br_par, ml_own, ml_par, mod, bias)


def swap(array, axis, bit, size):
    return lax.ppermute(array, axis, [(i, i ^ bit) for i in range(size)])


def place_pair(mine, other, second):
    lower = jnp.where(second, other, mine)
    upper = jnp.where(second, mine, other)
    return jnp.concatenate([lower, upper], axis=0)


def all_reduce(array, axis, size, order):
    me = lax.axis_index(axis)
    for bit in order:
        rows = array.shape[0] // 2
        second = (me >> bit) & 1
        keep = lax.dynamic_slice_in_dim(array, second * rows, rows)
        send = lax.dynamic_slice_in_dim(array, (1 - second) * rows, rows)
        got = swap(send, axis, 1 << bit, size)
        array = (keep.astype(F32) + got.astype(F32)).astype(array.dtype)
    for bit in reversed(order):
        other = swap(array, axis, 1 << bit, size)
        array = place_pair(array, other, ((me >> bit) & 1) == 1)
    return array


def all_reduce_two(array, axis, size):
    bits = list(range(size.bit_length() - 1))
    rows = array.shape[0] // 2
    first = all_reduce(array[:rows], axis, size, bits)
    second = all_reduce(array[rows:], axis, size, bits[1:] + bits[:1])
    return jnp.concatenate([first, second], axis=0)


def gather_slots(row, dp):
    out = row[None]
    tensor = lax.axis_index("tensor")
    out = place_pair(out, swap(out, "tensor", 1, 4), (tensor & 1) == 1)
    me = lax.axis_index("dp")
    for bit in range(dp.bit_length() - 1):
        out = place_pair(out, swap(out, "dp", 1 << bit, dp), ((me >> bit) & 1) == 1)
    return out


def doc_bounds(lengths_row, count):
    ends = jnp.cumsum(lengths_row)
    places = jnp.arange(count, dtype=jnp.int32)
    passed = (places[None, :] >= ends[:, None]).astype(jnp.int32)
    starts = jnp.sum(passed * lengths_row[:, None], axis=0)
    segment = jnp.sum(passed, axis=0)
    member = segment[None, :] == jnp.arange(lengths_row.shape[0])[:, None]
    own = jnp.sum(jnp.where(member, lengths_row[:, None], 0), axis=0)
    return starts, starts + own


def per_device(
    dp, tokens, lengths, time, qkv_weight, out_weight, up_weight, up_bias, down_weight, down_bias,
    gain_attn, gain_mlp, ada_weight, ada_bias, cotangent,
):
    slot_count, model = time.shape[0], tokens.shape[1]
    length = tokens.shape[0] // slot_count
    local = out_weight.shape[0]
    cond = ada_weight.shape[0]
    halves = 2
    core = lax.axis_index("tensor") & 1
    second = core == 1
    core_arr = core[None].astype(jnp.int32)

    own_qkv = jnp.transpose(qkv_weight, (1, 2, 0)).reshape(3 * local, model)
    par_qkv = swap(own_qkv, "tensor", 1, 4)
    par_out = swap(out_weight, "tensor", 1, 4)
    par_up = swap(up_weight, "tensor", 1, 4)
    par_down = swap(down_weight, "tensor", 1, 4)
    par_bias = swap(up_bias, "tensor", 1, 4)
    bias = jnp.stack([up_bias, par_bias]).astype(F32)

    my_time = lax.dynamic_index_in_dim(time, core, keepdims=False).astype(F32)
    my_lengths = lax.dynamic_index_in_dim(lengths, core, keepdims=False)
    half = cond // 2
    frequency = jnp.exp(jnp.arange(half, dtype=F32) * (-math.log(10000.0) / half))
    angles = my_time * frequency
    features = jnp.concatenate([jnp.cos(angles), jnp.sin(angles)])
    mod = jnp.sum(features[:, None, None] * ada_weight.astype(F32), axis=0) + ada_bias.astype(F32)

    lo, hi = doc_bounds(my_lengths, length)
    position = jnp.arange(length, dtype=jnp.int32) - lo
    inverse = jnp.exp(jnp.arange(HALF, dtype=F32) * (-2.0 * math.log(10000.0) / HEAD_DIM))
    angles = inverse[:, None] * position.astype(F32)[None, :]
    cos, sin = jnp.cos(angles), jnp.sin(angles)
    lo, hi = lo[None], hi[None]
    gain_one = gain_attn.astype(F32)[None]
    gain_two = gain_mlp.astype(F32)[None]
    down_b = down_bias.astype(F32)[None]

    normed, qt, kt, vt, q, k, v = qkv_call(core_arr, tokens, gain_one, mod, own_qkv, par_qkv, cos, sin, length)
    att, stat, br, br_par = [], [], [], []
    for n in range(halves):
        a, st, b = att_call(qt, k, vt, lo, hi, out_weight, par_out, n, halves)
        att.append(a)
        stat.append(st)
        br.append(b)
        br_par.append(swap(b, "tensor", 2, 4))
    mlp, gn_par, ml_par = [], [], []
    for n in range(halves):
        out = mlp_call(
            core_arr, tokens, cotangent, br[n], br_par[n], gain_two, mod, up_weight, par_up, bias,
            down_weight, par_down, n, halves, length,
        )
        mlp.append(out)
        gn_par.append(swap(out[5], "tensor", 2, 4))
    for n in range(halves):
        ml_par.append(swap(mlp[n][4], "tensor", 2, 4))

    dk = jnp.zeros((length, 2 * local), F32)
    dv = jnp.zeros((length, 2 * local), F32)
    gmid, gb, gq, sums = [], [], [], []
    for n in range(halves):
        out = att_back_call(
            core_arr, tokens, cotangent, br[n], br_par[n], mlp[n][5], gn_par[n], gain_two, mod,
            out_weight, par_out, qt, q, k, kt, v, lo, hi, stat[n], cos, sin, dk, dv, n, halves,
        )
        gmid.append(out[0])
        gb.append(out[1])
        sums.append(out[2])
        gq.append(out[3])
        dk, dv = out[4], out[5]
    gproj, gn1, sums_one = qkv_back_call(
        core_arr, tokens, jnp.concatenate(gq, axis=1), dk, dv, own_qkv, par_qkv, cos, sin
    )
    gn1_par = swap(gn1, "tensor", 2, 4)
    outs, gate_sums = [], []
    for n in range(halves):
        o, g = output_call(core_arr, tokens, cotangent, br[n], br_par[n], mlp[n][4], ml_par[n], mod, down_b, n, halves)
        outs.append(o)
        gate_sums.append(g)
    output = jnp.concatenate(outs, axis=0)
    output = place_pair(output, swap(output, "tensor", 1, 4), second)
    grad_tok = tokens_call(core_arr, tokens, gn1, gn1_par, jnp.concatenate(gmid, axis=0), gain_one, mod)
    grad_tok = place_pair(grad_tok, swap(grad_tok, "tensor", 1, 4), second)

    def pair_reduce(own, par):
        got = swap(par.astype(BF16), "tensor", 1, 4)
        return own + got.astype(F32)

    act = jnp.concatenate([m[1] for m in mlp], axis=0)
    pre = jnp.concatenate([m[2] for m in mlp], axis=0)
    n2 = jnp.concatenate([m[0] for m in mlp], axis=0)
    gml = jnp.concatenate([m[3] for m in mlp], axis=0)
    hidden = up_weight.shape[1]
    g_up = pair_reduce(mm(n2, pre[:, :hidden], TN), mm(n2, pre[:, hidden:], TN))
    g_down = pair_reduce(mm(act[:, :hidden], gml, TN), mm(act[:, hidden:], gml, TN))
    pre_sum = jnp.sum(pre.astype(F32), axis=0)
    g_upb = pre_sum[:hidden] + swap(pre_sum[hidden:], "tensor", 1, 4)
    upb_block = jnp.zeros((32 * dp, hidden), F32).at[0].set(g_upb)
    grads_mlp = jnp.concatenate([g_up, g_down], axis=0).astype(BF16)
    grads_mlp = all_reduce_two(grads_mlp, "dp", dp)
    sum_upb = g_upb
    for bit in range(dp.bit_length() - 1):
        sum_upb = sum_upb + swap(sum_upb, "dp", 1 << bit, dp)
    gbr = jnp.concatenate(gb, axis=0)
    att_t = jnp.concatenate(att, axis=1)
    g_out = pair_reduce(mm(att_t[:local], gbr), mm(att_t[local:], gbr))
    gq3 = gproj.reshape(3, 2, local, length)
    g_qkv = pair_reduce(
        mm(gq3[:, 0].reshape(3 * local, length), normed), mm(gq3[:, 1].reshape(3 * local, length), normed)
    )
    grads_att = jnp.concatenate([g_qkv, g_out], axis=0).astype(BF16)
    grads_att = all_reduce_two(grads_att, "dp", dp)

    sums_one = sums_one[:2] + swap(sums_one[:2], "tensor", 2, 4)
    sums_two = sums[0] + sums[1]
    gate_m = (gate_sums[0] + gate_sums[1])[0]
    shift_a, scale_a = sums_one[0], sums_one[1]
    shift_m, scale_m, gate_a, cot_sum = sums_two[0], sums_two[1], sums_two[2], sums_two[3]
    feature_row = jnp.pad(features, (0, model - cond))
    row = jnp.stack([
        shift_a, scale_a * gain_one[0], gate_a, shift_m, scale_m * gain_two[0], gate_m,
        (1.0 + mod[1]) * scale_a, (1.0 + mod[4]) * scale_m, mod[5] * cot_sum, feature_row,
    ])
    rows = gather_slots(row, dp)
    gmod = rows[:, :6].reshape(-1, 6 * model)
    feats = rows[:, 9, :cond]
    g_adaw = lax.dot_general(feats, gmod, TN, precision=PRECISE).reshape(cond, 6, model)
    totals = jnp.sum(rows, axis=0)

    f_mlp, f_att = grads_mlp.astype(F32), grads_att.astype(F32)
    g_qkv = jnp.transpose(f_att[: 3 * local].reshape(3, local, model), (2, 0, 1))
    return (
        output,
        grad_tok,
        g_qkv,
        f_att[3 * local :],
        f_mlp[:model],
        sum_upb,
        f_mlp[model:],
        totals[8],
        totals[6],
        totals[7],
        g_adaw,
        totals[:6],
    )


def solution(mesh):
    in_specs = (
        P("dp", None), P("dp", None), P("dp"), P(None, None, "tensor"), P("tensor", None), P(None, "tensor"),
        P("tensor"), P("tensor", None), P(), P(), P(), P(), P(), P("dp", None),
    )
    out_specs = (
        P("dp", None), P("dp", None), P(None, None, "tensor"), P("tensor", None), P(None, "tensor"), P("tensor"),
        P("tensor", None), P(), P(), P(), P(), P(),
    )
    return jax.shard_map(
        functools.partial(per_device, mesh.shape["dp"]),
        mesh=mesh, in_specs=in_specs, out_specs=out_specs, check_vma=False,
    )
```

```python
import functools
import math

import jax
import jax.numpy as jnp
from jax import lax
from jax.experimental import pallas as pl
from jax.experimental.pallas import tpu as pltpu
from jax.sharding import PartitionSpec as P

HEAD_DIM = 64
HALF = HEAD_DIM // 2
EPS = 1e-05
ROWS = 256
PRECISE = lax.Precision.HIGHEST
VMEM_LIMIT = 60 * 1024 * 1024
F32 = jnp.float32
BF16 = jnp.bfloat16
GELU_A = math.sqrt(2.0 / math.pi)
GELU_B = 0.044715

NN = (((1,), (0,)), ((), ()))
NT = (((1,), (1,)), ((), ()))
TN = (((0,), (0,)), ((), ()))


def mm(left, right, dims=NN):
    return lax.dot_general(left, right, dims, preferred_element_type=F32)


def params(**more):
    return pltpu.CompilerParams(vmem_limit_bytes=VMEM_LIMIT, **more)


def whole(shape):
    zeros = (0,) * len(shape)
    return pl.BlockSpec(shape, lambda *_: zeros)


def norm_parts(v):
    center = jnp.mean(v, axis=-1, keepdims=True)
    centered = v - center
    spread = jnp.mean(centered * centered, axis=-1, keepdims=True)
    rstd = lax.rsqrt(spread + EPS)
    return centered * rstd, rstd


def join_heads(own_ref, par_ref, part, width):
    rows = slice(part * width, (part + 1) * width)
    return jnp.concatenate([own_ref[rows, :], par_ref[rows, :]], axis=0)


def qkv_kernel(core, tok, gain, mod, own, par, cos, sin, normed_o, qt_o, kt_o, vt_o, q_o, k_o, v_o):
    width = own.shape[0] // 3
    xhat, _ = norm_parts(tok[...].astype(F32))
    normed = (xhat * gain[...] * (1.0 + mod[1:2, :]) + mod[0:1, :]).astype(BF16)
    normed_o[...] = normed
    c, s = cos[...], sin[...]
    for part, (t_o, r_o) in enumerate(((qt_o, q_o), (kt_o, k_o), (vt_o, v_o))):
        turned = mm(join_heads(own, par, part, width), normed, NT)
        if part < 2:
            pieces = []
            for h in range(2 * width // HEAD_DIM):
                a = turned[h * HEAD_DIM : h * HEAD_DIM + HALF]
                b = turned[h * HEAD_DIM + HALF : (h + 1) * HEAD_DIM]
                pieces += [a * c - b * s, b * c + a * s]
            turned = jnp.concatenate(pieces, axis=0)
        if part == 0:
            turned = turned * (1.0 / math.sqrt(HEAD_DIM))
        t_o[...] = turned.astype(BF16)
        r_o[...] = turned.T.astype(BF16)


def qkv_call(core, tokens, gain, mod, own, par, cos, sin, length):
    width, model = 2 * own.shape[0] // 3, tokens.shape[1]
    steps = length // ROWS
    col = pl.BlockSpec((width, ROWS), lambda i, c: (0, i))
    row = pl.BlockSpec((ROWS, width), lambda i, c: (i, 0))
    table = pl.BlockSpec((HALF, ROWS), lambda i, c: (0, i))
    return pl.pallas_call(
        qkv_kernel,
        grid_spec=pltpu.PrefetchScalarGridSpec(
            num_scalar_prefetch=1,
            grid=(steps,),
            in_specs=[
                pl.BlockSpec((ROWS, model), lambda i, c: (c[0] * steps + i, 0)),
                whole(gain.shape),
                whole(mod.shape),
                whole(own.shape),
                whole(par.shape),
                table,
                table,
            ],
            out_specs=[pl.BlockSpec((ROWS, model), lambda i, c: (i, 0))] + [col] * 3 + [row] * 3,
        ),
        out_shape=[jax.ShapeDtypeStruct((length, model), BF16)]
        + [jax.ShapeDtypeStruct((width, length), BF16)] * 3
        + [jax.ShapeDtypeStruct((length, width), BF16)] * 3,
        compiler_params=params(),
        name="norm_qkv",
    )(core, tokens, gain, mod, own, par, cos, sin)


def only_half(block, second):
    zero = jnp.zeros_like(block)
    return jnp.concatenate([zero, block] if second else [block, zero], axis=0)


def doc_mask(lo_ref, hi_ref, keys):
    place = lax.broadcasted_iota(jnp.int32, (keys, lo_ref.shape[1]), 0)
    return (place >= lo_ref[...]) & (place < hi_ref[...])


def att_kernel(qt, k, vt, lo, hi, own, par, at_o, stat_o, br_o):
    heads = qt.shape[0] // HEAD_DIM
    allowed = doc_mask(lo, hi, k.shape[0])
    for h in range(heads):
        pair = slice((h // 2) * 2 * HEAD_DIM, (h // 2 + 1) * 2 * HEAD_DIM)
        mine = slice(h * HEAD_DIM, (h + 1) * HEAD_DIM)
        scores = mm(k[:, pair], only_half(qt[mine, :], h % 2))
        scores = jnp.where(allowed, scores, -1000000000.0)
        top = jnp.max(scores, axis=0, keepdims=True)
        terms = jnp.exp(scores - top)
        inv = 1.0 / jnp.sum(terms, axis=0, keepdims=True)
        out = mm(vt[mine, :], (terms * inv).astype(BF16))
        at_o[mine, :] = out.astype(BF16)
        stat_o[h : h + 1, :] = top
        stat_o[8 + h : 9 + h, :] = inv
    weight = jnp.concatenate([own[...], par[...]], axis=0)
    br_o[...] = mm(at_o[...], weight, TN).astype(BF16)


def att_call(qt, k, vt, lo, hi, own, par, half, halves):
    width, length = qt.shape
    model = own.shape[1]
    steps = length // ROWS // halves
    first = half * steps
    col = pl.BlockSpec((width, ROWS), lambda i: (0, first + i))
    bound = pl.BlockSpec((1, ROWS), lambda i: (0, first + i))
    span = steps * ROWS
    return pl.pallas_call(
        att_kernel,
        grid=(steps,),
        in_specs=[col, whole(k.shape), whole(vt.shape), bound, bound, whole(own.shape), whole(par.shape)],
        out_specs=[
            pl.BlockSpec((width, ROWS), lambda i: (0, i)),
            pl.BlockSpec((16, ROWS), lambda i: (0, i)),
            pl.BlockSpec((ROWS, model), lambda i: (i, 0)),
        ],
        out_shape=[
            jax.ShapeDtypeStruct((width, span), BF16),
            jax.ShapeDtypeStruct((16, span), F32),
            jax.ShapeDtypeStruct((span, model), BF16),
        ],
        compiler_params=params(),
        cost_estimate=pl.CostEstimate(flops=10_000_000_000, bytes_accessed=4_000_000, transcendentals=0),
        name="attend",
    )(qt, k, vt, lo, hi, own, par)


MESH = pl.DeviceIdType.MESH


def bit_of(index, bit):
    return lax.rem(index // (1 << bit), 2)


def flip(index, bit):
    return index + (1 << bit) * (1 - 2 * bit_of(index, bit))


class Reduce:
    def __init__(self, total, base, rows, inbox, inbase, order, final, send, recv, first_sem):
        self.total, self.base, self.inbox, self.send, self.recv = total, base, inbox, send, recv
        self.final = final
        self.plan, self.sem = [], first_sem
        size, halved = rows, []
        for bit in order:
            if size % 32 == 0:
                self.plan.append(("halve", bit, size // 2, inbase, list(halved)))
                size //= 2
                halved.append((bit, size))
            else:
                self.plan.append(("whole", bit, size, inbase, list(halved)))
            inbase += size
        self.inend = inbase
        while halved:
            bit, size = halved.pop()
            self.plan.append(("double", bit, size, None, list(halved)))
        self.steps = len(self.plan)

    def offset(self, halved):
        me = lax.axis_index("dp")
        at = self.base
        for bit, size in halved:
            at = at + bit_of(me, bit) * size
        return at

    def copy(self, n):
        kind, bit, size, inbase, halved = self.plan[n]
        me = lax.axis_index("dp")
        start = self.offset(halved)
        if kind == "halve":
            source = start + (1 - bit_of(me, bit)) * size
        elif kind == "whole":
            source = start
        else:
            source = start + bit_of(me, bit) * size
        block = pl.ds(pl.multiple_of(source, 16), size)
        return pltpu.make_async_remote_copy(
            src_ref=(self.final if kind == "double" else self.total).at[block],
            dst_ref=self.final.at[block] if kind == "double" else self.inbox.at[pl.ds(inbase, size)],
            send_sem=self.send.at[self.sem + n],
            recv_sem=self.recv.at[self.sem + n],
            device_id={"dp": flip(me, bit)},
            device_id_type=MESH,
        )

    def start(self, n):
        if n < self.steps:
            self.copy(n).start()

    def finish(self, n):
        if n >= self.steps:
            return
        self.copy(n).wait()
        kind, bit, size, inbase, halved = self.plan[n]
        if kind == "double":
            return
        keep = self.offset(halved)
        if kind == "halve":
            keep = keep + bit_of(lax.axis_index("dp"), bit) * size
        tile = 48 if size % 48 == 0 else 16

        @pl.loop(0, size // tile)
        def _(j):
            mine = pl.ds(pl.multiple_of(keep + j * tile, 16), tile)
            came = pl.ds(pl.multiple_of(inbase + j * tile, 16), tile)
            added = self.total[mine, :].astype(F32) + self.inbox[came, :].astype(F32)
            self.total[mine, :] = added.astype(BF16)

        if n + 1 == self.steps or self.plan[n + 1][0] == "double":
            block = pl.ds(pl.multiple_of(keep, 16), size)
            slot = self.sem + self.steps
            store = pltpu.make_async_copy(self.total.at[block], self.final.at[block], self.send.at[slot])
            store.start()
            store.wait()


class Gather:
    def __init__(self, rows, dp, send, recv, first_sem):
        self.rows, self.send, self.recv, self.sem = rows, send, recv, first_sem
        self.bits = list(reversed(range(dp.bit_length() - 1))) + [None]
        self.steps = len(self.bits)

    def place(self):
        at, weight = 0, 1
        for bit in self.bits:
            index = lax.axis_index("tensor") if bit is None else lax.axis_index("dp")
            at = at + bit_of(index, bit or 0) * weight
            weight *= 2
        return at

    def own(self, row, sem):
        store = pltpu.make_async_copy(row, self.rows.at[self.place()], sem)
        store.start()
        store.wait()

    def copy(self, n):
        bit, size = self.bits[n], 1 << n
        block = self.rows.at[pl.ds((self.place() // size) * size, size)]
        axis = "tensor" if bit is None else "dp"
        return pltpu.make_async_remote_copy(
            src_ref=block,
            dst_ref=block,
            send_sem=self.send.at[self.sem + n],
            recv_sem=self.recv.at[self.sem + n],
            device_id={axis: flip(lax.axis_index(axis), bit or 0)},
            device_id_type=MESH,
        )

    def start(self, n):
        if n < self.steps:
            self.copy(n).start()

    def finish(self, n):
        if n < self.steps:
            self.copy(n).wait()


def norm_back(gn, xhat, rstd, gain):
    y = gn * gain
    mean_y = jnp.mean(y, axis=-1, keepdims=True)
    mean_yx = jnp.mean(y * xhat, axis=-1, keepdims=True)
    return rstd * (y - mean_y - xhat * mean_yx)


def col_sum(v):
    return jnp.sum(v, axis=0, keepdims=True)


def back_kernel(
    dp, tok_h, cot_h, up0_h, up1_h, dn0_h, dn1_h,
    br_own, br_par, gain1, gain2, mod, bias, downb, feats, out0, out1, qkv0, qkv1,
    qt, q, k, kt, v, att, normed, stat, lo, hi, cos, sin,
    out_h, gtok_h, gmlp_h, early_h, late_h, gatt_h,
    tok, cot, w_s, n2, act, pre, gml, ml_own, ml_par, gn_own, gn_par, gn1_par, gmid, dk, dv, gproj,
    box1, box2, gatt, inbox1, inbox2, vec_own, vec_par, row_own, sums,
    load_sem, y_send, y_recv, c_send, c_recv, d_send, d_recv, o_sem,
):
    length, model = tok.shape
    hidden = bias.shape[1]
    local = out0.shape[0]
    heads = 2 * local // HEAD_DIM
    chunks = length // ROWS
    tensor, here_dp = lax.axis_index("tensor"), lax.axis_index("dp")
    core = lax.rem(tensor, 2)
    other_core, other_y = flip(tensor, 0), flip(tensor, 1)
    bits = dp.bit_length() - 1

    sums[...] = jnp.zeros_like(sums)
    vec_own[...] = jnp.zeros_like(vec_own)
    row_own[...] = jnp.zeros_like(row_own)
    barrier = pltpu.get_barrier_semaphore()
    for peer in [{"tensor": other_core}, {"tensor": other_y}] + [{"dp": flip(here_dp, b)} for b in range(bits)]:
        pl.semaphore_signal(barrier, inc=1, device_id=peer, device_id_type=MESH)
    mine_rows = pl.ds(pl.multiple_of(core * length, 16), length)
    loads = [
        pltpu.make_async_copy(tok_h.at[mine_rows], tok, load_sem.at[0]),
        pltpu.make_async_copy(cot_h.at[mine_rows], cot, load_sem.at[1]),
    ]
    for n, ref in enumerate((up0_h, up1_h, dn0_h, dn1_h)):
        loads.append(pltpu.make_async_copy(ref, w_s.at[pl.ds(n * model, model)], load_sem.at[2 + n]))
    for load in loads:
        load.start()
    for load in loads:
        load.wait()
    pl.semaphore_wait(barrier, 2 + bits)

    def rows_of(i):
        return pl.ds(pl.multiple_of(i * ROWS, ROWS), ROWS)

    def to_y(source, target, n, send=None, recv=None):
        return pltpu.make_async_remote_copy(
            src_ref=source, dst_ref=target, send_sem=y_send.at[n], recv_sem=y_recv.at[n],
            device_id={"tensor": other_y}, device_id_type=MESH,
        )

    def to_core(source, target, n):
        return pltpu.make_async_remote_copy(
            src_ref=source, dst_ref=target, send_sem=c_send.at[n], recv_sem=c_recv.at[n],
            device_id={"tensor": other_core}, device_id_type=MESH,
        )

    def gn_copy(i):
        return to_y(gn_own.at[rows_of(i)], gn_par.at[rows_of(i)], i)

    def ml_copy(i):
        return to_y(ml_own.at[rows_of(i)], ml_par.at[rows_of(i)], chunks + i)

    def gn1_copy(i):
        return to_y(n2.at[rows_of(i)], gn1_par.at[rows_of(i)], 2 * chunks + i)

    def vec_copy(n):
        return to_y(vec_own.at[n], vec_par.at[n], 3 * chunks + n)


    @pl.loop(0, chunks)
    def _(i):
        r = rows_of(i)
        middle = tok[r, :].astype(F32) + mod[2:3, :] * (br_own[r, :].astype(F32) + br_par[r, :].astype(F32))
        xhat, _ = norm_parts(middle)
        x2 = (xhat * gain2[...] * (1.0 + mod[4:5, :]) + mod[3:4, :]).astype(BF16)
        n2[r, :] = x2
        grad_out = cot[r, :].astype(F32)
        g = (mod[5:6, :] * grad_out).astype(BF16)
        gml[r, :] = g
        part = jnp.zeros((ROWS, model), F32)
        grad = jnp.zeros((ROWS, model), F32)
        for n in range(2):
            up, down = w_s.at[pl.ds(n * model, model)], w_s.at[pl.ds((2 + n) * model, hidden)]
            cols = slice(n * hidden, (n + 1) * hidden)
            z = mm(x2, up[...]) + bias[n : n + 1, :]
            square = z * z
            t = jnp.tanh(GELU_A * z * (1.0 + GELU_B * square))
            a = (0.5 * z * (1.0 + t)).astype(BF16)
            act[r, cols] = a
            slope = 0.5 * (1.0 + t) + (0.5 * GELU_A) * z * (1.0 - t * t) * (1.0 + 3.0 * GELU_B * square)
            part = part + mm(a, down[...])
            p = (mm(g, down[...], NT) * slope).astype(BF16)
            pre[r, cols] = p
            sums[n : n + 1, :] += col_sum(p.astype(F32))
            grad = grad + mm(p, up[...], NT)
        ml_own[r, :] = part.astype(BF16)
        gn_own[r, :] = grad.astype(BF16)
        vec_own[0, 0:1, :] += col_sum(grad_out * part)
        sums[2:3, :] += col_sum(grad_out)
        gn_copy(i).start()

    vec_copy(0).start()

    def up_grad(j, n):
        cols = pl.ds(pl.multiple_of(j * ROWS, ROWS), ROWS)
        return mm(n2[:, cols], pre[:, n * hidden : (n + 1) * hidden], TN)

    def down_grad(j, n):
        cols = pl.ds(pl.multiple_of(n * hidden + j * ROWS, ROWS), ROWS)
        return mm(act[:, cols], gml[...], TN)

    outbox = w_s.at[pl.ds(2 * model, model + hidden)]

    @pl.loop(0, model // ROWS)
    def _(j):
        outbox[rows_of(j), :] = up_grad(j, 1).astype(BF16)

    up_copy = to_core(outbox.at[pl.ds(0, model)], box1.at[pl.ds(0, model)], 0)
    up_copy.start()

    @pl.loop(0, hidden // ROWS)
    def _(j):
        outbox[pl.ds(pl.multiple_of(model + j * ROWS, ROWS), ROWS), :] = down_grad(j, 1).astype(BF16)

    down_copy = to_core(outbox.at[pl.ds(model, hidden)], box1.at[pl.ds(model, hidden)], 1)
    down_copy.start()
    up_copy.wait()

    @pl.loop(0, model // ROWS)
    def _(j):
        r = rows_of(j)
        w_s[r, :] = (up_grad(j, 0) + box1[r, :].astype(F32)).astype(BF16)

    order = list(range(bits))
    red_up = Reduce(w_s, 0, model, inbox1, 0, order, gmlp_h, d_send, d_recv, 0)
    red_up.start(0)
    down_copy.wait()

    @pl.loop(0, hidden // ROWS)
    def _(j):
        r = pl.ds(pl.multiple_of(model + j * ROWS, ROWS), ROWS)
        w_s[r, :] = (down_grad(j, 0) + box1[r, :].astype(F32)).astype(BF16)

    red_down = Reduce(
        w_s, model, hidden, inbox1, red_up.inend, order[1:] + order[:1], gmlp_h, d_send, d_recv, red_up.steps + 1
    )
    red_down.start(0)
    first = red_up.steps + red_down.steps + 2

    dk[...] = jnp.zeros_like(dk)
    dv[...] = jnp.zeros_like(dv)

    @pl.loop(0, chunks)
    def _(i):
        r = rows_of(i)
        gn_copy(i).wait_recv()
        ml_copy(i).start()
        branch = br_own[r, :].astype(F32) + br_par[r, :].astype(F32)
        xhat, rstd = norm_parts(tok[r, :].astype(F32) + mod[2:3, :] * branch)
        gn = gn_own[r, :].astype(F32) + gn_par[r, :].astype(F32)
        g = cot[r, :].astype(F32) + norm_back(gn, xhat, rstd, (1.0 + mod[4:5, :]) * gain2[...])
        gmid[r, :] = g
        sums[3:4, :] += col_sum(gn)
        sums[4:5, :] += col_sum(gn * xhat)
        sums[5:6, :] += col_sum(g * branch)
        gb = (mod[2:3, :] * g).astype(BF16)
        gml[r, :] = gb
        weight = jnp.concatenate([out0[...], out1[...]], axis=0)
        do_t = mm(weight, gb, NT).astype(BF16)
        do = mm(gb, weight, NT).astype(BF16)
        place = lax.broadcasted_iota(jnp.int32, (length, ROWS), 0)
        allowed = (place >= lo[:, r]) & (place < hi[:, r])
        lane = lax.broadcasted_iota(jnp.int32, (ROWS, 2 * HEAD_DIM), 1)
        c, s = cos[:, r], sin[:, r]
        for p in range(heads // 2):
            pair = slice(p * 2 * HEAD_DIM, (p + 1) * 2 * HEAD_DIM)
            dk_sum, dv_sum = dk[:, pair], dv[:, pair]
            for n in range(2):
                h = 2 * p + n
                mine = slice(h * HEAD_DIM, (h + 1) * HEAD_DIM)
                scores = mm(k[:, pair], only_half(qt[mine, r], n))
                probs = jnp.where(allowed, jnp.exp(scores - stat[h : h + 1, r]), 0.0) * stat[8 + h : 9 + h, r]
                grad_p = mm(v[:, pair], only_half(do_t[mine, :], n))
                centre = col_sum(probs * grad_p)
                grad_s = (probs * (grad_p - centre)).astype(BF16)
                dq = mm(kt[mine, :], grad_s) * (1.0 / math.sqrt(HEAD_DIM))
                ua, ub = dq[:HALF], dq[HALF:]
                gproj[h * HEAD_DIM : h * HEAD_DIM + HALF, r] = (ua * c + ub * s).astype(BF16)
                gproj[h * HEAD_DIM + HALF : (h + 1) * HEAD_DIM, r] = (ub * c - ua * s).astype(BF16)
                here = (lane >= HEAD_DIM) if n else (lane < HEAD_DIM)
                none = jnp.zeros((ROWS, 2 * HEAD_DIM), BF16)
                dk_sum = dk_sum + mm(grad_s, jnp.where(here, q[r, pair], none))
                dv_sum = dv_sum + mm(probs.astype(BF16), jnp.where(here, do[:, pair], none))
            dk[:, pair] = dk_sum
            dv[:, pair] = dv_sum
        for n in range(chunks):

            @pl.when(i == n)
            def _():
                for stream in (red_up, red_down):
                    stream.finish(n)
                    stream.start(n + 1)

    vec_copy(0).wait()
    early = Gather(early_h, dp, d_send, d_recv, first)
    row_own[0, 0:1, :] = sums[3:4, :]
    row_own[0, 1:2, :] = sums[4:5, :] * gain2[...]
    row_own[0, 2:3, :] = sums[5:6, :]
    row_own[0, 3:4, :] = vec_own[0, 0:1, :] + vec_par[0, 0:1, :] + sums[2:3, :] * downb[...]
    row_own[0, 4:5, :] = mod[5:6, :] * sums[2:3, :]
    row_own[0, 5:6, :] = (1.0 + mod[4:5, :]) * sums[4:5, :]
    row_own[0, 6:7, :] = jnp.where(core == 0, sums[0:1, :], sums[1:2, :])
    row_own[0, 7:8, :] = jnp.where(core == 0, sums[1:2, :], sums[0:1, :])
    early.own(row_own.at[0], load_sem.at[0])
    early.start(0)
    first += early.steps
    for n in range(chunks):
        gn_copy(n).wait_send()

    @pl.loop(0, chunks)
    def _(i):
        r = rows_of(i)
        c, s = cos[:, r], sin[:, r]
        turned = dk[r, :].T
        pieces = []
        for h in range(heads):
            ua = turned[h * HEAD_DIM : h * HEAD_DIM + HALF]
            ub = turned[h * HEAD_DIM + HALF : (h + 1) * HEAD_DIM]
            pieces += [ua * c + ub * s, ub * c - ua * s]
        gk = jnp.concatenate(pieces, axis=0).astype(BF16)
        gv = dv[r, :].T.astype(BF16)
        gproj[2 * local : 4 * local, r] = gk
        gproj[4 * local :, r] = gv
        grads = (gproj[: 2 * local, r], gk, gv)
        gn = jnp.zeros((ROWS, model), F32)
        for part in range(3):
            gn = gn + mm(grads[part], join_heads(qkv0, qkv1, part, local), TN)
        n2[r, :] = gn.astype(BF16)
        gn1_copy(i).start()
        xhat, _ = norm_parts(tok[r, :].astype(F32))
        vec_own[1, 0:1, :] += col_sum(gn)
        vec_own[1, 1:2, :] += col_sum(gn * xhat)

    vec_copy(1).start()
    early.finish(0)
    early.start(1)
    for stream in (red_up, red_down):
        stream.finish(chunks)
        stream.start(chunks + 1)

    sent2 = w_s.at[pl.ds(2 * model, 4 * local)]

    def att_grads(n):
        pieces = []
        for part in range(3):
            rows = slice((2 * part + n) * local, (2 * part + n + 1) * local)
            pieces.append(mm(gproj[rows, :], normed[...]))
        pieces.append(mm(att[n * local : (n + 1) * local, :], gml[...]))
        return pieces

    for part, piece in enumerate(att_grads(1)):
        sent2[part * local : (part + 1) * local, :] = piece.astype(BF16)
    att_copy = to_core(sent2, box2, 2)
    att_copy.start()
    early.finish(1)
    early.start(2)
    for part, piece in enumerate(att_grads(0)):
        gatt[part * local : (part + 1) * local, :] = piece.astype(BF16)
    att_copy.wait()
    gatt[...] = (gatt[...].astype(F32) + box2[...].astype(F32)).astype(BF16)
    part_rows = 2 * local
    red_a = Reduce(gatt, 0, part_rows, inbox2, 0, order, gatt_h, d_send, d_recv, first)
    first += red_a.steps + 1
    red_b = Reduce(
        gatt, part_rows, part_rows, inbox2, red_a.inend, order[1:] + order[:1], gatt_h, d_send, d_recv, first
    )
    first += red_b.steps + 1
    red_a.start(0)
    red_b.start(0)

    late = Gather(late_h, dp, d_send, d_recv, first)
    vec_copy(1).wait()
    shift_a = vec_own[1, 0:1, :] + vec_par[1, 0:1, :]
    scale_a = vec_own[1, 1:2, :] + vec_par[1, 1:2, :]
    row_own[1, 0:1, :] = shift_a
    row_own[1, 1:2, :] = scale_a * gain1[...]
    row_own[1, 2:3, :] = (1.0 + mod[1:2, :]) * scale_a
    row_own[1, 3:4, :] = feats[...]
    late.own(row_own.at[1], load_sem.at[1])
    late.start(0)

    out_copies = []

    def hand_over(source, target, i, n):
        rows = pl.ds(pl.multiple_of(core * length + i * ROWS, 16), ROWS)
        keep = pltpu.make_async_copy(source, target.at[rows], o_sem.at[n])
        give = to_core(source, target.at[rows], 3 + n)
        keep.start()
        give.start()
        out_copies.append((keep, give))

    streams = (red_a, red_b, early, late)
    done = [0, 0, 2, 0]

    def advance():
        for n, stream in enumerate(streams):
            if done[n] < stream.steps:
                stream.finish(done[n])
                stream.start(done[n] + 1)
                done[n] += 1

    left = [chunks + 1, chunks + 1]

    def advance_mlp():
        for n, stream in enumerate((red_up, red_down)):
            if left[n] < stream.steps:
                stream.finish(left[n])
                stream.start(left[n] + 1)
                left[n] += 1

    for i in range(chunks):
        r = slice(i * ROWS, (i + 1) * ROWS)
        ml_copy(i).wait()
        middle = tok[r, :].astype(F32) + mod[2:3, :] * (br_own[r, :].astype(F32) + br_par[r, :].astype(F32))
        total = ml_own[r, :].astype(F32) + ml_par[r, :].astype(F32) + downb[...]
        act[r, :model] = (middle + mod[5:6, :] * total).astype(BF16)
        hand_over(act.at[r, :model], out_h, i, i)
        advance_mlp()
        if i % 2:
            advance()
    for i in range(chunks):
        r = slice(i * ROWS, (i + 1) * ROWS)
        gn1_copy(i).wait()
        xhat, rstd = norm_parts(tok[r, :].astype(F32))
        gn = n2[r, :].astype(F32) + gn1_par[r, :].astype(F32)
        g = gmid[r, :] + norm_back(gn, xhat, rstd, (1.0 + mod[1:2, :]) * gain1[...])
        act[r, model : 2 * model] = g.astype(BF16)
        hand_over(act.at[r, model : 2 * model], gtok_h, i, chunks + i)
        advance()
    while left[0] < red_up.steps or left[1] < red_down.steps:
        advance_mlp()
    while any(done[n] < stream.steps for n, stream in enumerate(streams)):
        advance()
    for keep, give in out_copies:
        keep.wait()
        give.wait()


def back_call(dp, hbm, vmem, length):
    tokens = hbm[0]
    model = tokens.shape[1]
    hidden = hbm[2].shape[1]
    qt = vmem[12]
    width = qt.shape[0]
    local = width // 2
    chunks = length // ROWS
    slots = 2 * dp
    sems = 4 * (2 * dp.bit_length()) + 2 * dp.bit_length()
    any_spec, vmem_spec = pl.BlockSpec(memory_space=pl.ANY), pl.BlockSpec(memory_space=pltpu.VMEM)
    rows_bf = pltpu.VMEM((length, model), BF16)
    inbox_rows = inbox_need(dp, model) + inbox_need(dp, hidden)
    inbox2_rows = 2 * inbox_need(dp, width)
    dma = pltpu.SemaphoreType.DMA
    return pl.pallas_call(
        functools.partial(back_kernel, dp),
        in_specs=[any_spec] * len(hbm) + [vmem_spec] * len(vmem),
        out_specs=[any_spec] * 6,
        out_shape=[
            jax.ShapeDtypeStruct(tokens.shape, BF16),
            jax.ShapeDtypeStruct(tokens.shape, BF16),
            jax.ShapeDtypeStruct((model + hidden, model), BF16),
            jax.ShapeDtypeStruct((slots, 8, model), F32),
            jax.ShapeDtypeStruct((slots, 8, model), F32),
            jax.ShapeDtypeStruct((4 * local, model), BF16),
        ],
        scratch_shapes=[
            rows_bf, rows_bf, pltpu.VMEM((2 * (model + hidden), model), BF16), rows_bf,
            pltpu.VMEM((length, 2 * hidden), BF16), pltpu.VMEM((length, 2 * hidden), BF16), rows_bf,
            rows_bf, rows_bf, rows_bf, rows_bf, rows_bf, pltpu.VMEM((length, model), F32),
            pltpu.VMEM((length, width), F32), pltpu.VMEM((length, width), F32), pltpu.VMEM((3 * width, length), BF16),
            pltpu.VMEM((model + hidden, model), BF16), pltpu.VMEM((4 * local, model), BF16),
            pltpu.VMEM((4 * local, model), BF16),
            pltpu.VMEM((inbox_rows, model), BF16),
            pltpu.VMEM((inbox2_rows, model), BF16), pltpu.VMEM((2, 8, model), F32), pltpu.VMEM((2, 8, model), F32), pltpu.VMEM((2, 8, model), F32),
            pltpu.VMEM((8, model), F32),
            dma((6,)), dma((3 * chunks + 2,)), dma((3 * chunks + 2,)), dma((3 + 2 * chunks,)), dma((3 + 2 * chunks,)),
            dma((sems,)), dma((sems,)), dma((2 * chunks,)),
        ],
        compiler_params=pltpu.CompilerParams(
            collective_id=0, has_side_effects=True, vmem_limit_bytes=VMEM_LIMIT
        ),
        cost_estimate=pl.CostEstimate(flops=60_000_000_000, bytes_accessed=40_000_000, transcendentals=0),
        name="mlp_and_backward",
    )(*hbm, *vmem)


def inbox_need(dp, rows):
    need = 0
    for _ in range(dp.bit_length() - 1):
        if rows % 32 == 0:
            rows //= 2
        need += rows
    return need


def swap(array, axis, bit, size):
    return lax.ppermute(array, axis, [(i, i ^ bit) for i in range(size)])


def place_pair(mine, other, second):
    lower = jnp.where(second, other, mine)
    upper = jnp.where(second, mine, other)
    return jnp.concatenate([lower, upper], axis=0)


def doc_bounds(lengths_row, count):
    ends = jnp.cumsum(lengths_row)
    places = jnp.arange(count, dtype=jnp.int32)
    passed = (places[None, :] >= ends[:, None]).astype(jnp.int32)
    starts = jnp.sum(passed * lengths_row[:, None], axis=0)
    segment = jnp.sum(passed, axis=0)
    member = segment[None, :] == jnp.arange(lengths_row.shape[0])[:, None]
    own = jnp.sum(jnp.where(member, lengths_row[:, None], 0), axis=0)
    return starts, starts + own


def per_device(
    dp, tokens, lengths, time, qkv_weight, out_weight, up_weight, up_bias, down_weight, down_bias,
    gain_attn, gain_mlp, ada_weight, ada_bias, cotangent,
):
    slot_count, model = time.shape[0], tokens.shape[1]
    length = tokens.shape[0] // slot_count
    local = out_weight.shape[0]
    cond = ada_weight.shape[0]
    halves = 2
    core = lax.axis_index("tensor") & 1
    second = core == 1
    core_arr = core[None].astype(jnp.int32)

    own_qkv = jnp.transpose(qkv_weight, (1, 2, 0)).reshape(3 * local, model)
    par_qkv = swap(own_qkv, "tensor", 1, 4)
    par_out = swap(out_weight, "tensor", 1, 4)
    par_up = swap(up_weight, "tensor", 1, 4)
    par_down = swap(down_weight, "tensor", 1, 4)
    par_bias = swap(up_bias, "tensor", 1, 4)
    bias = jnp.stack([up_bias, par_bias]).astype(F32)

    my_time = lax.dynamic_index_in_dim(time, core, keepdims=False).astype(F32)
    my_lengths = lax.dynamic_index_in_dim(lengths, core, keepdims=False)
    half = cond // 2
    frequency = jnp.exp(jnp.arange(half, dtype=F32) * (-math.log(10000.0) / half))
    angles = my_time * frequency
    features = jnp.concatenate([jnp.cos(angles), jnp.sin(angles)])
    mod = jnp.sum(features[:, None, None] * ada_weight.astype(F32), axis=0) + ada_bias.astype(F32)

    lo, hi = doc_bounds(my_lengths, length)
    position = jnp.arange(length, dtype=jnp.int32) - lo
    inverse = jnp.exp(jnp.arange(HALF, dtype=F32) * (-2.0 * math.log(10000.0) / HEAD_DIM))
    angles = inverse[:, None] * position.astype(F32)[None, :]
    cos, sin = jnp.cos(angles), jnp.sin(angles)
    lo, hi = lo[None], hi[None]
    gain_one = gain_attn.astype(F32)[None]
    gain_two = gain_mlp.astype(F32)[None]
    down_b = down_bias.astype(F32)[None]

    normed, qt, kt, vt, q, k, v = qkv_call(core_arr, tokens, gain_one, mod, own_qkv, par_qkv, cos, sin, length)
    att, stat, br, br_par = [], [], [], []
    for n in range(halves):
        a, st, b = att_call(qt, k, vt, lo, hi, out_weight, par_out, n, halves)
        att.append(a)
        stat.append(st)
        br.append(b)
        br_par.append(swap(b, "tensor", 2, 4))
    feats = jnp.pad(features, (0, model - cond))[None]
    br_own = jnp.concatenate(br, axis=0)
    br_other = jnp.concatenate(br_par, axis=0)
    output, grad_tok, g_mlp, early, late, g_att = back_call(
        dp,
        [tokens, cotangent, up_weight, par_up, down_weight, par_down],
        [
            br_own, br_other, gain_one, gain_two, mod, bias, down_b, feats, out_weight, par_out, own_qkv, par_qkv,
            qt, q, k, kt, v, jnp.concatenate(att, axis=1), normed, jnp.concatenate(stat, axis=1), lo, hi, cos, sin,
        ],
        length,
    )
    gmod = jnp.concatenate([late[:, 0:2], early[:, 2:3], early[:, 0:2], early[:, 3:4]], axis=1)
    slots = gmod.shape[0]
    g_adaw = lax.dot_general(
        late[:, 3, :cond], gmod.reshape(slots, 6 * model), TN, precision=PRECISE
    ).reshape(cond, 6, model)
    f_mlp, f_att = g_mlp.astype(F32), g_att.astype(F32)
    return (
        output,
        grad_tok,
        jnp.transpose(f_att[: 3 * local].reshape(3, local, model), (2, 0, 1)),
        f_att[3 * local :],
        f_mlp[:model],
        jnp.where(second, jnp.sum(early[:, 7], axis=0), jnp.sum(early[:, 6], axis=0)),
        f_mlp[model:],
        jnp.sum(early[:, 4], axis=0),
        jnp.sum(late[:, 2], axis=0),
        jnp.sum(early[:, 5], axis=0),
        g_adaw,
        jnp.sum(gmod, axis=0),
    )


def solution(mesh):
    in_specs = (
        P("dp", None), P("dp", None), P("dp"), P(None, None, "tensor"), P("tensor", None), P(None, "tensor"),
        P("tensor"), P("tensor", None), P(), P(), P(), P(), P(), P("dp", None),
    )
    out_specs = (
        P("dp", None), P("dp", None), P(None, None, "tensor"), P("tensor", None), P(None, "tensor"), P("tensor"),
        P("tensor", None), P(), P(), P(), P(), P(),
    )
    return jax.shard_map(
        functools.partial(per_device, mesh.shape["dp"]),
        mesh=mesh, in_specs=in_specs, out_specs=out_specs, check_vma=False,
    )
```

```python
import functools
import math

import jax
import jax.numpy as jnp
import numpy as np
from jax import lax
from jax.experimental import pallas as pl
from jax.experimental.pallas import tpu as pltpu
from jax.sharding import PartitionSpec as P

HEAD_DIM = 64
HALF = HEAD_DIM // 2
EPS = 1e-05
ROWS = 256
PRECISE = lax.Precision.HIGHEST
GROUP = 16
LONGEST = 512
VMEM_LIMIT = 61 * 1024 * 1024
F32 = jnp.float32
BF16 = jnp.bfloat16
GELU_A = math.sqrt(2.0 / math.pi)
GELU_B = 0.044715

NN = (((1,), (0,)), ((), ()))
NT = (((1,), (1,)), ((), ()))
TN = (((0,), (0,)), ((), ()))


def mm(left, right, dims=NN):
    return lax.dot_general(left, right, dims, preferred_element_type=F32)


def norm_parts(v):
    center = jnp.mean(v, axis=-1, keepdims=True)
    centered = v - center
    spread = jnp.mean(centered * centered, axis=-1, keepdims=True)
    rstd = lax.rsqrt(spread + EPS)
    return centered * rstd, rstd


def only_half(block, second):
    zero = jnp.zeros_like(block)
    return jnp.concatenate([zero, block] if second else [block, zero], axis=0)


MESH = pl.DeviceIdType.MESH


def bit_of(index, bit):
    return lax.rem(index // (1 << bit), 2)


def flip(index, bit):
    return index + (1 << bit) * (1 - 2 * bit_of(index, bit))


class Reduce:
    def __init__(self, total, base, rows, inbox, inbase, order, final, send, recv, first_sem):
        self.total, self.base, self.inbox, self.send, self.recv = total, base, inbox, send, recv
        self.final = final
        self.plan, self.sem = [], first_sem
        size, halved = rows, []
        for bit in order:
            if size % 32 == 0:
                self.plan.append(("halve", bit, size // 2, inbase, list(halved)))
                size //= 2
                halved.append((bit, size))
            else:
                self.plan.append(("whole", bit, size, inbase, list(halved)))
            inbase += size
        self.inend = inbase
        while halved:
            bit, size = halved.pop()
            self.plan.append(("double", bit, size, None, list(halved)))
        self.steps = len(self.plan)

    def offset(self, halved):
        me = lax.axis_index("dp")
        at = self.base
        for bit, size in halved:
            at = at + bit_of(me, bit) * size
        return at

    def copy(self, n):
        kind, bit, size, inbase, halved = self.plan[n]
        me = lax.axis_index("dp")
        start = self.offset(halved)
        if kind == "halve":
            source = start + (1 - bit_of(me, bit)) * size
        elif kind == "whole":
            source = start
        else:
            source = start + bit_of(me, bit) * size
        block = pl.ds(pl.multiple_of(source, 16), size)
        return pltpu.make_async_remote_copy(
            src_ref=(self.final if kind == "double" else self.total).at[block],
            dst_ref=self.final.at[block] if kind == "double" else self.inbox.at[pl.ds(inbase, size)],
            send_sem=self.send.at[self.sem + n],
            recv_sem=self.recv.at[self.sem + n],
            device_id={"dp": flip(me, bit)},
            device_id_type=MESH,
        )

    def start(self, n):
        if n < self.steps:
            self.copy(n).start()

    def finish(self, n):
        if n >= self.steps:
            return
        self.copy(n).wait()
        kind, bit, size, inbase, halved = self.plan[n]
        if kind == "double":
            return
        keep = self.offset(halved)
        if kind == "halve":
            keep = keep + bit_of(lax.axis_index("dp"), bit) * size
        tile = 48 if size % 48 == 0 else 16

        @pl.loop(0, size // tile)
        def _(j):
            mine = pl.ds(pl.multiple_of(keep + j * tile, 16), tile)
            came = pl.ds(pl.multiple_of(inbase + j * tile, 16), tile)
            added = self.total[mine, :].astype(F32) + self.inbox[came, :].astype(F32)
            self.total[mine, :] = added.astype(BF16)

        if n + 1 == self.steps or self.plan[n + 1][0] == "double":
            block = pl.ds(pl.multiple_of(keep, 16), size)
            slot = self.sem + self.steps
            store = pltpu.make_async_copy(self.total.at[block], self.final.at[block], self.send.at[slot])
            store.start()
            store.wait()


class Gather:
    def __init__(self, rows, dp, send, recv, first_sem):
        self.rows, self.send, self.recv, self.sem = rows, send, recv, first_sem
        self.bits = list(reversed(range(dp.bit_length() - 1))) + [None]
        self.steps = len(self.bits)

    def place(self):
        at, weight = 0, 1
        for bit in self.bits:
            index = lax.axis_index("tensor") if bit is None else lax.axis_index("dp")
            at = at + bit_of(index, bit or 0) * weight
            weight *= 2
        return at

    def own(self, row, sem):
        store = pltpu.make_async_copy(row, self.rows.at[self.place()], sem)
        store.start()
        store.wait()

    def copy(self, n):
        bit, size = self.bits[n], 1 << n
        block = self.rows.at[pl.ds((self.place() // size) * size, size)]
        axis = "tensor" if bit is None else "dp"
        return pltpu.make_async_remote_copy(
            src_ref=block,
            dst_ref=block,
            send_sem=self.send.at[self.sem + n],
            recv_sem=self.recv.at[self.sem + n],
            device_id={axis: flip(lax.axis_index(axis), bit or 0)},
            device_id_type=MESH,
        )

    def start(self, n):
        if n < self.steps:
            self.copy(n).start()

    def finish(self, n):
        if n < self.steps:
            self.copy(n).wait()


def norm_back(gn, xhat, rstd, gain):
    y = gn * gain
    mean_y = jnp.mean(y, axis=-1, keepdims=True)
    mean_yx = jnp.mean(y * xhat, axis=-1, keepdims=True)
    return rstd * (y - mean_y - xhat * mean_yx)


def col_sum(v):
    return jnp.sum(v, axis=0, keepdims=True)


class Steps:
    def __init__(self, *streams):
        self.streams, self.done = streams, [0] * len(streams)

    def start(self):
        for stream in self.streams:
            stream.start(0)

    def advance(self):
        for n, stream in enumerate(self.streams):
            if self.done[n] < stream.steps:
                stream.finish(self.done[n])
                stream.start(self.done[n] + 1)
                self.done[n] += 1

    def busy(self):
        return any(done < stream.steps for done, stream in zip(self.done, self.streams))


def block_kernel(
    dp, lengths, time, tok_h, cot_h, qkv_h, out_wh, up_h, dn_h, ada_h, small, freq, inverse,
    out_h, gtok_h, gmlp_h, gatt_h, rows_h, adaw_h, totals_o,
    tok, cot, qkv_s, out_s, w_s, n2, act, pre, gml, br_own, br_par, ml_own, ml_par, gn_own, gn_par, gn1_par,
    gmid, dk, dv, gproj, qt, kt, q, k, v, att, normed, stat, cos_s, sin_s, bound, mod, small_par,
    box1, box2, inbox1, inbox2, vec_own, vec_par, row_own, rows_s, sums,
    load_sem, y_send, y_recv, c_send, c_recv, d_send, d_recv, o_sem,
):
    length, model = tok.shape
    local = out_wh.shape[0]
    hidden = up_h.shape[1]
    cond = freq.shape[1]
    width = 2 * local
    heads = width // HEAD_DIM
    chunks = length // ROWS
    tensor, here_dp = lax.axis_index("tensor"), lax.axis_index("dp")
    core = lax.rem(tensor, 2)
    other_core, other_y = flip(tensor, 0), flip(tensor, 1)
    bits = dp.bit_length() - 1
    scale = 1.0 / math.sqrt(HEAD_DIM)
    vt = gproj.at[pl.ds(2 * width, width)]

    barrier = pltpu.get_barrier_semaphore()
    for peer in [{"tensor": other_core}, {"tensor": other_y}] + [{"dp": flip(here_dp, b)} for b in range(bits)]:
        pl.semaphore_signal(barrier, inc=1, device_id=peer, device_id_type=MESH)

    mine_rows = pl.ds(pl.multiple_of(core * length, 16), length)
    moves = (
        (ada_h, act.at[pl.ds(0, ada_h.shape[0]), pl.ds(0, model)]),
        (tok_h.at[mine_rows], tok),
        (qkv_h, qkv_s.at[:, pl.ds(0, local)]),
        (out_wh, out_s.at[pl.ds(0, local)]),
        (up_h, w_s.at[pl.ds(0, model)]),
        (dn_h, w_s.at[pl.ds(2 * model, hidden)]),
        (cot_h.at[mine_rows], cot),
    )
    loads = [pltpu.make_async_copy(source, target, load_sem.at[n]) for n, (source, target) in enumerate(moves)]
    for load in loads:
        load.start()

    def rows_of(i):
        return pl.ds(pl.multiple_of(i * ROWS, ROWS), ROWS)

    def to_y(source, target, n):
        return pltpu.make_async_remote_copy(
            src_ref=source, dst_ref=target, send_sem=y_send.at[n], recv_sem=y_recv.at[n],
            device_id={"tensor": other_y}, device_id_type=MESH,
        )

    def to_core(source, target, n):
        return pltpu.make_async_remote_copy(
            src_ref=source, dst_ref=target, send_sem=c_send.at[n], recv_sem=c_recv.at[n],
            device_id={"tensor": other_core}, device_id_type=MESH,
        )

    def br_copy(i):
        return to_y(br_own.at[rows_of(i)], br_par.at[rows_of(i)], i)

    def gn_copy(i):
        return to_y(gn_own.at[rows_of(i)], gn_par.at[rows_of(i)], chunks + i)

    def ml_copy(i):
        return to_y(ml_own.at[rows_of(i)], ml_par.at[rows_of(i)], 2 * chunks + i)

    def gn1_copy(i):
        return to_y(n2.at[rows_of(i)], gn1_par.at[rows_of(i)], 3 * chunks + i)

    def vec_copy(n):
        return to_y(vec_own.at[n], vec_par.at[n], 4 * chunks + n)

    shares = [
        to_core(qkv_h, qkv_s.at[:, pl.ds(local, local)], 0),
        to_core(out_wh, out_s.at[pl.ds(local, local)], 1),
        to_core(small, small_par, 2),
        to_core(up_h, w_s.at[pl.ds(model, model)], 3),
        to_core(dn_h, w_s.at[pl.ds(2 * model + hidden, hidden)], 4),
    ]
    pl.semaphore_wait(barrier, 2 + bits)
    for share in shares:
        share.start()

    gain1, gain2, downb = small[0:1, :], small[1:2, :], small[3:4, :]
    when = time[core].astype(F32)
    angle = jnp.broadcast_to(freq[...] * when, (8, cond))
    lane = lax.broadcasted_iota(jnp.int32, (8, cond), 1)
    feats = jnp.where(lane < cond // 2, jnp.cos(angle), jnp.sin(angle))
    high = feats.astype(BF16)
    rest = feats - high.astype(F32)
    middle_part = rest.astype(BF16)
    low_part = (rest - middle_part.astype(F32)).astype(BF16)
    sums[...] = jnp.zeros_like(sums)
    vec_own[...] = jnp.zeros_like(vec_own)
    row_own[...] = jnp.zeros_like(row_own)
    row_own[1, 3:4, :cond] = feats[0:1, :]
    place = lax.broadcasted_iota(jnp.int32, (8, length), 1)
    start, begin, end = jnp.int32(0), jnp.zeros((8, length), jnp.int32), jnp.zeros((8, length), jnp.int32)
    for n in range(lengths.shape[1]):
        size = lengths[core, n]
        end = end + jnp.where(place >= start, size, 0)
        start = start + size
        begin = begin + jnp.where(place >= start, size, 0)
    bound[0:8, :] = begin
    bound[8:16, :] = end
    turns = inverse[...] * (place - begin)[0:1, :].astype(F32)
    cos_s[...] = jnp.cos(turns)
    sin_s[...] = jnp.sin(turns)
    loads[0].wait()
    for j in range(6):
        ada = act[j * cond : (j + 1) * cond, :model]
        vec = mm(high, ada) + mm(middle_part, ada) + mm(low_part, ada)
        mod[j : j + 1, :] = vec[0:1, :] + small[4 + j : 5 + j, :]
    for n in (1, 2):
        loads[n].wait()
    shares[0].wait()

    def project(i):
        r = rows_of(i)
        xhat, _ = norm_parts(tok[r, :].astype(F32))
        x1 = (xhat * gain1 * (1.0 + mod[1:2, :]) + mod[0:1, :]).astype(BF16)
        normed[r, :] = x1
        c, s = cos_s[:, r], sin_s[:, r]
        for part, (t_o, r_o) in enumerate(((qt, q), (kt, k), (vt, v))):
            turned = mm(qkv_s[part], x1, NT)
            if part < 2:
                pieces = []
                for h in range(heads):
                    a = turned[h * HEAD_DIM : h * HEAD_DIM + HALF]
                    b = turned[h * HEAD_DIM + HALF : (h + 1) * HEAD_DIM]
                    pieces += [a * c - b * s, b * c + a * s]
                turned = jnp.concatenate(pieces, axis=0)
            if part == 0:
                turned = turned * scale
            t_o[:, r] = turned.astype(BF16)
            r_o[r, :] = turned.T.astype(BF16)

    def allowed_keys(r, keys):
        place = lax.broadcasted_iota(jnp.int32, (keys.size, ROWS), 0) + keys.start
        return (place >= bound[0:1, r]) & (place < bound[8:9, r])

    def attend(i, keys):
        r = rows_of(i)
        allowed = allowed_keys(r, keys)
        for h in range(heads):
            pair = slice((h // 2) * 2 * HEAD_DIM, (h // 2 + 1) * 2 * HEAD_DIM)
            mine = slice(h * HEAD_DIM, (h + 1) * HEAD_DIM)
            scores = mm(k[keys, pair], only_half(qt[mine, r], h % 2))
            scores = jnp.where(allowed, scores, -1000000000.0)
            top = jnp.max(scores, axis=0, keepdims=True)
            terms = jnp.exp(scores - top)
            inv = 1.0 / jnp.sum(terms, axis=0, keepdims=True)
            att[mine, r] = mm(vt[mine, keys], (terms * inv).astype(BF16)).astype(BF16)
            stat[h : h + 1, r] = top
            stat[8 + h : 9 + h, r] = inv
        br_own[r, :] = mm(att[:, r], out_s[...], TN).astype(BF16)
        br_copy(i).start()

    reach = min(length, ROWS + LONGEST)
    first_keys, last_keys = pl.ds(0, reach), pl.ds(length - reach, reach)

    pl.loop(0, reach // ROWS)(project)
    loads[3].wait()
    shares[1].wait()
    attend(0, first_keys)
    pl.loop(reach // ROWS, chunks)(project)

    @pl.loop(1, chunks - 1)
    def _(i):
        attend(i, pl.ds(0, length))

    attend(chunks - 1, last_keys)

    for n in (4, 5, 6):
        loads[n].wait()
    for n in (2, 3, 4):
        shares[n].wait()

    @pl.loop(0, chunks)
    def _(i):
        r = rows_of(i)
        br_copy(i).wait_recv()
        middle = tok[r, :].astype(F32) + mod[2:3, :] * (br_own[r, :].astype(F32) + br_par[r, :].astype(F32))
        xhat, _ = norm_parts(middle)
        x2 = (xhat * gain2 * (1.0 + mod[4:5, :]) + mod[3:4, :]).astype(BF16)
        n2[r, :] = x2
        grad_out = cot[r, :].astype(F32)
        g = (mod[5:6, :] * grad_out).astype(BF16)
        gml[r, :] = g
        part = jnp.zeros((ROWS, model), F32)
        grad = jnp.zeros((ROWS, model), F32)
        for n in range(2):
            up, down = w_s.at[pl.ds(n * model, model)], w_s.at[pl.ds(2 * model + n * hidden, hidden)]
            cols = slice(n * hidden, (n + 1) * hidden)
            z = mm(x2, up[...]) + (small_par if n else small)[2:3, :hidden]
            square = z * z
            t = jnp.tanh(GELU_A * z * (1.0 + GELU_B * square))
            a = (0.5 * z * (1.0 + t)).astype(BF16)
            act[r, cols] = a
            slope = 0.5 * (1.0 + t) + (0.5 * GELU_A) * z * (1.0 - t * t) * (1.0 + 3.0 * GELU_B * square)
            part = part + mm(a, down[...])
            p = (mm(g, down[...], NT) * slope).astype(BF16)
            pre[r, cols] = p
            sums[n : n + 1, :hidden] += col_sum(p.astype(F32))
            grad = grad + mm(p, up[...], NT)
        ml_own[r, :] = part.astype(BF16)
        gn_own[r, :] = grad.astype(BF16)
        vec_own[0, 0:1, :] += col_sum(grad_out * part)
        sums[2:3, :] += col_sum(grad_out)
        gn_copy(i).start()

    vec_copy(0).start()

    def up_grad(j, n):
        cols = pl.ds(pl.multiple_of(j * ROWS, ROWS), ROWS)
        return mm(n2[:, cols], pre[:, n * hidden : (n + 1) * hidden], TN)

    def down_grad(j, n):
        cols = pl.ds(pl.multiple_of(n * hidden + j * ROWS, ROWS), ROWS)
        return mm(act[:, cols], gml[...], TN)

    outbox = w_s.at[pl.ds(2 * model, model + hidden)]

    @pl.loop(0, model // ROWS)
    def _(j):
        outbox[rows_of(j), :] = up_grad(j, 1).astype(BF16)

    up_copy = to_core(outbox.at[pl.ds(0, model)], box1.at[pl.ds(0, model)], 5)
    up_copy.start()

    @pl.loop(0, hidden // ROWS)
    def _(j):
        outbox[pl.ds(pl.multiple_of(model + j * ROWS, ROWS), ROWS), :] = down_grad(j, 1).astype(BF16)

    down_copy = to_core(outbox.at[pl.ds(model, hidden)], box1.at[pl.ds(model, hidden)], 6)
    down_copy.start()
    up_copy.wait()

    @pl.loop(0, model // ROWS)
    def _(j):
        r = rows_of(j)
        w_s[r, :] = (up_grad(j, 0) + box1[r, :].astype(F32)).astype(BF16)

    order = list(range(bits))
    turned_order = order[1:2] + order[:1] + order[2:]
    red_up = Reduce(w_s, 0, model, inbox1, 0, order, gmlp_h, d_send, d_recv, 0)
    red_up.start(0)
    down_copy.wait()

    @pl.loop(0, hidden // ROWS)
    def _(j):
        r = pl.ds(pl.multiple_of(model + j * ROWS, ROWS), ROWS)
        w_s[r, :] = (down_grad(j, 0) + box1[r, :].astype(F32)).astype(BF16)

    first = red_up.steps + 1
    red_down = Reduce(w_s, model, hidden, inbox1, red_up.inend, turned_order, gmlp_h, d_send, d_recv, first)
    red_down.start(0)
    first += red_down.steps + 1
    mlp_sums = Steps(red_up, red_down)

    dk[...] = jnp.zeros_like(dk)
    dv[...] = jnp.zeros_like(dv)

    @pl.loop(0, chunks)
    def _(i):
        r = rows_of(i)
        gn_copy(i).wait_recv()

        @pl.when(i == chunks - 1)
        def _():
            for n in range(chunks):
                ml_copy(n).start()

        branch = br_own[r, :].astype(F32) + br_par[r, :].astype(F32)
        xhat, rstd = norm_parts(tok[r, :].astype(F32) + mod[2:3, :] * branch)
        gn = gn_own[r, :].astype(F32) + gn_par[r, :].astype(F32)
        g = cot[r, :].astype(F32) + norm_back(gn, xhat, rstd, (1.0 + mod[4:5, :]) * gain2)
        gmid[r, :] = g
        sums[3:4, :] += col_sum(gn)
        sums[4:5, :] += col_sum(gn * xhat)
        sums[5:6, :] += col_sum(g * branch)
        gb = (mod[2:3, :] * g).astype(BF16)
        gml[r, :] = gb
        do_t = mm(out_s[...], gb, NT).astype(BF16)
        do = mm(gb, out_s[...], NT).astype(BF16)
        allowed = allowed_keys(r, pl.ds(0, length))
        lane = lax.broadcasted_iota(jnp.int32, (ROWS, 2 * HEAD_DIM), 1)
        c, s = cos_s[:, r], sin_s[:, r]
        for p in range(heads // 2):
            pair = slice(p * 2 * HEAD_DIM, (p + 1) * 2 * HEAD_DIM)
            dk_sum, dv_sum = dk[:, pair], dv[:, pair]
            for n in range(2):
                h = 2 * p + n
                mine = slice(h * HEAD_DIM, (h + 1) * HEAD_DIM)
                scores = mm(k[:, pair], only_half(qt[mine, r], n))
                probs = jnp.where(allowed, jnp.exp(scores - stat[h : h + 1, r]), 0.0) * stat[8 + h : 9 + h, r]
                grad_p = mm(v[:, pair], only_half(do_t[mine, :], n))
                centre = col_sum(probs * grad_p)
                grad_s = (probs * (grad_p - centre)).astype(BF16)
                dq = mm(kt[mine, :], grad_s) * scale
                ua, ub = dq[:HALF], dq[HALF:]
                gproj[h * HEAD_DIM : h * HEAD_DIM + HALF, r] = (ua * c + ub * s).astype(BF16)
                gproj[h * HEAD_DIM + HALF : (h + 1) * HEAD_DIM, r] = (ub * c - ua * s).astype(BF16)
                here = (lane >= HEAD_DIM) if n else (lane < HEAD_DIM)
                none = jnp.zeros((ROWS, 2 * HEAD_DIM), BF16)
                dk_sum = dk_sum + mm(grad_s, jnp.where(here, q[r, pair], none))
                dv_sum = dv_sum + mm(probs.astype(BF16), jnp.where(here, do[:, pair], none))
            dk[:, pair] = dk_sum
            dv[:, pair] = dv_sum
        for step, n in enumerate((chunks - 2, chunks - 1)):

            @pl.when(i == n)
            def _():
                for stream in mlp_sums.streams:
                    stream.finish(step)
                    stream.start(step + 1)

    mlp_sums.done = [2, 2]

    vec_copy(0).wait()
    early = Gather(rows_h.at[0], dp, d_send, d_recv, first)
    first += early.steps
    row_own[0, 0:1, :] = sums[3:4, :]
    row_own[0, 1:2, :] = sums[4:5, :] * gain2
    row_own[0, 2:3, :] = sums[5:6, :]
    row_own[0, 3:4, :] = vec_own[0, 0:1, :] + vec_par[0, 0:1, :] + sums[2:3, :] * downb
    row_own[0, 4:5, :] = mod[5:6, :] * sums[2:3, :]
    row_own[0, 5:6, :] = (1.0 + mod[4:5, :]) * sums[4:5, :]
    row_own[0, 6:7, :] = jnp.where(core == 0, sums[0:1, :], sums[1:2, :])
    row_own[0, 7:8, :] = jnp.where(core == 0, sums[1:2, :], sums[0:1, :])
    early.own(row_own.at[0], load_sem.at[0])
    early.start(0)
    for n in range(chunks):
        br_copy(n).wait_send()
        gn_copy(n).wait_send()

    @pl.loop(0, chunks)
    def _(i):
        r = rows_of(i)
        c, s = cos_s[:, r], sin_s[:, r]
        turned = dk[r, :].T
        pieces = []
        for h in range(heads):
            ua = turned[h * HEAD_DIM : h * HEAD_DIM + HALF]
            ub = turned[h * HEAD_DIM + HALF : (h + 1) * HEAD_DIM]
            pieces += [ua * c + ub * s, ub * c - ua * s]
        gproj[width : 2 * width, r] = jnp.concatenate(pieces, axis=0).astype(BF16)
        gproj[2 * width :, r] = dv[r, :].T.astype(BF16)

    sent2 = w_s.at[pl.ds(2 * model, 4 * local)]
    gatt = w_s.at[pl.ds(2 * model + 4 * local, 4 * local)]

    def att_grads(n):
        for part in range(3):
            rows = slice((2 * part + n) * local, (2 * part + n + 1) * local)
            yield mm(gproj[rows, :], normed[...])
        yield mm(att[n * local : (n + 1) * local, :], gml[...])

    for part, piece in enumerate(att_grads(1)):
        sent2[part * local : (part + 1) * local, :] = piece.astype(BF16)
    att_copy = to_core(sent2, box2, 7)
    att_copy.start()

    @pl.loop(0, chunks)
    def _(i):
        r = rows_of(i)
        gn = jnp.zeros((ROWS, model), F32)
        for part in range(3):
            gn = gn + mm(gproj[part * width : (part + 1) * width, r], qkv_s[part], TN)
        n2[r, :] = gn.astype(BF16)
        xhat, _ = norm_parts(tok[r, :].astype(F32))
        vec_own[1, 0:1, :] += col_sum(gn)
        vec_own[1, 1:2, :] += col_sum(gn * xhat)

    vec_copy(1).start()
    for n in range(chunks):
        gn1_copy(n).start()
    for part, piece in enumerate(att_grads(0)):
        gatt[part * local : (part + 1) * local, :] = piece.astype(BF16)
    att_copy.wait()
    for part in range(4):
        rows = slice(part * local, (part + 1) * local)
        gatt[rows, :] = (gatt[rows, :].astype(F32) + box2[rows, :].astype(F32)).astype(BF16)
    red_a = Reduce(gatt, 0, width, inbox2, 0, order, gatt_h, d_send, d_recv, first)
    first += red_a.steps + 1
    red_b = Reduce(gatt, width, width, inbox2, red_a.inend, turned_order, gatt_h, d_send, d_recv, first)
    first += red_b.steps + 1
    att_sums = Steps(red_a, red_b)
    att_sums.start()
    mlp_sums.advance()
    early_steps = Steps(early)
    early_steps.advance()
    late = Gather(rows_h.at[1], dp, d_send, d_recv, first)
    late_steps = Steps(late)

    out_copies = []

    def hand_over(source, target, i, n):
        rows = pl.ds(pl.multiple_of(core * length + i * ROWS, 16), ROWS)
        keep = pltpu.make_async_copy(source, target.at[rows], o_sem.at[n])
        give = to_core(source, target.at[rows], 8 + n)
        keep.start()
        give.start()
        out_copies.append((keep, give))

    def output_chunk(i):
        r = slice(i * ROWS, (i + 1) * ROWS)
        ml_copy(i).wait()
        middle = tok[r, :].astype(F32) + mod[2:3, :] * (br_own[r, :].astype(F32) + br_par[r, :].astype(F32))
        total = ml_own[r, :].astype(F32) + ml_par[r, :].astype(F32) + downb
        act[r, :model] = (middle + mod[5:6, :] * total).astype(BF16)
        hand_over(act.at[r, :model], out_h, i, i)

    def token_chunk(i):
        r = slice(i * ROWS, (i + 1) * ROWS)
        gn1_copy(i).wait()
        xhat, rstd = norm_parts(tok[r, :].astype(F32))
        gn = n2[r, :].astype(F32) + gn1_par[r, :].astype(F32)
        g = gmid[r, :] + norm_back(gn, xhat, rstd, (1.0 + mod[1:2, :]) * gain1)
        act[r, model : 2 * model] = g.astype(BF16)
        hand_over(act.at[r, model : 2 * model], gtok_h, i, chunks + i)

    att_sums.advance()
    early_steps.advance()
    output_chunk(0)
    mlp_sums.advance()
    att_sums.advance()
    early_steps.advance()
    output_chunk(1)
    output_chunk(2)
    vec_copy(1).wait()
    shift_a = vec_own[1, 0:1, :] + vec_par[1, 0:1, :]
    scale_a = vec_own[1, 1:2, :] + vec_par[1, 1:2, :]
    row_own[1, 0:1, :] = shift_a
    row_own[1, 1:2, :] = scale_a * gain1
    row_own[1, 2:3, :] = (1.0 + mod[1:2, :]) * scale_a
    late.own(row_own.at[1], load_sem.at[1])
    late.start(0)
    att_sums.advance()
    late_steps.advance()
    early_steps.advance()
    for i in range(3, chunks):
        output_chunk(i)
    att_sums.advance()
    mlp_sums.advance()
    late_steps.advance()
    token_chunk(0)
    late_steps.advance()
    att_sums.advance()
    while late_steps.busy() or early_steps.busy():
        early_steps.advance()
        late_steps.advance()

    slots = 2 * dp
    group = min(slots, GROUP)
    totals_o[...] = jnp.zeros_like(totals_o)
    picks = ((1, 0), (1, 1), (0, 2), (0, 0), (0, 1), (0, 3))
    for first_slot in range(0, slots, group):
        takes = [
            pltpu.make_async_copy(rows_h.at[n, pl.ds(first_slot, group)], rows_s.at[n], load_sem.at[n])
            for n in range(2)
        ]
        for take in takes:
            take.start()
        for take in takes:
            take.wait()

        def pick(n, row):
            return jnp.concatenate([rows_s[n, g, row : row + 1, :] for g in range(group)], axis=0)

        feat = pick(1, 3)[:, :cond]
        for j, (n, row) in enumerate(picks):
            vecs = pick(n, row)
            totals_o[j : j + 1, :] += col_sum(vecs)
            outer = lax.dot_general(feat, vecs, TN, precision=PRECISE, preferred_element_type=F32)
            rows = slice(j * cond, (j + 1) * cond)
            for side, ref in enumerate((dk, dv)):
                cut = outer[:, side * width : (side + 1) * width]
                ref[rows, :] = cut if first_slot == 0 else ref[rows, :] + cut
        totals_o[6:7, :] += col_sum(pick(1, 2))
        totals_o[7:8, :] += col_sum(pick(0, 5))
        totals_o[8:9, :] += col_sum(pick(0, 4))
        totals_o[9:10, :] += jnp.where(core == 0, col_sum(pick(0, 6)), col_sum(pick(0, 7)))
    puts = [
        pltpu.make_async_copy(
            ref.at[pl.ds(0, 6 * cond)], adaw_h.at[:, pl.ds(side * width, width)], load_sem.at[2 + side]
        )
        for side, ref in enumerate((dk, dv))
    ]
    for put in puts:
        put.start()

    for i in range(1, chunks - 1):
        token_chunk(i)
    att_sums.advance()
    mlp_sums.advance()
    token_chunk(chunks - 1)
    while mlp_sums.busy() or att_sums.busy():
        mlp_sums.advance()
        att_sums.advance()
    for put in puts:
        put.wait()
    for keep, give in out_copies:
        keep.wait()
        give.wait()


def block_call(dp, lengths, time, hbm, small, freq, inverse):
    tokens, _, qkv_w, out_w, up_w, down_w, ada = hbm
    slot_count, model = time.shape[0], tokens.shape[1]
    length = tokens.shape[0] // slot_count
    hidden, local = up_w.shape[1], out_w.shape[0]
    width = 2 * local
    chunks = length // ROWS
    slots = slot_count * dp
    sems = 4 * (2 * dp.bit_length()) + 2 * dp.bit_length()
    any_spec, vmem_spec = pl.BlockSpec(memory_space=pl.ANY), pl.BlockSpec(memory_space=pltpu.VMEM)
    smem_spec = pl.BlockSpec(memory_space=pltpu.SMEM)
    inbox_rows = inbox_need(dp, model) + inbox_need(dp, hidden)
    inbox2_rows = 2 * inbox_need(dp, width)
    dma = pltpu.SemaphoreType.DMA

    def low(*shape):
        return pltpu.VMEM(shape, BF16)

    def full(*shape):
        return pltpu.VMEM(shape, F32)

    tokens_like = low(length, model)
    return pl.pallas_call(
        functools.partial(block_kernel, dp),
        in_specs=[smem_spec] * 2 + [any_spec] * len(hbm) + [vmem_spec] * 3,
        out_specs=[any_spec] * 6 + [vmem_spec],
        out_shape=[
            jax.ShapeDtypeStruct(tokens.shape, BF16),
            jax.ShapeDtypeStruct(tokens.shape, BF16),
            jax.ShapeDtypeStruct((model + hidden, model), BF16),
            jax.ShapeDtypeStruct((4 * local, model), BF16),
            jax.ShapeDtypeStruct((2, slots, 8, model), F32),
            jax.ShapeDtypeStruct(ada.shape, F32),
            jax.ShapeDtypeStruct((16, model), F32),
        ],
        scratch_shapes=[
            tokens_like, tokens_like, low(3, width, model), low(width, model), low(2 * (model + hidden), model),
            tokens_like, low(length, 2 * hidden), low(length, 2 * hidden), tokens_like,
            tokens_like, tokens_like, tokens_like, tokens_like, tokens_like, tokens_like, tokens_like,
            full(length, model), full(length, width), full(length, width), low(3 * width, length),
            low(width, length), low(width, length), low(length, width), low(length, width), low(length, width),
            low(width, length), tokens_like, full(16, length), full(HALF, length), full(HALF, length),
            pltpu.VMEM((16, length), jnp.int32), full(8, model), full(*small.shape),
            low(model + hidden, model), low(4 * local, model), low(inbox_rows, model),
            low(inbox2_rows, model), full(2, 8, model), full(2, 8, model), full(2, 8, model),
            full(2, min(slots, GROUP), 8, model), full(8, model),
            dma((7,)), dma((4 * chunks + 2,)), dma((4 * chunks + 2,)), dma((8 + 2 * chunks,)), dma((8 + 2 * chunks,)),
            dma((sems,)), dma((sems,)), dma((2 * chunks,)),
        ],
        compiler_params=pltpu.CompilerParams(
            collective_id=0, has_side_effects=True, vmem_limit_bytes=VMEM_LIMIT
        ),
        cost_estimate=pl.CostEstimate(flops=80_000_000_000, bytes_accessed=40_000_000, transcendentals=0),
        name="transformer_block",
    )(lengths, time, *hbm, small, freq, inverse)


def inbox_need(dp, rows):
    need = 0
    for _ in range(dp.bit_length() - 1):
        if rows % 32 == 0:
            rows //= 2
        need += rows
    return need


def finish_kernel(*refs):
    half = len(refs) // 2
    for source, target in zip(refs[:half], refs[half:]):
        target[...] = source[...].astype(target.dtype)


def finish_call(output, grad_tok, adaw, g_mlp, g_att, model, hidden, local):
    steps = 4

    def rows(count, start=0):
        return pl.BlockSpec((count // steps, model), lambda i: (start * steps // count + i, 0))

    whole = [a.shape[0] for a in (output, grad_tok, adaw)]
    parts = ((model, 0), (hidden, model), (3 * local, 0), (local, 3 * local))
    return pl.pallas_call(
        finish_kernel,
        grid=(steps,),
        in_specs=[rows(count) for count in whole] + [rows(*part) for part in parts],
        out_specs=[rows(count) for count in whole] + [rows(count) for count, _ in parts],
        out_shape=[jax.ShapeDtypeStruct(a.shape, a.dtype) for a in (output, grad_tok, adaw)]
        + [jax.ShapeDtypeStruct((count, model), F32) for count, _ in parts],
        compiler_params=pltpu.CompilerParams(vmem_limit_bytes=VMEM_LIMIT),
        name="grads_to_float32",
    )(output, grad_tok, adaw, g_mlp, g_mlp, g_att, g_att)


def per_device(
    dp, tokens, lengths, time, qkv_weight, out_weight, up_weight, up_bias, down_weight, down_bias,
    gain_attn, gain_mlp, ada_weight, ada_bias, cotangent,
):
    model, local = tokens.shape[1], out_weight.shape[0]
    cond = ada_weight.shape[0]
    qkv = jnp.transpose(qkv_weight, (1, 2, 0))
    ada = jnp.transpose(ada_weight, (1, 0, 2)).reshape(6 * cond, model)
    bias = jnp.pad(up_bias, (0, model - up_bias.shape[0]))
    small = jnp.concatenate(
        [jnp.stack([gain_attn, gain_mlp, bias, down_bias]), ada_bias, jnp.zeros((6, model), ada_bias.dtype)]
    ).astype(F32)
    half = cond // 2
    freq = np.exp(np.arange(half) * (-math.log(10000.0) / half)).astype(np.float32)
    freq = jnp.asarray(np.concatenate([freq, freq])[None])
    inverse = jnp.asarray(np.exp(np.arange(HALF) * (-2.0 * math.log(10000.0) / HEAD_DIM)).astype(np.float32)[:, None])
    output, grad_tok, g_mlp, g_att, _, g_ada, totals = block_call(
        dp, lengths, time, [tokens, cotangent, qkv, out_weight, up_weight, down_weight, ada], small, freq, inverse
    )
    output, grad_tok, g_ada, g_up, g_down, g_qkv, g_out = finish_call(
        output, grad_tok, g_ada, g_mlp, g_att, model, up_bias.shape[0], local
    )
    return (
        output,
        grad_tok,
        jnp.transpose(g_qkv.reshape(3, local, model), (2, 0, 1)),
        g_out,
        g_up,
        totals[9, : up_bias.shape[0]],
        g_down,
        totals[8],
        totals[6],
        totals[7],
        jnp.transpose(g_ada.reshape(6, cond, model), (1, 0, 2)),
        totals[:6],
    )


def solution(mesh):
    in_specs = (
        P("dp", None), P("dp", None), P("dp"), P(None, None, "tensor"), P("tensor", None), P(None, "tensor"),
        P("tensor"), P("tensor", None), P(), P(), P(), P(), P(), P("dp", None),
    )
    out_specs = (
        P("dp", None), P("dp", None), P(None, None, "tensor"), P("tensor", None), P(None, "tensor"), P("tensor"),
        P("tensor", None), P(), P(), P(), P(), P(),
    )
    return jax.shard_map(
        functools.partial(per_device, mesh.shape["dp"]),
        mesh=mesh, in_specs=in_specs, out_specs=out_specs, check_vma=False,
    )
```

```python
import functools
import math

import jax
import jax.numpy as jnp
import numpy as np
from jax import lax
from jax.experimental import pallas as pl
from jax.experimental.pallas import tpu as pltpu
from jax.sharding import PartitionSpec as P

HEAD_DIM = 64
HALF = HEAD_DIM // 2
EPS = 1e-05
ROWS = 256
PRECISE = lax.Precision.HIGHEST
GROUP = 16
LONGEST = 512
VMEM_LIMIT = 61 * 1024 * 1024
F32 = jnp.float32
BF16 = jnp.bfloat16
GELU_A = math.sqrt(2.0 / math.pi)
GELU_B = 0.044715

NN = (((1,), (0,)), ((), ()))
NT = (((1,), (1,)), ((), ()))
TN = (((0,), (0,)), ((), ()))


def mm(left, right, dims=NN):
    return lax.dot_general(left, right, dims, preferred_element_type=F32)


def norm_parts(v):
    center = jnp.mean(v, axis=-1, keepdims=True)
    centered = v - center
    spread = jnp.mean(centered * centered, axis=-1, keepdims=True)
    rstd = lax.rsqrt(spread + EPS)
    return centered * rstd, rstd


def only_half(block, second):
    zero = jnp.zeros_like(block)
    return jnp.concatenate([zero, block] if second else [block, zero], axis=0)


MESH = pl.DeviceIdType.MESH


def bit_of(index, bit):
    return lax.rem(index // (1 << bit), 2)


def flip(index, bit):
    return index + (1 << bit) * (1 - 2 * bit_of(index, bit))


class Reduce:
    def __init__(self, total, base, rows, inbox, inbase, order, final, send, recv, first_sem):
        self.total, self.base, self.inbox, self.send, self.recv = total, base, inbox, send, recv
        self.final = final
        self.plan, self.sem = [], first_sem
        size, halved = rows, []
        for bit in order:
            if size % 32 == 0:
                self.plan.append(("halve", bit, size // 2, inbase, list(halved)))
                size //= 2
                halved.append((bit, size))
            else:
                self.plan.append(("whole", bit, size, inbase, list(halved)))
            inbase += size
        self.inend = inbase
        while halved:
            bit, size = halved.pop()
            self.plan.append(("double", bit, size, None, list(halved)))
        self.steps = len(self.plan)
        self.turn = next((n for n, step in enumerate(self.plan) if step[0] == "double"), self.steps)

    def offset(self, halved):
        me = lax.axis_index("dp")
        at = self.base
        for bit, size in halved:
            at = at + bit_of(me, bit) * size
        return at

    def copy(self, n):
        kind, bit, size, inbase, halved = self.plan[n]
        me = lax.axis_index("dp")
        start = self.offset(halved)
        if kind == "halve":
            source = start + (1 - bit_of(me, bit)) * size
        elif kind == "whole":
            source = start
        else:
            source = start + bit_of(me, bit) * size
        origin = self.final if kind == "double" and n > self.turn else self.total
        block = pl.ds(pl.multiple_of(source, 16), size)
        return pltpu.make_async_remote_copy(
            src_ref=origin.at[block],
            dst_ref=self.final.at[block] if kind == "double" else self.inbox.at[pl.ds(inbase, size)],
            send_sem=self.send.at[self.sem + n],
            recv_sem=self.recv.at[self.sem + n],
            device_id={"dp": flip(me, bit)},
            device_id_type=MESH,
        )

    def store(self):
        at = self.offset(self.plan[self.turn - 1][4])
        kind, bit, size = self.plan[self.turn - 1][:3]
        if kind == "halve":
            at = at + bit_of(lax.axis_index("dp"), bit) * size
        block = pl.ds(pl.multiple_of(at, 16), size)
        return pltpu.make_async_copy(self.total.at[block], self.final.at[block], self.send.at[self.sem + self.steps])

    def start(self, n):
        if n < self.steps:
            self.copy(n).start()

    def finish(self, n):
        if n >= self.steps:
            return
        self.copy(n).wait()
        kind, bit, size, inbase, halved = self.plan[n]
        if kind == "double":
            if n == self.turn:
                self.store().wait()
            return
        keep = self.offset(halved)
        if kind == "halve":
            keep = keep + bit_of(lax.axis_index("dp"), bit) * size
        tile = 48 if size % 48 == 0 else 16

        @pl.loop(0, size // tile)
        def _(j):
            mine = pl.ds(pl.multiple_of(keep + j * tile, 16), tile)
            came = pl.ds(pl.multiple_of(inbase + j * tile, 16), tile)
            added = self.total[mine, :].astype(F32) + self.inbox[came, :].astype(F32)
            self.total[mine, :] = added.astype(BF16)

        if n + 1 == self.turn:
            self.store().start()
            if self.turn == self.steps:
                self.store().wait()


class Gather:
    def __init__(self, rows, dp, send, recv, first_sem):
        self.rows, self.send, self.recv, self.sem = rows, send, recv, first_sem
        self.bits = list(reversed(range(dp.bit_length() - 1))) + [None]
        self.steps = len(self.bits)

    def place(self):
        at, weight = 0, 1
        for bit in self.bits:
            index = lax.axis_index("tensor") if bit is None else lax.axis_index("dp")
            at = at + bit_of(index, bit or 0) * weight
            weight *= 2
        return at

    def own(self, row, sem):
        store = pltpu.make_async_copy(row, self.rows.at[self.place()], sem)
        store.start()
        store.wait()

    def copy(self, n):
        bit, size = self.bits[n], 1 << n
        block = self.rows.at[pl.ds((self.place() // size) * size, size)]
        axis = "tensor" if bit is None else "dp"
        return pltpu.make_async_remote_copy(
            src_ref=block,
            dst_ref=block,
            send_sem=self.send.at[self.sem + n],
            recv_sem=self.recv.at[self.sem + n],
            device_id={axis: flip(lax.axis_index(axis), bit or 0)},
            device_id_type=MESH,
        )

    def start(self, n):
        if n < self.steps:
            self.copy(n).start()

    def finish(self, n):
        if n < self.steps:
            self.copy(n).wait()


def norm_back(gn, xhat, rstd, gain):
    y = gn * gain
    mean_y = jnp.mean(y, axis=-1, keepdims=True)
    mean_yx = jnp.mean(y * xhat, axis=-1, keepdims=True)
    return rstd * (y - mean_y - xhat * mean_yx)


def col_sum(v):
    return jnp.sum(v, axis=0, keepdims=True)


class Steps:
    def __init__(self, *streams):
        self.streams, self.done = streams, [0] * len(streams)

    def start(self):
        for stream in self.streams:
            stream.start(0)

    def advance(self):
        for n, stream in enumerate(self.streams):
            if self.done[n] < stream.steps:
                stream.finish(self.done[n])
                stream.start(self.done[n] + 1)
                self.done[n] += 1

    def busy(self):
        return any(done < stream.steps for done, stream in zip(self.done, self.streams))


def block_kernel(
    dp, lengths, time, tok_h, cot_h, qkv_h, out_wh, up_h, dn_h, ada_h, gain1_i, gain2_i, bias_i, downb_i, adab_i,
    freq, inverse,
    out_h, gtok_h, gmlp_h, gatt_h, rows_h, adaw_h, totals_o,
    tok, cot, qkv_s, out_s, w_s, n2, act, pre, gml, br_own, br_par, ml_own, ml_par, gn_own, gn_par, gn1_par,
    gmid, dk, dv, gproj, qt, kt, q, k, v, att, normed, stat, cos_s, sin_s, bound, mod, small, small_par,
    box1, box2, inbox1, inbox2, vec_own, vec_par, row_own, rows_s, sums,
    load_sem, y_send, y_recv, c_send, c_recv, d_send, d_recv, o_sem,
):
    length, model = tok.shape
    local = out_wh.shape[0]
    hidden = up_h.shape[1]
    cond = freq.shape[1]
    width = 2 * local
    heads = width // HEAD_DIM
    chunks = length // ROWS
    tensor, here_dp = lax.axis_index("tensor"), lax.axis_index("dp")
    core = lax.rem(tensor, 2)
    other_core, other_y = flip(tensor, 0), flip(tensor, 1)
    bits = dp.bit_length() - 1
    scale = 1.0 / math.sqrt(HEAD_DIM)
    vt = gproj.at[pl.ds(2 * width, width)]

    barrier = pltpu.get_barrier_semaphore()
    for peer in [{"tensor": other_core}, {"tensor": other_y}] + [{"dp": flip(here_dp, b)} for b in range(bits)]:
        pl.semaphore_signal(barrier, inc=1, device_id=peer, device_id_type=MESH)

    mine_rows = pl.ds(pl.multiple_of(core * length, 16), length)
    moves = (
        (ada_h, act.at[pl.ds(0, ada_h.shape[0]), pl.ds(0, model)]),
        (tok_h.at[mine_rows], tok),
        (qkv_h, qkv_s.at[:, pl.ds(0, local)]),
        (out_wh, out_s.at[pl.ds(0, local)]),
        (up_h, w_s.at[pl.ds(0, model)]),
        (dn_h, w_s.at[pl.ds(2 * model, hidden)]),
        (cot_h.at[mine_rows], cot),
    )
    loads = [pltpu.make_async_copy(source, target, load_sem.at[n]) for n, (source, target) in enumerate(moves)]
    for load in loads:
        load.start()

    def rows_of(i):
        return pl.ds(pl.multiple_of(i * ROWS, ROWS), ROWS)

    def to_y(source, target, n):
        return pltpu.make_async_remote_copy(
            src_ref=source, dst_ref=target, send_sem=y_send.at[n], recv_sem=y_recv.at[n],
            device_id={"tensor": other_y}, device_id_type=MESH,
        )

    def to_core(source, target, n):
        return pltpu.make_async_remote_copy(
            src_ref=source, dst_ref=target, send_sem=c_send.at[n], recv_sem=c_recv.at[n],
            device_id={"tensor": other_core}, device_id_type=MESH,
        )

    def br_copy(i):
        return to_y(br_own.at[rows_of(i)], br_par.at[rows_of(i)], i)

    def gn_copy(i):
        return to_y(gn_own.at[rows_of(i)], gn_par.at[rows_of(i)], chunks + i)

    def ml_copy(i):
        return to_y(ml_own.at[rows_of(i)], ml_par.at[rows_of(i)], 2 * chunks + i)

    def gn1_copy(i):
        return to_y(n2.at[rows_of(i)], gn1_par.at[rows_of(i)], 3 * chunks + i)

    def vec_copy(n):
        return to_y(vec_own.at[n], vec_par.at[n], 4 * chunks + n)

    for n, ref in enumerate((gain1_i, gain2_i, bias_i, downb_i)):
        small[n : n + 1, : ref.shape[0]] = ref[...].astype(F32).reshape(1, ref.shape[0])
    small[4:10, :] = adab_i[...].astype(F32)
    shares = [
        to_core(qkv_h, qkv_s.at[:, pl.ds(local, local)], 0),
        to_core(out_wh, out_s.at[pl.ds(local, local)], 1),
        to_core(small, small_par, 2),
        to_core(up_h, w_s.at[pl.ds(model, model)], 3),
        to_core(dn_h, w_s.at[pl.ds(2 * model + hidden, hidden)], 4),
    ]
    pl.semaphore_wait(barrier, 2 + bits)
    for share in shares:
        share.start()

    gain1, gain2, downb = small[0:1, :], small[1:2, :], small[3:4, :]
    when = time[core].astype(F32)
    angle = jnp.broadcast_to(freq[...] * when, (8, cond))
    lane = lax.broadcasted_iota(jnp.int32, (8, cond), 1)
    feats = jnp.where(lane < cond // 2, jnp.cos(angle), jnp.sin(angle))
    high = feats.astype(BF16)
    rest = feats - high.astype(F32)
    middle_part = rest.astype(BF16)
    low_part = (rest - middle_part.astype(F32)).astype(BF16)
    sums[...] = jnp.zeros_like(sums)
    vec_own[...] = jnp.zeros_like(vec_own)
    row_own[...] = jnp.zeros_like(row_own)
    row_own[11:12, :cond] = feats[0:1, :]
    place = lax.broadcasted_iota(jnp.int32, (8, length), 1)
    start, begin, end = jnp.int32(0), jnp.zeros((8, length), jnp.int32), jnp.zeros((8, length), jnp.int32)
    for n in range(lengths.shape[1]):
        size = lengths[core, n]
        end = end + jnp.where(place >= start, size, 0)
        start = start + size
        begin = begin + jnp.where(place >= start, size, 0)
    bound[0:8, :] = begin
    bound[8:16, :] = end
    turns = inverse[...] * (place - begin)[0:1, :].astype(F32)
    cos_s[...] = jnp.cos(turns)
    sin_s[...] = jnp.sin(turns)
    loads[0].wait()
    for j in range(6):
        ada = act[j * cond : (j + 1) * cond, :model]
        vec = mm(high, ada) + mm(middle_part, ada) + mm(low_part, ada)
        mod[j : j + 1, :] = vec[0:1, :] + small[4 + j : 5 + j, :]
    for n in (1, 2):
        loads[n].wait()
    shares[0].wait()

    def project(i):
        r = rows_of(i)
        xhat, _ = norm_parts(tok[r, :].astype(F32))
        x1 = (xhat * gain1 * (1.0 + mod[1:2, :]) + mod[0:1, :]).astype(BF16)
        normed[r, :] = x1
        c, s = cos_s[:, r], sin_s[:, r]
        for part, (t_o, r_o) in enumerate(((qt, q), (kt, k), (vt, v))):
            turned = mm(qkv_s[part], x1, NT)
            if part < 2:
                pieces = []
                for h in range(heads):
                    a = turned[h * HEAD_DIM : h * HEAD_DIM + HALF]
                    b = turned[h * HEAD_DIM + HALF : (h + 1) * HEAD_DIM]
                    pieces += [a * c - b * s, b * c + a * s]
                turned = jnp.concatenate(pieces, axis=0)
            if part == 0:
                turned = turned * scale
            t_o[:, r] = turned.astype(BF16)
            r_o[r, :] = turned.T.astype(BF16)

    def allowed_keys(r, keys):
        place = lax.broadcasted_iota(jnp.int32, (keys.size, ROWS), 0) + keys.start
        return (place >= bound[0:1, r]) & (place < bound[8:9, r])

    def attend(i, keys):
        r = rows_of(i)
        allowed = allowed_keys(r, keys)
        for h in range(heads):
            pair = slice((h // 2) * 2 * HEAD_DIM, (h // 2 + 1) * 2 * HEAD_DIM)
            mine = slice(h * HEAD_DIM, (h + 1) * HEAD_DIM)
            scores = mm(k[keys, pair], only_half(qt[mine, r], h % 2))
            scores = jnp.where(allowed, scores, -1000000000.0)
            top = jnp.max(scores, axis=0, keepdims=True)
            terms = jnp.exp(scores - top)
            inv = 1.0 / jnp.sum(terms, axis=0, keepdims=True)
            att[mine, r] = (mm(vt[mine, keys], terms.astype(BF16)) * inv).astype(BF16)
            stat[h : h + 1, r] = top
            stat[8 + h : 9 + h, r] = inv
        br_own[r, :] = mm(att[:, r], out_s[...], TN).astype(BF16)
        br_copy(i).start()

    reach = min(length, ROWS + LONGEST)
    first_keys, last_keys = pl.ds(0, reach), pl.ds(length - reach, reach)

    pl.loop(0, reach // ROWS)(project)
    loads[3].wait()
    shares[1].wait()
    attend(0, first_keys)
    pl.loop(reach // ROWS, chunks)(project)

    @pl.loop(1, chunks - 1)
    def _(i):
        attend(i, pl.ds(0, length))

    attend(chunks - 1, last_keys)

    for n in (4, 5, 6):
        loads[n].wait()
    for n in (2, 3, 4):
        shares[n].wait()

    @pl.loop(0, chunks)
    def _(i):
        r = rows_of(i)
        br_copy(i).wait_recv()
        middle = tok[r, :].astype(F32) + mod[2:3, :] * (br_own[r, :].astype(F32) + br_par[r, :].astype(F32))
        xhat, _ = norm_parts(middle)
        x2 = (xhat * gain2 * (1.0 + mod[4:5, :]) + mod[3:4, :]).astype(BF16)
        n2[r, :] = x2
        grad_out = cot[r, :].astype(F32)
        g = (mod[5:6, :] * grad_out).astype(BF16)
        gml[r, :] = g
        part = jnp.zeros((ROWS, model), F32)
        grad = jnp.zeros((ROWS, model), F32)
        for n in range(2):
            up, down = w_s.at[pl.ds(n * model, model)], w_s.at[pl.ds(2 * model + n * hidden, hidden)]
            cols = slice(n * hidden, (n + 1) * hidden)
            z = mm(x2, up[...]) + (small_par if n else small)[2:3, :hidden]
            square = z * z
            t = jnp.tanh(GELU_A * z * (1.0 + GELU_B * square))
            a = (0.5 * z * (1.0 + t)).astype(BF16)
            act[r, cols] = a
            slope = 0.5 * (1.0 + t) + (0.5 * GELU_A) * z * (1.0 - t * t) * (1.0 + 3.0 * GELU_B * square)
            part = part + mm(a, down[...])
            p = (mm(g, down[...], NT) * slope).astype(BF16)
            pre[r, cols] = p
            sums[n : n + 1, :hidden] += col_sum(p.astype(F32))
            grad = grad + mm(p, up[...], NT)
        ml_own[r, :] = part.astype(BF16)
        gn_own[r, :] = grad.astype(BF16)
        vec_own[0, 0:1, :] += col_sum(grad_out * part)
        sums[2:3, :] += col_sum(grad_out)
        gn_copy(i).start()

    vec_copy(0).start()

    def up_grad(j, n):
        cols = pl.ds(pl.multiple_of(j * ROWS, ROWS), ROWS)
        return mm(n2[:, cols], pre[:, n * hidden : (n + 1) * hidden], TN)

    def down_grad(j, n):
        cols = pl.ds(pl.multiple_of(n * hidden + j * ROWS, ROWS), ROWS)
        return mm(act[:, cols], gml[...], TN)

    outbox = w_s.at[pl.ds(2 * model, model + hidden)]

    @pl.loop(0, model // ROWS)
    def _(j):
        outbox[rows_of(j), :] = up_grad(j, 1).astype(BF16)

    up_copy = to_core(outbox.at[pl.ds(0, model)], box1.at[pl.ds(0, model)], 5)
    up_copy.start()

    @pl.loop(0, hidden // ROWS)
    def _(j):
        outbox[pl.ds(pl.multiple_of(model + j * ROWS, ROWS), ROWS), :] = down_grad(j, 1).astype(BF16)

    down_copy = to_core(outbox.at[pl.ds(model, hidden)], box1.at[pl.ds(model, hidden)], 6)
    down_copy.start()
    up_copy.wait()

    @pl.loop(0, model // ROWS)
    def _(j):
        r = rows_of(j)
        w_s[r, :] = (up_grad(j, 0) + box1[r, :].astype(F32)).astype(BF16)

    order = list(range(bits))
    turned_order = order[1:2] + order[:1] + order[2:]
    orders = (order, turned_order)
    used = [0]

    def streams(total, base, rows, count, shift, inbox, inbase, final):
        made = []
        for n in range(count):
            size = rows // count
            made.append(
                Reduce(total, base + n * size, size, inbox, inbase, orders[(n + shift) % 2], final, d_send, d_recv, used[0])
            )
            inbase = made[-1].inend
            used[0] += made[-1].steps + 1
        return made, inbase

    red_up, inbase = streams(w_s, 0, model, 2, 0, inbox1, 0, gmlp_h)
    for stream in red_up:
        stream.start(0)
    down_copy.wait()

    @pl.loop(0, hidden // ROWS)
    def _(j):
        r = pl.ds(pl.multiple_of(model + j * ROWS, ROWS), ROWS)
        w_s[r, :] = (down_grad(j, 0) + box1[r, :].astype(F32)).astype(BF16)

    red_down, _ = streams(w_s, model, hidden, 2, 0, inbox1, inbase, gmlp_h)
    for stream in red_down:
        stream.start(0)
    mlp_sums = Steps(*red_up, *red_down)

    dk[...] = jnp.zeros_like(dk)
    dv[...] = jnp.zeros_like(dv)

    @pl.loop(0, chunks)
    def _(i):
        r = rows_of(i)
        gn_copy(i).wait_recv()

        @pl.when(i == chunks - 1)
        def _():
            for n in range(chunks - 1):
                ml_copy(n).start()

        branch = br_own[r, :].astype(F32) + br_par[r, :].astype(F32)
        xhat, rstd = norm_parts(tok[r, :].astype(F32) + mod[2:3, :] * branch)
        gn = gn_own[r, :].astype(F32) + gn_par[r, :].astype(F32)
        g = cot[r, :].astype(F32) + norm_back(gn, xhat, rstd, (1.0 + mod[4:5, :]) * gain2)
        gmid[r, :] = g
        sums[3:4, :] += col_sum(gn)
        sums[4:5, :] += col_sum(gn * xhat)
        sums[5:6, :] += col_sum(g * branch)
        gb = (mod[2:3, :] * g).astype(BF16)
        gml[r, :] = gb
        do_t = mm(out_s[...], gb, NT).astype(BF16)
        do = mm(gb, out_s[...], NT).astype(BF16)
        allowed = allowed_keys(r, pl.ds(0, length))
        lane = lax.broadcasted_iota(jnp.int32, (ROWS, 2 * HEAD_DIM), 1)
        c, s = cos_s[:, r], sin_s[:, r]
        for p in range(heads // 2):
            pair = slice(p * 2 * HEAD_DIM, (p + 1) * 2 * HEAD_DIM)
            dk_sum, dv_sum = dk[:, pair], dv[:, pair]
            for n in range(2):
                h = 2 * p + n
                mine = slice(h * HEAD_DIM, (h + 1) * HEAD_DIM)
                scores = mm(k[:, pair], only_half(qt[mine, r], n))
                probs = jnp.where(allowed, jnp.exp(scores - stat[h : h + 1, r]), 0.0) * stat[8 + h : 9 + h, r]
                grad_p = mm(v[:, pair], only_half(do_t[mine, :], n))
                centre = col_sum(probs * grad_p)
                grad_s = (probs * (grad_p - centre)).astype(BF16)
                dq = mm(kt[mine, :], grad_s) * scale
                ua, ub = dq[:HALF], dq[HALF:]
                gproj[h * HEAD_DIM : h * HEAD_DIM + HALF, r] = (ua * c + ub * s).astype(BF16)
                gproj[h * HEAD_DIM + HALF : (h + 1) * HEAD_DIM, r] = (ub * c - ua * s).astype(BF16)
                here = (lane >= HEAD_DIM) if n else (lane < HEAD_DIM)
                none = jnp.zeros((ROWS, 2 * HEAD_DIM), BF16)
                dk_sum = dk_sum + mm(grad_s, jnp.where(here, q[r, pair], none))
                dv_sum = dv_sum + mm(probs.astype(BF16), jnp.where(here, do[:, pair], none))
            dk[:, pair] = dk_sum
            dv[:, pair] = dv_sum
        for step, n in enumerate((chunks - 2, chunks - 1)):

            @pl.when(i == n)
            def _():
                for stream in mlp_sums.streams:
                    stream.finish(step)
                    stream.start(step + 1)

    mlp_sums.done = [2] * len(mlp_sums.streams)

    vec_copy(0).wait()
    row_own[0:1, :] = sums[3:4, :]
    row_own[1:2, :] = sums[4:5, :] * gain2
    row_own[2:3, :] = sums[5:6, :]
    row_own[3:4, :] = vec_own[0, 0:1, :] + vec_par[0, 0:1, :] + sums[2:3, :] * downb
    row_own[4:5, :] = mod[5:6, :] * sums[2:3, :]
    row_own[5:6, :] = (1.0 + mod[4:5, :]) * sums[4:5, :]
    row_own[6:7, :] = jnp.where(core == 0, sums[0:1, :], sums[1:2, :])
    row_own[7:8, :] = jnp.where(core == 0, sums[1:2, :], sums[0:1, :])
    for n in range(chunks):
        br_copy(n).wait_send()
        gn_copy(n).wait_send()

    @pl.loop(0, chunks)
    def _(i):
        r = rows_of(i)
        c, s = cos_s[:, r], sin_s[:, r]
        turned = dk[r, :].T
        pieces = []
        for h in range(heads):
            ua = turned[h * HEAD_DIM : h * HEAD_DIM + HALF]
            ub = turned[h * HEAD_DIM + HALF : (h + 1) * HEAD_DIM]
            pieces += [ua * c + ub * s, ub * c - ua * s]
        gproj[width : 2 * width, r] = jnp.concatenate(pieces, axis=0).astype(BF16)
        gproj[2 * width :, r] = dv[r, :].T.astype(BF16)

    sent2 = w_s.at[pl.ds(2 * model, 4 * local)]
    gatt = w_s.at[pl.ds(2 * model + 4 * local, 4 * local)]

    def att_grads(n):
        for part in range(3):
            rows = slice((2 * part + n) * local, (2 * part + n + 1) * local)
            yield mm(gproj[rows, :], normed[...])
        yield mm(att[n * local : (n + 1) * local, :], gml[...])

    for part, piece in enumerate(att_grads(1)):
        sent2[part * local : (part + 1) * local, :] = piece.astype(BF16)
    att_copy = to_core(sent2, box2, 7)
    att_copy.start()

    for part, piece in enumerate(att_grads(0)):
        gatt[part * local : (part + 1) * local, :] = piece.astype(BF16)
    att_copy.wait()
    for part in range(4):
        rows = slice(part * local, (part + 1) * local)
        gatt[rows, :] = (gatt[rows, :].astype(F32) + box2[rows, :].astype(F32)).astype(BF16)
    red_att, _ = streams(gatt, 0, 4 * local, 3, 1, inbox2, 0, gatt_h)
    att_sums = Steps(*red_att)
    att_sums.start()
    mlp_sums.advance()

    @pl.loop(0, chunks)
    def _(i):
        r = rows_of(i)
        gn = jnp.zeros((ROWS, model), F32)
        for part in range(3):
            gn = gn + mm(gproj[part * width : (part + 1) * width, r], qkv_s[part], TN)
        n2[r, :] = gn.astype(BF16)
        xhat, _ = norm_parts(tok[r, :].astype(F32))
        vec_own[1, 0:1, :] += col_sum(gn)
        vec_own[1, 1:2, :] += col_sum(gn * xhat)

    vec_copy(1).start()
    for n in range(chunks):
        gn1_copy(n).start()
    ml_copy(chunks - 1).start()
    slot_rows = Gather(rows_h, dp, d_send, d_recv, used[0])
    row_steps = Steps(slot_rows)

    out_copies = []

    def hand_over(source, target, i, n):
        rows = pl.ds(pl.multiple_of(core * length + i * ROWS, 16), ROWS)
        keep = pltpu.make_async_copy(source, target.at[rows], o_sem.at[n])
        give = to_core(source, target.at[rows], 8 + n)
        keep.start()
        give.start()
        out_copies.append((keep, give))

    def output_chunk(i):
        r = slice(i * ROWS, (i + 1) * ROWS)
        ml_copy(i).wait()
        middle = tok[r, :].astype(F32) + mod[2:3, :] * (br_own[r, :].astype(F32) + br_par[r, :].astype(F32))
        total = ml_own[r, :].astype(F32) + ml_par[r, :].astype(F32) + downb
        act[r, :model] = (middle + mod[5:6, :] * total).astype(BF16)
        hand_over(act.at[r, :model], out_h, i, i)

    def token_chunk(i):
        r = slice(i * ROWS, (i + 1) * ROWS)
        gn1_copy(i).wait()
        xhat, rstd = norm_parts(tok[r, :].astype(F32))
        gn = n2[r, :].astype(F32) + gn1_par[r, :].astype(F32)
        g = gmid[r, :] + norm_back(gn, xhat, rstd, (1.0 + mod[1:2, :]) * gain1)
        act[r, model : 2 * model] = g.astype(BF16)
        hand_over(act.at[r, model : 2 * model], gtok_h, i, chunks + i)

    att_sums.advance()
    output_chunk(0)
    vec_copy(1).wait()
    shift_a = vec_own[1, 0:1, :] + vec_par[1, 0:1, :]
    scale_a = vec_own[1, 1:2, :] + vec_par[1, 1:2, :]
    row_own[8:9, :] = shift_a
    row_own[9:10, :] = scale_a * gain1
    row_own[10:11, :] = (1.0 + mod[1:2, :]) * scale_a
    slot_rows.own(row_own, load_sem.at[1])
    slot_rows.start(0)
    output_chunk(1)
    mlp_sums.advance()
    att_sums.advance()
    row_steps.advance()
    for i in range(2, chunks - 1):
        output_chunk(i)
    att_sums.advance()
    row_steps.advance()
    mlp_sums.advance()
    token_chunk(0)
    att_sums.advance()
    row_steps.advance()
    token_chunk(1)
    while row_steps.busy():
        row_steps.advance()

    slots = 2 * dp
    group = min(slots, GROUP)
    totals_o[...] = jnp.zeros_like(totals_o)
    picks = ((1, 0), (1, 1), (0, 2), (0, 0), (0, 1), (0, 3))
    for first_slot in range(0, slots, group):
        take = pltpu.make_async_copy(rows_h.at[pl.ds(first_slot, group)], rows_s, load_sem.at[0])
        take.start()
        take.wait()

        def pick(n, row):
            return jnp.concatenate([rows_s[g, 8 * n + row : 8 * n + row + 1, :] for g in range(group)], axis=0)

        feat = pick(1, 3)[:, :cond]
        for j, (n, row) in enumerate(picks):
            vecs = pick(n, row)
            totals_o[j : j + 1, :] += col_sum(vecs)
            outer = lax.dot_general(feat, vecs, TN, precision=PRECISE, preferred_element_type=F32)
            rows = slice(j * cond, (j + 1) * cond)
            for side, ref in enumerate((dk, dv)):
                cut = outer[:, side * width : (side + 1) * width]
                ref[rows, :] = cut if first_slot == 0 else ref[rows, :] + cut
        totals_o[6:7, :] += col_sum(pick(1, 2))
        totals_o[7:8, :] += col_sum(pick(0, 5))
        totals_o[8:9, :] += col_sum(pick(0, 4))
        totals_o[9:10, :] += jnp.where(core == 0, col_sum(pick(0, 6)), col_sum(pick(0, 7)))
    puts = [
        pltpu.make_async_copy(
            ref.at[pl.ds(0, 6 * cond)], adaw_h.at[:, pl.ds(side * width, width)], load_sem.at[2 + side]
        )
        for side, ref in enumerate((dk, dv))
    ]
    for put in puts:
        put.start()

    att_sums.advance()
    mlp_sums.advance()
    for i in range(2, chunks - 1):
        token_chunk(i)
    att_sums.advance()
    token_chunk(chunks - 1)
    output_chunk(chunks - 1)
    while mlp_sums.busy() or att_sums.busy():
        mlp_sums.advance()
        att_sums.advance()
    for put in puts:
        put.wait()
    for keep, give in out_copies:
        keep.wait()
        give.wait()


def block_call(dp, lengths, time, hbm, small):
    tokens, _, qkv_w, out_w, up_w, down_w, ada = hbm
    slot_count, model = time.shape[0], tokens.shape[1]
    length = tokens.shape[0] // slot_count
    hidden, local = up_w.shape[1], out_w.shape[0]
    width = 2 * local
    chunks = length // ROWS
    slots = slot_count * dp
    sems = 7 * (2 * dp.bit_length()) + dp.bit_length()
    any_spec, vmem_spec = pl.BlockSpec(memory_space=pl.ANY), pl.BlockSpec(memory_space=pltpu.VMEM)
    smem_spec = pl.BlockSpec(memory_space=pltpu.SMEM)
    inbox_rows = 2 * inbox_need(dp, model // 2) + 2 * inbox_need(dp, hidden // 2)
    inbox2_rows = 3 * inbox_need(dp, 4 * local // 3)
    dma = pltpu.SemaphoreType.DMA

    def low(*shape):
        return pltpu.VMEM(shape, BF16)

    def full(*shape):
        return pltpu.VMEM(shape, F32)

    tokens_like = low(length, model)
    return pl.pallas_call(
        functools.partial(block_kernel, dp),
        in_specs=[smem_spec] * 2 + [any_spec] * len(hbm) + [vmem_spec] * len(small),
        out_specs=[any_spec] * 6 + [vmem_spec],
        out_shape=[
            jax.ShapeDtypeStruct(tokens.shape, BF16),
            jax.ShapeDtypeStruct(tokens.shape, BF16),
            jax.ShapeDtypeStruct((model + hidden, model), BF16),
            jax.ShapeDtypeStruct((4 * local, model), BF16),
            jax.ShapeDtypeStruct((slots, 16, model), F32),
            jax.ShapeDtypeStruct(ada.shape, F32),
            jax.ShapeDtypeStruct((16, model), F32),
        ],
        scratch_shapes=[
            tokens_like, tokens_like, low(3, width, model), low(width, model), low(2 * (model + hidden), model),
            tokens_like, low(length, 2 * hidden), low(length, 2 * hidden), tokens_like,
            tokens_like, tokens_like, tokens_like, tokens_like, tokens_like, tokens_like, tokens_like,
            full(length, model), full(length, width), full(length, width), low(3 * width, length),
            low(width, length), low(width, length), low(length, width), low(length, width), low(length, width),
            low(width, length), tokens_like, full(16, length), full(HALF, length), full(HALF, length),
            pltpu.VMEM((16, length), jnp.int32), full(8, model), full(16, model), full(16, model),
            low(model + hidden, model), low(4 * local, model), low(inbox_rows, model),
            low(inbox2_rows, model), full(2, 8, model), full(2, 8, model), full(16, model),
            full(min(slots, GROUP), 16, model), full(8, model),
            dma((7,)), dma((4 * chunks + 2,)), dma((4 * chunks + 2,)), dma((8 + 2 * chunks,)), dma((8 + 2 * chunks,)),
            dma((sems,)), dma((sems,)), dma((2 * chunks,)),
        ],
        compiler_params=pltpu.CompilerParams(
            collective_id=0, has_side_effects=True, vmem_limit_bytes=VMEM_LIMIT
        ),
        cost_estimate=pl.CostEstimate(flops=80_000_000_000, bytes_accessed=40_000_000, transcendentals=0),
        name="transformer_block",
    )(lengths, time, *hbm, *small)


def inbox_need(dp, rows):
    need = 0
    for _ in range(dp.bit_length() - 1):
        if rows % 32 == 0:
            rows //= 2
        need += rows
    return need


def finish_kernel(totals, *refs):
    *refs, adab_o, gain1_o, gain2_o, downb_o, upb_o = refs
    half = len(refs) // 2
    for source, target in zip(refs[:half], refs[half:]):
        target[...] = source[...].astype(target.dtype)
    adab_o[...] = totals[0:6, :]
    for n, ref in enumerate((gain1_o, gain2_o, downb_o, upb_o)):
        ref[...] = totals[6 + n : 7 + n, : ref.shape[0]].reshape(ref.shape[0])


def finish_call(totals, output, grad_tok, adaw, g_mlp, g_att, hidden, local):
    steps = 4
    model = output.shape[1]

    def rows(count, start=0):
        return pl.BlockSpec((count // steps, model), lambda i: (start * steps // count + i, 0))

    def vector(count):
        return pl.BlockSpec((count,), lambda i: (0,))

    whole = [a.shape[0] for a in (output, grad_tok, adaw)]
    parts = ((model, 0), (hidden, model), (3 * local, 0), (local, 3 * local))
    vectors = (model, model, model, hidden)
    return pl.pallas_call(
        finish_kernel,
        grid=(steps,),
        in_specs=[pl.BlockSpec(totals.shape, lambda i: (0, 0))]
        + [rows(count) for count in whole]
        + [rows(*part) for part in parts],
        out_specs=[rows(count) for count in whole]
        + [rows(count) for count, _ in parts]
        + [pl.BlockSpec((6, model), lambda i: (0, 0))]
        + [vector(count) for count in vectors],
        out_shape=[jax.ShapeDtypeStruct(a.shape, a.dtype) for a in (output, grad_tok, adaw)]
        + [jax.ShapeDtypeStruct((count, model), F32) for count, _ in parts]
        + [jax.ShapeDtypeStruct((6, model), F32)]
        + [jax.ShapeDtypeStruct((count,), F32) for count in vectors],
        compiler_params=pltpu.CompilerParams(vmem_limit_bytes=VMEM_LIMIT),
        name="grads_to_float32",
    )(totals, output, grad_tok, adaw, g_mlp, g_mlp, g_att, g_att)


def per_device(
    dp, tokens, lengths, time, qkv_weight, out_weight, up_weight, up_bias, down_weight, down_bias,
    gain_attn, gain_mlp, ada_weight, ada_bias, cotangent,
):
    model, local = tokens.shape[1], out_weight.shape[0]
    cond = ada_weight.shape[0]
    qkv = jnp.transpose(qkv_weight, (1, 2, 0))
    ada = jnp.transpose(ada_weight, (1, 0, 2)).reshape(6 * cond, model)
    half = cond // 2
    freq = np.exp(np.arange(half) * (-math.log(10000.0) / half)).astype(np.float32)
    freq = jnp.asarray(np.concatenate([freq, freq])[None])
    inverse = jnp.asarray(np.exp(np.arange(HALF) * (-2.0 * math.log(10000.0) / HEAD_DIM)).astype(np.float32)[:, None])
    output, grad_tok, g_mlp, g_att, _, g_ada, totals = block_call(
        dp, lengths, time, [tokens, cotangent, qkv, out_weight, up_weight, down_weight, ada],
        [gain_attn, gain_mlp, up_bias, down_bias, ada_bias, freq, inverse],
    )
    output, grad_tok, g_ada, g_up, g_down, g_qkv, g_out, g_adab, g_gain1, g_gain2, g_downb, g_upb = finish_call(
        totals, output, grad_tok, g_ada, g_mlp, g_att, up_bias.shape[0], local
    )
    return (
        output,
        grad_tok,
        jnp.transpose(g_qkv.reshape(3, local, model), (2, 0, 1)),
        g_out,
        g_up,
        g_upb,
        g_down,
        g_downb,
        g_gain1,
        g_gain2,
        jnp.transpose(g_ada.reshape(6, cond, model), (1, 0, 2)),
        g_adab,
    )


def solution(mesh):
    in_specs = (
        P("dp", None), P("dp", None), P("dp"), P(None, None, "tensor"), P("tensor", None), P(None, "tensor"),
        P("tensor"), P("tensor", None), P(), P(), P(), P(), P(), P("dp", None),
    )
    out_specs = (
        P("dp", None), P("dp", None), P(None, None, "tensor"), P("tensor", None), P(None, "tensor"), P("tensor"),
        P("tensor", None), P(), P(), P(), P(), P(),
    )
    return jax.shard_map(
        functools.partial(per_device, mesh.shape["dp"]),
        mesh=mesh, in_specs=in_specs, out_specs=out_specs, check_vma=False,
    )
```

```python
import functools
import math

import jax
import jax.numpy as jnp
import numpy as np
from jax import lax
from jax.experimental import pallas as pl
from jax.experimental.pallas import tpu as pltpu
from jax.sharding import PartitionSpec as P

HEAD_DIM = 64
HALF = HEAD_DIM // 2
EPS = 1e-05
ROWS = 256
PRECISE = lax.Precision.HIGHEST
GROUP = 16
LONGEST = 512
VMEM_LIMIT = 61 * 1024 * 1024
F32 = jnp.float32
BF16 = jnp.bfloat16
GELU_A = math.sqrt(2.0 / math.pi)
GELU_B = 0.044715

NN = (((1,), (0,)), ((), ()))
NT = (((1,), (1,)), ((), ()))
TN = (((0,), (0,)), ((), ()))


def mm(left, right, dims=NN):
    return lax.dot_general(left, right, dims, preferred_element_type=F32)


def norm_parts(v):
    center = jnp.mean(v, axis=-1, keepdims=True)
    centered = v - center
    spread = jnp.mean(centered * centered, axis=-1, keepdims=True)
    rstd = lax.rsqrt(spread + EPS)
    return centered * rstd, rstd


def only_half(block, second):
    zero = jnp.zeros_like(block)
    return jnp.concatenate([zero, block] if second else [block, zero], axis=0)


MESH = pl.DeviceIdType.MESH


def bit_of(index, bit):
    return lax.rem(index // (1 << bit), 2)


def flip(index, bit):
    return index + (1 << bit) * (1 - 2 * bit_of(index, bit))


class Reduce:
    def __init__(self, total, base, rows, inbox, inbase, order, final, send, recv, first_sem):
        self.total, self.base, self.inbox, self.send, self.recv = total, base, inbox, send, recv
        self.final = final
        self.plan, self.sem = [], first_sem
        size, halved = rows, []
        for bit in order:
            if size % 32 == 0:
                self.plan.append(("halve", bit, size // 2, inbase, list(halved)))
                size //= 2
                halved.append((bit, size))
            else:
                self.plan.append(("whole", bit, size, inbase, list(halved)))
            inbase += size
        self.inend = inbase
        while halved:
            bit, size = halved.pop()
            self.plan.append(("double", bit, size, None, list(halved)))
        self.steps = len(self.plan)
        self.turn = next((n for n, step in enumerate(self.plan) if step[0] == "double"), self.steps)

    def offset(self, halved):
        me = lax.axis_index("dp")
        at = self.base
        for bit, size in halved:
            at = at + bit_of(me, bit) * size
        return at

    def copy(self, n):
        kind, bit, size, inbase, halved = self.plan[n]
        me = lax.axis_index("dp")
        start = self.offset(halved)
        if kind == "halve":
            source = start + (1 - bit_of(me, bit)) * size
        elif kind == "whole":
            source = start
        else:
            source = start + bit_of(me, bit) * size
        origin = self.final if kind == "double" and n > self.turn else self.total
        block = pl.ds(pl.multiple_of(source, 16), size)
        return pltpu.make_async_remote_copy(
            src_ref=origin.at[block],
            dst_ref=self.final.at[block] if kind == "double" else self.inbox.at[pl.ds(inbase, size)],
            send_sem=self.send.at[self.sem + n],
            recv_sem=self.recv.at[self.sem + n],
            device_id={"dp": flip(me, bit)},
            device_id_type=MESH,
        )

    def store(self):
        at = self.offset(self.plan[self.turn - 1][4])
        kind, bit, size = self.plan[self.turn - 1][:3]
        if kind == "halve":
            at = at + bit_of(lax.axis_index("dp"), bit) * size
        block = pl.ds(pl.multiple_of(at, 16), size)
        return pltpu.make_async_copy(self.total.at[block], self.final.at[block], self.send.at[self.sem + self.steps])

    def start(self, n):
        if n < self.steps:
            self.copy(n).start()

    def finish(self, n):
        if n >= self.steps:
            return
        self.copy(n).wait()
        kind, bit, size, inbase, halved = self.plan[n]
        if kind == "double":
            if n == self.turn:
                self.store().wait()
            return
        keep = self.offset(halved)
        if kind == "halve":
            keep = keep + bit_of(lax.axis_index("dp"), bit) * size
        tile = next(t for t in (128, 96, 64, 48, 32, 16, size) if size % t == 0)

        @pl.loop(0, size // tile)
        def _(j):
            mine = pl.ds(pl.multiple_of(keep + j * tile, 16), tile)
            came = pl.ds(pl.multiple_of(inbase + j * tile, 16), tile)
            added = self.total[mine, :].astype(F32) + self.inbox[came, :].astype(F32)
            self.total[mine, :] = added.astype(BF16)

        if n + 1 == self.turn:
            self.store().start()
            if self.turn == self.steps:
                self.store().wait()


class Gather:
    def __init__(self, rows, dp, send, recv, first_sem):
        self.rows, self.send, self.recv, self.sem = rows, send, recv, first_sem
        self.bits = list(reversed(range(dp.bit_length() - 1))) + [None]
        self.steps = len(self.bits)

    def place(self):
        at, weight = 0, 1
        for bit in self.bits:
            index = lax.axis_index("tensor") if bit is None else lax.axis_index("dp")
            at = at + bit_of(index, bit or 0) * weight
            weight *= 2
        return at

    def own(self, row, sem):
        store = pltpu.make_async_copy(row, self.rows.at[self.place()], sem)
        store.start()
        store.wait()

    def copy(self, n):
        bit, size = self.bits[n], 1 << n
        block = self.rows.at[pl.ds((self.place() // size) * size, size)]
        axis = "tensor" if bit is None else "dp"
        return pltpu.make_async_remote_copy(
            src_ref=block,
            dst_ref=block,
            send_sem=self.send.at[self.sem + n],
            recv_sem=self.recv.at[self.sem + n],
            device_id={axis: flip(lax.axis_index(axis), bit or 0)},
            device_id_type=MESH,
        )

    def start(self, n):
        if n < self.steps:
            self.copy(n).start()

    def finish(self, n):
        if n < self.steps:
            self.copy(n).wait()


def norm_back(gn, xhat, rstd, gain):
    y = gn * gain
    mean_y = jnp.mean(y, axis=-1, keepdims=True)
    mean_yx = jnp.mean(y * xhat, axis=-1, keepdims=True)
    return rstd * (y - mean_y - xhat * mean_yx)


def col_sum(v):
    return jnp.sum(v, axis=0, keepdims=True)


class Steps:
    def __init__(self, *streams):
        self.streams, self.done = streams, [0] * len(streams)

    def start(self):
        for stream in self.streams:
            stream.start(0)

    def advance(self):
        for n, stream in enumerate(self.streams):
            if self.done[n] < stream.steps:
                stream.finish(self.done[n])
                stream.start(self.done[n] + 1)
                self.done[n] += 1

    def busy(self):
        return any(done < stream.steps for done, stream in zip(self.done, self.streams))


def block_kernel(
    dp, lengths, time, tok_h, cot_h, qkv_h, out_wh, up_h, dn_h, ada_h, gain1_i, gain2_i, bias_i, downb_i, adab_i,
    freq, inverse,
    out_h, gtok_h, gmlp_h, gatt_h, rows_h, adaw_h, totals_o,
    tok, cot, qkv_s, out_s, w_s, n2, act, pre, gml, br_own, br_par, ml_own, ml_par, gn_own, gn_par, gn1_par,
    gmid, dk, dv, gproj, qt, kt, q, k, v, att, normed, stat, cos_s, sin_s, bound, mod, small, small_par,
    box1, box2, inbox1, inbox2, vec_own, vec_par, row_own, rows_s, sums,
    load_sem, y_send, y_recv, c_send, c_recv, d_send, d_recv, o_sem,
):
    length, model = tok.shape
    local = out_wh.shape[0]
    hidden = up_h.shape[1]
    cond = freq.shape[1]
    width = 2 * local
    heads = width // HEAD_DIM
    chunks = length // ROWS
    tensor, here_dp = lax.axis_index("tensor"), lax.axis_index("dp")
    core = lax.rem(tensor, 2)
    other_core, other_y = flip(tensor, 0), flip(tensor, 1)
    bits = dp.bit_length() - 1
    scale = 1.0 / math.sqrt(HEAD_DIM)
    vt = gproj.at[pl.ds(2 * width, width)]

    barrier = pltpu.get_barrier_semaphore()
    for peer in [{"tensor": other_core}, {"tensor": other_y}] + [{"dp": flip(here_dp, b)} for b in range(bits)]:
        pl.semaphore_signal(barrier, inc=1, device_id=peer, device_id_type=MESH)

    mine_rows = pl.ds(pl.multiple_of(core * length, 16), length)
    moves = (
        (ada_h, act.at[pl.ds(0, ada_h.shape[0]), pl.ds(0, model)]),
        (tok_h.at[mine_rows], tok),
        (qkv_h, qkv_s.at[:, pl.ds(0, local)]),
        (out_wh, out_s.at[pl.ds(0, local)]),
        (up_h, w_s.at[pl.ds(0, model)]),
        (dn_h, w_s.at[pl.ds(2 * model, hidden)]),
        (cot_h.at[mine_rows], cot),
    )
    loads = [pltpu.make_async_copy(source, target, load_sem.at[n]) for n, (source, target) in enumerate(moves)]
    for load in loads:
        load.start()

    def rows_of(i):
        return pl.ds(pl.multiple_of(i * ROWS, ROWS), ROWS)

    def to_y(source, target, n):
        return pltpu.make_async_remote_copy(
            src_ref=source, dst_ref=target, send_sem=y_send.at[n], recv_sem=y_recv.at[n],
            device_id={"tensor": other_y}, device_id_type=MESH,
        )

    def to_core(source, target, n):
        return pltpu.make_async_remote_copy(
            src_ref=source, dst_ref=target, send_sem=c_send.at[n], recv_sem=c_recv.at[n],
            device_id={"tensor": other_core}, device_id_type=MESH,
        )

    def br_copy(i):
        return to_y(br_own.at[rows_of(i)], br_par.at[rows_of(i)], i)

    def gn_copy(i):
        return to_y(gn_own.at[rows_of(i)], gn_par.at[rows_of(i)], chunks + i)

    def ml_copy(i):
        return to_y(ml_own.at[rows_of(i)], ml_par.at[rows_of(i)], 2 * chunks + i)

    def gn1_copy(i):
        return to_y(n2.at[rows_of(i)], gn1_par.at[rows_of(i)], 3 * chunks + i)

    def vec_copy(n):
        return to_y(vec_own.at[n], vec_par.at[n], 4 * chunks + n)

    for n, ref in enumerate((gain1_i, gain2_i, bias_i, downb_i)):
        small[n : n + 1, : ref.shape[0]] = ref[...].astype(F32).reshape(1, ref.shape[0])
    small[4:10, :] = adab_i[...].astype(F32)
    shares = [
        to_core(qkv_h, qkv_s.at[:, pl.ds(local, local)], 0),
        to_core(out_wh, out_s.at[pl.ds(local, local)], 1),
        to_core(small, small_par, 2),
        to_core(up_h, w_s.at[pl.ds(model, model)], 3),
        to_core(dn_h, w_s.at[pl.ds(2 * model + hidden, hidden)], 4),
    ]
    pl.semaphore_wait(barrier, 2 + bits)
    for share in shares:
        share.start()

    gain1, gain2, downb = small[0:1, :], small[1:2, :], small[3:4, :]
    when = time[core].astype(F32)
    angle = jnp.broadcast_to(freq[...] * when, (8, cond))
    lane = lax.broadcasted_iota(jnp.int32, (8, cond), 1)
    feats = jnp.where(lane < cond // 2, jnp.cos(angle), jnp.sin(angle))
    high = feats.astype(BF16)
    rest = feats - high.astype(F32)
    middle_part = rest.astype(BF16)
    low_part = (rest - middle_part.astype(F32)).astype(BF16)
    sums[...] = jnp.zeros_like(sums)
    vec_own[...] = jnp.zeros_like(vec_own)
    row_own[...] = jnp.zeros_like(row_own)
    row_own[11:12, :cond] = feats[0:1, :]
    place = lax.broadcasted_iota(jnp.int32, (8, length), 1)
    start, begin, end = jnp.int32(0), jnp.zeros((8, length), jnp.int32), jnp.zeros((8, length), jnp.int32)
    for n in range(lengths.shape[1]):
        size = lengths[core, n]
        end = end + jnp.where(place >= start, size, 0)
        start = start + size
        begin = begin + jnp.where(place >= start, size, 0)
    bound[0:8, :] = begin
    bound[8:16, :] = end
    turns = inverse[...] * (place - begin)[0:1, :].astype(F32)
    cos_s[...] = jnp.cos(turns)
    sin_s[...] = jnp.sin(turns)
    loads[0].wait()
    for j in range(6):
        ada = act[j * cond : (j + 1) * cond, :model]
        vec = mm(high, ada) + mm(middle_part, ada) + mm(low_part, ada)
        mod[j : j + 1, :] = vec[0:1, :] + small[4 + j : 5 + j, :]
    for n in (1, 2):
        loads[n].wait()
    shares[0].wait()

    def project(i):
        r = rows_of(i)
        xhat, _ = norm_parts(tok[r, :].astype(F32))
        x1 = (xhat * gain1 * (1.0 + mod[1:2, :]) + mod[0:1, :]).astype(BF16)
        normed[r, :] = x1
        c, s = cos_s[:, r], sin_s[:, r]
        for part, (t_o, r_o) in enumerate(((qt, q), (kt, k), (vt, v))):
            turned = mm(qkv_s[part], x1, NT)
            if part < 2:
                pieces = []
                for h in range(heads):
                    a = turned[h * HEAD_DIM : h * HEAD_DIM + HALF]
                    b = turned[h * HEAD_DIM + HALF : (h + 1) * HEAD_DIM]
                    pieces += [a * c - b * s, b * c + a * s]
                turned = jnp.concatenate(pieces, axis=0)
            if part == 0:
                turned = turned * scale
            t_o[:, r] = turned.astype(BF16)
            r_o[r, :] = turned.T.astype(BF16)

    def allowed_keys(r, keys):
        place = lax.broadcasted_iota(jnp.int32, (keys.size, ROWS), 0) + keys.start
        return (place >= bound[0:1, r]) & (place < bound[8:9, r])

    def attend(i, keys):
        r = rows_of(i)
        allowed = allowed_keys(r, keys)
        for h in range(heads):
            pair = slice((h // 2) * 2 * HEAD_DIM, (h // 2 + 1) * 2 * HEAD_DIM)
            mine = slice(h * HEAD_DIM, (h + 1) * HEAD_DIM)
            scores = mm(k[keys, pair], only_half(qt[mine, r], h % 2))
            scores = jnp.where(allowed, scores, -1000000000.0)
            top = jnp.max(scores, axis=0, keepdims=True)
            terms = jnp.exp(scores - top)
            inv = 1.0 / jnp.sum(terms, axis=0, keepdims=True)
            att[mine, r] = (mm(vt[mine, keys], terms.astype(BF16)) * inv).astype(BF16)
            stat[h : h + 1, r] = top
            stat[8 + h : 9 + h, r] = inv
        br_own[r, :] = mm(att[:, r], out_s[...], TN).astype(BF16)
        br_copy(i).start()

    reach = min(length, ROWS + LONGEST)
    first_keys, last_keys = pl.ds(0, reach), pl.ds(length - reach, reach)

    pl.loop(0, reach // ROWS)(project)
    loads[3].wait()
    shares[1].wait()
    attend(0, first_keys)
    pl.loop(reach // ROWS, chunks)(project)

    @pl.loop(1, chunks - 1)
    def _(i):
        attend(i, pl.ds(0, length))

    attend(chunks - 1, last_keys)

    for n in (4, 5, 6):
        loads[n].wait()
    for n in (2, 3, 4):
        shares[n].wait()

    @pl.loop(0, chunks)
    def _(i):
        r = rows_of(i)
        br_copy(i).wait_recv()
        middle = tok[r, :].astype(F32) + mod[2:3, :] * (br_own[r, :].astype(F32) + br_par[r, :].astype(F32))
        xhat, _ = norm_parts(middle)
        x2 = (xhat * gain2 * (1.0 + mod[4:5, :]) + mod[3:4, :]).astype(BF16)
        n2[r, :] = x2
        grad_out = cot[r, :].astype(F32)
        g = (mod[5:6, :] * grad_out).astype(BF16)
        gml[r, :] = g
        part = jnp.zeros((ROWS, model), F32)
        grad = jnp.zeros((ROWS, model), F32)
        for n in range(2):
            up, down = w_s.at[pl.ds(n * model, model)], w_s.at[pl.ds(2 * model + n * hidden, hidden)]
            cols = slice(n * hidden, (n + 1) * hidden)
            z = mm(x2, up[...]) + (small_par if n else small)[2:3, :hidden]
            square = z * z
            t = jnp.tanh(GELU_A * z * (1.0 + GELU_B * square))
            a = (0.5 * z * (1.0 + t)).astype(BF16)
            act[r, cols] = a
            slope = 0.5 * (1.0 + t) + (0.5 * GELU_A) * z * (1.0 - t * t) * (1.0 + 3.0 * GELU_B * square)
            part = part + mm(a, down[...])
            p = (mm(g, down[...], NT) * slope).astype(BF16)
            pre[r, cols] = p
            sums[n : n + 1, :hidden] += col_sum(p.astype(F32))
            grad = grad + mm(p, up[...], NT)
        ml_own[r, :] = part.astype(BF16)
        gn_own[r, :] = grad.astype(BF16)
        vec_own[0, 0:1, :] += col_sum(grad_out * part)
        sums[2:3, :] += col_sum(grad_out)
        gn_copy(i).start()

    vec_copy(0).start()

    def up_grad(j, n):
        cols = pl.ds(pl.multiple_of(j * ROWS, ROWS), ROWS)
        return mm(n2[:, cols], pre[:, n * hidden : (n + 1) * hidden], TN)

    def down_grad(j, n):
        cols = pl.ds(pl.multiple_of(n * hidden + j * ROWS, ROWS), ROWS)
        return mm(act[:, cols], gml[...], TN)

    outbox = w_s.at[pl.ds(2 * model, model + hidden)]

    @pl.loop(0, model // ROWS)
    def _(j):
        outbox[rows_of(j), :] = up_grad(j, 1).astype(BF16)

    up_copy = to_core(outbox.at[pl.ds(0, model)], box1.at[pl.ds(0, model)], 5)
    up_copy.start()

    @pl.loop(0, hidden // ROWS)
    def _(j):
        outbox[pl.ds(pl.multiple_of(model + j * ROWS, ROWS), ROWS), :] = down_grad(j, 1).astype(BF16)

    down_copy = to_core(outbox.at[pl.ds(model, hidden)], box1.at[pl.ds(model, hidden)], 6)
    down_copy.start()
    up_copy.wait()

    @pl.loop(0, model // ROWS)
    def _(j):
        r = rows_of(j)
        w_s[r, :] = (up_grad(j, 0) + box1[r, :].astype(F32)).astype(BF16)

    order = list(range(bits))
    turned_order = order[1:2] + order[:1] + order[2:]
    orders = (order, turned_order)
    used = [0]

    def streams(total, base, rows, count, shift, inbox, inbase, final):
        made = []
        for n in range(count):
            size = rows // count
            made.append(
                Reduce(total, base + n * size, size, inbox, inbase, orders[(n + shift) % 2], final, d_send, d_recv, used[0])
            )
            inbase = made[-1].inend
            used[0] += made[-1].steps + 1
        return made, inbase

    red_up, inbase = streams(w_s, 0, model, 2, 0, inbox1, 0, gmlp_h)
    for stream in red_up:
        stream.start(0)
    down_copy.wait()

    @pl.loop(0, hidden // ROWS)
    def _(j):
        r = pl.ds(pl.multiple_of(model + j * ROWS, ROWS), ROWS)
        w_s[r, :] = (down_grad(j, 0) + box1[r, :].astype(F32)).astype(BF16)

    red_down, _ = streams(w_s, model, hidden, 2, 0, inbox1, inbase, gmlp_h)
    for stream in red_down:
        stream.start(0)
    mlp_sums = Steps(*red_up, *red_down)

    dk[...] = jnp.zeros_like(dk)
    dv[...] = jnp.zeros_like(dv)

    @pl.loop(0, chunks)
    def _(i):
        r = rows_of(i)
        gn_copy(i).wait_recv()

        @pl.when(i == chunks - 1)
        def _():
            for n in range(chunks - 1):
                ml_copy(n).start()

        branch = br_own[r, :].astype(F32) + br_par[r, :].astype(F32)
        xhat, rstd = norm_parts(tok[r, :].astype(F32) + mod[2:3, :] * branch)
        gn = gn_own[r, :].astype(F32) + gn_par[r, :].astype(F32)
        g = cot[r, :].astype(F32) + norm_back(gn, xhat, rstd, (1.0 + mod[4:5, :]) * gain2)
        gmid[r, :] = g
        sums[3:4, :] += col_sum(gn)
        sums[4:5, :] += col_sum(gn * xhat)
        sums[5:6, :] += col_sum(g * branch)
        gb = (mod[2:3, :] * g).astype(BF16)
        gml[r, :] = gb
        do_t = mm(out_s[...], gb, NT).astype(BF16)
        do = mm(gb, out_s[...], NT).astype(BF16)
        allowed = allowed_keys(r, pl.ds(0, length))
        lane = lax.broadcasted_iota(jnp.int32, (ROWS, 2 * HEAD_DIM), 1)
        c, s = cos_s[:, r], sin_s[:, r]
        for p in range(heads // 2):
            pair = slice(p * 2 * HEAD_DIM, (p + 1) * 2 * HEAD_DIM)
            dk_sum, dv_sum = dk[:, pair], dv[:, pair]
            for n in range(2):
                h = 2 * p + n
                mine = slice(h * HEAD_DIM, (h + 1) * HEAD_DIM)
                scores = mm(k[:, pair], only_half(qt[mine, r], n))
                probs = jnp.where(allowed, jnp.exp(scores - stat[h : h + 1, r]), 0.0) * stat[8 + h : 9 + h, r]
                grad_p = mm(v[:, pair], only_half(do_t[mine, :], n))
                centre = col_sum(probs * grad_p)
                grad_s = (probs * (grad_p - centre)).astype(BF16)
                dq = mm(kt[mine, :], grad_s) * scale
                ua, ub = dq[:HALF], dq[HALF:]
                gproj[h * HEAD_DIM : h * HEAD_DIM + HALF, r] = (ua * c + ub * s).astype(BF16)
                gproj[h * HEAD_DIM + HALF : (h + 1) * HEAD_DIM, r] = (ub * c - ua * s).astype(BF16)
                here = (lane >= HEAD_DIM) if n else (lane < HEAD_DIM)
                none = jnp.zeros((ROWS, 2 * HEAD_DIM), BF16)
                dk_sum = dk_sum + mm(grad_s, jnp.where(here, q[r, pair], none))
                dv_sum = dv_sum + mm(probs.astype(BF16), jnp.where(here, do[:, pair], none))
            dk[:, pair] = dk_sum
            dv[:, pair] = dv_sum
        for step, n in enumerate((chunks - 3, chunks - 2)):

            @pl.when(i == n)
            def _():
                for stream in mlp_sums.streams:
                    stream.finish(step)
                    stream.start(step + 1)

    mlp_sums.done = [2] * len(mlp_sums.streams)

    vec_copy(0).wait()
    row_own[0:1, :] = sums[3:4, :]
    row_own[1:2, :] = sums[4:5, :] * gain2
    row_own[2:3, :] = sums[5:6, :]
    row_own[3:4, :] = vec_own[0, 0:1, :] + vec_par[0, 0:1, :] + sums[2:3, :] * downb
    row_own[4:5, :] = mod[5:6, :] * sums[2:3, :]
    row_own[5:6, :] = (1.0 + mod[4:5, :]) * sums[4:5, :]
    row_own[6:7, :] = jnp.where(core == 0, sums[0:1, :], sums[1:2, :])
    row_own[7:8, :] = jnp.where(core == 0, sums[1:2, :], sums[0:1, :])
    for n in range(chunks):
        br_copy(n).wait_send()
        gn_copy(n).wait_send()

    @pl.loop(0, chunks)
    def _(i):
        r = rows_of(i)
        c, s = cos_s[:, r], sin_s[:, r]
        turned = dk[r, :].T
        pieces = []
        for h in range(heads):
            ua = turned[h * HEAD_DIM : h * HEAD_DIM + HALF]
            ub = turned[h * HEAD_DIM + HALF : (h + 1) * HEAD_DIM]
            pieces += [ua * c + ub * s, ub * c - ua * s]
        gproj[width : 2 * width, r] = jnp.concatenate(pieces, axis=0).astype(BF16)
        gproj[2 * width :, r] = dv[r, :].T.astype(BF16)

    sent2 = w_s.at[pl.ds(2 * model, 4 * local)]
    gatt = w_s.at[pl.ds(2 * model + 4 * local, 4 * local)]

    def att_grads(n):
        for part in range(3):
            rows = slice((2 * part + n) * local, (2 * part + n + 1) * local)
            yield mm(gproj[rows, :], normed[...])
        yield mm(att[n * local : (n + 1) * local, :], gml[...])

    for part, piece in enumerate(att_grads(1)):
        sent2[part * local : (part + 1) * local, :] = piece.astype(BF16)
    att_copy = to_core(sent2, box2, 7)
    att_copy.start()
    mlp_sums.advance()

    for part, piece in enumerate(att_grads(0)):
        gatt[part * local : (part + 1) * local, :] = piece.astype(BF16)
    att_copy.wait()
    for part in range(4):
        rows = slice(part * local, (part + 1) * local)
        gatt[rows, :] = (gatt[rows, :].astype(F32) + box2[rows, :].astype(F32)).astype(BF16)
    red_att, _ = streams(gatt, 0, 4 * local, 2, 0, inbox2, 0, gatt_h)
    att_sums = Steps(*red_att)
    att_sums.start()

    @pl.loop(0, chunks)
    def _(i):
        r = rows_of(i)
        gn = jnp.zeros((ROWS, model), F32)
        for part in range(3):
            gn = gn + mm(gproj[part * width : (part + 1) * width, r], qkv_s[part], TN)
        n2[r, :] = gn.astype(BF16)
        xhat, _ = norm_parts(tok[r, :].astype(F32))
        vec_own[1, 0:1, :] += col_sum(gn)
        vec_own[1, 1:2, :] += col_sum(gn * xhat)

    vec_copy(1).start()
    for n in range(chunks):
        gn1_copy(n).start()
    ml_copy(chunks - 1).start()
    slot_rows = Gather(rows_h, dp, d_send, d_recv, used[0])
    row_steps = Steps(slot_rows)

    out_copies = []

    def hand_over(source, target, i, n):
        rows = pl.ds(pl.multiple_of(core * length + i * ROWS, 16), ROWS)
        keep = pltpu.make_async_copy(source, target.at[rows], o_sem.at[n])
        give = to_core(source, target.at[rows], 8 + n)
        keep.start()
        give.start()
        out_copies.append((keep, give))

    def output_chunk(i):
        r = slice(i * ROWS, (i + 1) * ROWS)
        ml_copy(i).wait()
        middle = tok[r, :].astype(F32) + mod[2:3, :] * (br_own[r, :].astype(F32) + br_par[r, :].astype(F32))
        total = ml_own[r, :].astype(F32) + ml_par[r, :].astype(F32) + downb
        act[r, :model] = (middle + mod[5:6, :] * total).astype(BF16)
        hand_over(act.at[r, :model], out_h, i, i)

    def token_chunk(i):
        r = slice(i * ROWS, (i + 1) * ROWS)
        gn1_copy(i).wait()
        xhat, rstd = norm_parts(tok[r, :].astype(F32))
        gn = n2[r, :].astype(F32) + gn1_par[r, :].astype(F32)
        g = gmid[r, :] + norm_back(gn, xhat, rstd, (1.0 + mod[1:2, :]) * gain1)
        act[r, model : 2 * model] = g.astype(BF16)
        hand_over(act.at[r, model : 2 * model], gtok_h, i, chunks + i)

    att_sums.advance()
    output_chunk(0)
    att_sums.advance()
    vec_copy(1).wait()
    shift_a = vec_own[1, 0:1, :] + vec_par[1, 0:1, :]
    scale_a = vec_own[1, 1:2, :] + vec_par[1, 1:2, :]
    row_own[8:9, :] = shift_a
    row_own[9:10, :] = scale_a * gain1
    row_own[10:11, :] = (1.0 + mod[1:2, :]) * scale_a
    slot_rows.own(row_own, load_sem.at[1])
    slot_rows.start(0)
    output_chunk(1)
    mlp_sums.advance()
    att_sums.advance()
    row_steps.advance()
    for i in range(2, chunks - 1):
        output_chunk(i)
    mlp_sums.advance()
    att_sums.advance()
    row_steps.advance()
    token_chunk(0)
    att_sums.advance()
    row_steps.advance()
    token_chunk(1)
    mlp_sums.advance()
    while row_steps.busy():
        row_steps.advance()

    slots = 2 * dp
    group = min(slots, GROUP)
    totals_o[...] = jnp.zeros_like(totals_o)
    picks = ((1, 0), (1, 1), (0, 2), (0, 0), (0, 1), (0, 3))
    for first_slot in range(0, slots, group):
        take = pltpu.make_async_copy(rows_h.at[pl.ds(first_slot, group)], rows_s, load_sem.at[0])
        take.start()
        take.wait()

        def pick(n, row):
            return jnp.concatenate([rows_s[g, 8 * n + row : 8 * n + row + 1, :] for g in range(group)], axis=0)

        feat = pick(1, 3)[:, :cond]
        for j, (n, row) in enumerate(picks):
            vecs = pick(n, row)
            totals_o[j : j + 1, :] += col_sum(vecs)
            outer = lax.dot_general(feat, vecs, TN, precision=PRECISE, preferred_element_type=F32)
            rows = slice(j * cond, (j + 1) * cond)
            for side, ref in enumerate((dk, dv)):
                cut = outer[:, side * width : (side + 1) * width]
                ref[rows, :] = cut if first_slot == 0 else ref[rows, :] + cut
        totals_o[6:7, :] += col_sum(pick(1, 2))
        totals_o[7:8, :] += col_sum(pick(0, 5))
        totals_o[8:9, :] += col_sum(pick(0, 4))
        totals_o[9:10, :] += jnp.where(core == 0, col_sum(pick(0, 6)), col_sum(pick(0, 7)))
    puts = [
        pltpu.make_async_copy(
            ref.at[pl.ds(0, 6 * cond)], adaw_h.at[:, pl.ds(side * width, width)], load_sem.at[2 + side]
        )
        for side, ref in enumerate((dk, dv))
    ]
    for put in puts:
        put.start()

    att_sums.advance()
    for i in range(2, chunks):
        token_chunk(i)
    output_chunk(chunks - 1)
    while mlp_sums.busy() or att_sums.busy():
        mlp_sums.advance()
        att_sums.advance()
    for put in puts:
        put.wait()
    for keep, give in out_copies:
        keep.wait()
        give.wait()


def block_call(dp, lengths, time, hbm, small):
    tokens, _, qkv_w, out_w, up_w, down_w, ada = hbm
    slot_count, model = time.shape[0], tokens.shape[1]
    length = tokens.shape[0] // slot_count
    hidden, local = up_w.shape[1], out_w.shape[0]
    width = 2 * local
    chunks = length // ROWS
    slots = slot_count * dp
    sems = 7 * (2 * dp.bit_length()) + dp.bit_length()
    any_spec, vmem_spec = pl.BlockSpec(memory_space=pl.ANY), pl.BlockSpec(memory_space=pltpu.VMEM)
    smem_spec = pl.BlockSpec(memory_space=pltpu.SMEM)
    inbox_rows = 2 * inbox_need(dp, model // 2) + 2 * inbox_need(dp, hidden // 2)
    inbox2_rows = 2 * inbox_need(dp, width)
    dma = pltpu.SemaphoreType.DMA

    def low(*shape):
        return pltpu.VMEM(shape, BF16)

    def full(*shape):
        return pltpu.VMEM(shape, F32)

    tokens_like = low(length, model)
    return pl.pallas_call(
        functools.partial(block_kernel, dp),
        in_specs=[smem_spec] * 2 + [any_spec] * len(hbm) + [vmem_spec] * len(small),
        out_specs=[any_spec] * 6 + [vmem_spec],
        out_shape=[
            jax.ShapeDtypeStruct(tokens.shape, BF16),
            jax.ShapeDtypeStruct(tokens.shape, BF16),
            jax.ShapeDtypeStruct((model + hidden, model), BF16),
            jax.ShapeDtypeStruct((4 * local, model), BF16),
            jax.ShapeDtypeStruct((slots, 16, model), F32),
            jax.ShapeDtypeStruct(ada.shape, F32),
            jax.ShapeDtypeStruct((16, model), F32),
        ],
        scratch_shapes=[
            tokens_like, tokens_like, low(3, width, model), low(width, model), low(2 * (model + hidden), model),
            tokens_like, low(length, 2 * hidden), low(length, 2 * hidden), tokens_like,
            tokens_like, tokens_like, tokens_like, tokens_like, tokens_like, tokens_like, tokens_like,
            full(length, model), full(length, width), full(length, width), low(3 * width, length),
            low(width, length), low(width, length), low(length, width), low(length, width), low(length, width),
            low(width, length), tokens_like, full(16, length), full(HALF, length), full(HALF, length),
            pltpu.VMEM((16, length), jnp.int32), full(8, model), full(16, model), full(16, model),
            low(model + hidden, model), low(4 * local, model), low(inbox_rows, model),
            low(inbox2_rows, model), full(2, 8, model), full(2, 8, model), full(16, model),
            full(min(slots, GROUP), 16, model), full(8, model),
            dma((7,)), dma((4 * chunks + 2,)), dma((4 * chunks + 2,)), dma((8 + 2 * chunks,)), dma((8 + 2 * chunks,)),
            dma((sems,)), dma((sems,)), dma((2 * chunks,)),
        ],
        compiler_params=pltpu.CompilerParams(
            collective_id=0, has_side_effects=True, vmem_limit_bytes=VMEM_LIMIT
        ),
        cost_estimate=pl.CostEstimate(flops=80_000_000_000, bytes_accessed=40_000_000, transcendentals=0),
        name="transformer_block",
    )(lengths, time, *hbm, *small)


def inbox_need(dp, rows):
    need = 0
    for _ in range(dp.bit_length() - 1):
        if rows % 32 == 0:
            rows //= 2
        need += rows
    return need


def finish_kernel(totals, *refs):
    *refs, adab_o, gain1_o, gain2_o, downb_o, upb_o = refs
    half = len(refs) // 2
    for source, target in zip(refs[:half], refs[half:]):
        target[...] = source[...].astype(target.dtype)
    adab_o[...] = totals[0:6, :]
    for n, ref in enumerate((gain1_o, gain2_o, downb_o, upb_o)):
        ref[...] = totals[6 + n : 7 + n, : ref.shape[0]].reshape(ref.shape[0])


def finish_call(totals, output, grad_tok, adaw, g_mlp, g_att, hidden, local):
    steps = 4
    model = output.shape[1]

    def rows(count, start=0):
        return pl.BlockSpec((count // steps, model), lambda i: (start * steps // count + i, 0))

    def vector(count):
        return pl.BlockSpec((count,), lambda i: (0,))

    whole = [a.shape[0] for a in (output, grad_tok, adaw)]
    parts = ((model, 0), (hidden, model), (3 * local, 0), (local, 3 * local))
    vectors = (model, model, model, hidden)
    return pl.pallas_call(
        finish_kernel,
        grid=(steps,),
        in_specs=[pl.BlockSpec(totals.shape, lambda i: (0, 0))]
        + [rows(count) for count in whole]
        + [rows(*part) for part in parts],
        out_specs=[rows(count) for count in whole]
        + [rows(count) for count, _ in parts]
        + [pl.BlockSpec((6, model), lambda i: (0, 0))]
        + [vector(count) for count in vectors],
        out_shape=[jax.ShapeDtypeStruct(a.shape, a.dtype) for a in (output, grad_tok, adaw)]
        + [jax.ShapeDtypeStruct((count, model), F32) for count, _ in parts]
        + [jax.ShapeDtypeStruct((6, model), F32)]
        + [jax.ShapeDtypeStruct((count,), F32) for count in vectors],
        compiler_params=pltpu.CompilerParams(vmem_limit_bytes=VMEM_LIMIT),
        name="grads_to_float32",
    )(totals, output, grad_tok, adaw, g_mlp, g_mlp, g_att, g_att)


def per_device(
    dp, tokens, lengths, time, qkv_weight, out_weight, up_weight, up_bias, down_weight, down_bias,
    gain_attn, gain_mlp, ada_weight, ada_bias, cotangent,
):
    model, local = tokens.shape[1], out_weight.shape[0]
    cond = ada_weight.shape[0]
    qkv = jnp.transpose(qkv_weight, (1, 2, 0))
    ada = jnp.transpose(ada_weight, (1, 0, 2)).reshape(6 * cond, model)
    half = cond // 2
    freq = np.exp(np.arange(half) * (-math.log(10000.0) / half)).astype(np.float32)
    freq = jnp.asarray(np.concatenate([freq, freq])[None])
    inverse = jnp.asarray(np.exp(np.arange(HALF) * (-2.0 * math.log(10000.0) / HEAD_DIM)).astype(np.float32)[:, None])
    output, grad_tok, g_mlp, g_att, _, g_ada, totals = block_call(
        dp, lengths, time, [tokens, cotangent, qkv, out_weight, up_weight, down_weight, ada],
        [gain_attn, gain_mlp, up_bias, down_bias, ada_bias, freq, inverse],
    )
    output, grad_tok, g_ada, g_up, g_down, g_qkv, g_out, g_adab, g_gain1, g_gain2, g_downb, g_upb = finish_call(
        totals, output, grad_tok, g_ada, g_mlp, g_att, up_bias.shape[0], local
    )
    return (
        output,
        grad_tok,
        jnp.transpose(g_qkv.reshape(3, local, model), (2, 0, 1)),
        g_out,
        g_up,
        g_upb,
        g_down,
        g_downb,
        g_gain1,
        g_gain2,
        jnp.transpose(g_ada.reshape(6, cond, model), (1, 0, 2)),
        g_adab,
    )


def solution(mesh):
    in_specs = (
        P("dp", None), P("dp", None), P("dp"), P(None, None, "tensor"), P("tensor", None), P(None, "tensor"),
        P("tensor"), P("tensor", None), P(), P(), P(), P(), P(), P("dp", None),
    )
    out_specs = (
        P("dp", None), P("dp", None), P(None, None, "tensor"), P("tensor", None), P(None, "tensor"), P("tensor"),
        P("tensor", None), P(), P(), P(), P(), P(),
    )
    return jax.shard_map(
        functools.partial(per_device, mesh.shape["dp"]),
        mesh=mesh, in_specs=in_specs, out_specs=out_specs, check_vma=False,
    )
```

```python
import functools
import math

import jax
import jax.numpy as jnp
import numpy as np
from jax import lax
from jax.experimental import pallas as pl
from jax.experimental.pallas import tpu as pltpu
from jax.sharding import PartitionSpec as P

HEAD_DIM = 64
HALF = HEAD_DIM // 2
EPS = 1e-05
ROWS = 256
PRECISE = lax.Precision.HIGHEST
GROUP = 16
LONGEST = 512
VMEM_LIMIT = 61 * 1024 * 1024
F32 = jnp.float32
BF16 = jnp.bfloat16
GELU_A = math.sqrt(2.0 / math.pi)
GELU_B = 0.044715

NN = (((1,), (0,)), ((), ()))
NT = (((1,), (1,)), ((), ()))
TN = (((0,), (0,)), ((), ()))


def mm(left, right, dims=NN):
    return lax.dot_general(left, right, dims, preferred_element_type=F32)


def norm_parts(v):
    center = jnp.mean(v, axis=-1, keepdims=True)
    centered = v - center
    spread = jnp.mean(centered * centered, axis=-1, keepdims=True)
    rstd = lax.rsqrt(spread + EPS)
    return centered * rstd, rstd


def only_half(block, second):
    zero = jnp.zeros_like(block)
    return jnp.concatenate([zero, block] if second else [block, zero], axis=0)


MESH = pl.DeviceIdType.MESH


def bit_of(index, bit):
    return lax.rem(index // (1 << bit), 2)


def flip(index, bit):
    return index + (1 << bit) * (1 - 2 * bit_of(index, bit))


class Reduce:
    def __init__(self, total, base, rows, inbox, inbase, order, final, send, recv, first_sem):
        self.total, self.base, self.inbox, self.send, self.recv = total, base, inbox, send, recv
        self.final = final
        self.plan, self.sem = [], first_sem
        size, halved = rows, []
        for bit in order:
            if size % 32 == 0:
                self.plan.append(("halve", bit, size // 2, inbase, list(halved)))
                size //= 2
                halved.append((bit, size))
            else:
                self.plan.append(("whole", bit, size, inbase, list(halved)))
            inbase += size
        self.inend = inbase
        while halved:
            bit, size = halved.pop()
            self.plan.append(("double", bit, size, None, list(halved)))
        self.steps = len(self.plan)
        self.turn = next((n for n, step in enumerate(self.plan) if step[0] == "double"), self.steps)

    def offset(self, halved):
        me = lax.axis_index("dp")
        at = self.base
        for bit, size in halved:
            at = at + bit_of(me, bit) * size
        return at

    def copy(self, n):
        kind, bit, size, inbase, halved = self.plan[n]
        me = lax.axis_index("dp")
        start = self.offset(halved)
        if kind == "halve":
            source = start + (1 - bit_of(me, bit)) * size
        elif kind == "whole":
            source = start
        else:
            source = start + bit_of(me, bit) * size
        origin = self.final if kind == "double" and n > self.turn else self.total
        block = pl.ds(pl.multiple_of(source, 16), size)
        return pltpu.make_async_remote_copy(
            src_ref=origin.at[block],
            dst_ref=self.final.at[block] if kind == "double" else self.inbox.at[pl.ds(inbase, size)],
            send_sem=self.send.at[self.sem + n],
            recv_sem=self.recv.at[self.sem + n],
            device_id={"dp": flip(me, bit)},
            device_id_type=MESH,
        )

    def store(self):
        at = self.offset(self.plan[self.turn - 1][4])
        kind, bit, size = self.plan[self.turn - 1][:3]
        if kind == "halve":
            at = at + bit_of(lax.axis_index("dp"), bit) * size
        block = pl.ds(pl.multiple_of(at, 16), size)
        return pltpu.make_async_copy(self.total.at[block], self.final.at[block], self.send.at[self.sem + self.steps])

    def start(self, n):
        if n < self.steps:
            self.copy(n).start()

    def finish(self, n):
        if n >= self.steps:
            return
        self.copy(n).wait()
        kind, bit, size, inbase, halved = self.plan[n]
        if kind == "double":
            if n == self.turn:
                self.store().wait()
            return
        keep = self.offset(halved)
        if kind == "halve":
            keep = keep + bit_of(lax.axis_index("dp"), bit) * size
        tile = next(t for t in (128, 96, 64, 48, 32, 16, size) if size % t == 0)

        @pl.loop(0, size // tile)
        def _(j):
            mine = pl.ds(pl.multiple_of(keep + j * tile, 16), tile)
            came = pl.ds(pl.multiple_of(inbase + j * tile, 16), tile)
            added = self.total[mine, :].astype(F32) + self.inbox[came, :].astype(F32)
            self.total[mine, :] = added.astype(BF16)

        if n + 1 == self.turn:
            self.store().start()
            if self.turn == self.steps:
                self.store().wait()


class Gather:
    def __init__(self, rows, dp, send, recv, first_sem):
        self.rows, self.send, self.recv, self.sem = rows, send, recv, first_sem
        self.bits = list(reversed(range(dp.bit_length() - 1))) + [None]
        self.steps = len(self.bits)

    def place(self):
        at, weight = 0, 1
        for bit in self.bits:
            index = lax.axis_index("tensor") if bit is None else lax.axis_index("dp")
            at = at + bit_of(index, bit or 0) * weight
            weight *= 2
        return at

    def own(self, row, sem):
        store = pltpu.make_async_copy(row, self.rows.at[self.place()], sem)
        store.start()
        store.wait()

    def copy(self, n):
        bit, size = self.bits[n], 1 << n
        block = self.rows.at[pl.ds((self.place() // size) * size, size)]
        axis = "tensor" if bit is None else "dp"
        return pltpu.make_async_remote_copy(
            src_ref=block,
            dst_ref=block,
            send_sem=self.send.at[self.sem + n],
            recv_sem=self.recv.at[self.sem + n],
            device_id={axis: flip(lax.axis_index(axis), bit or 0)},
            device_id_type=MESH,
        )

    def start(self, n):
        if n < self.steps:
            self.copy(n).start()

    def finish(self, n):
        if n < self.steps:
            self.copy(n).wait()


def norm_back(gn, xhat, rstd, gain):
    y = gn * gain
    mean_y = jnp.mean(y, axis=-1, keepdims=True)
    mean_yx = jnp.mean(y * xhat, axis=-1, keepdims=True)
    return rstd * (y - mean_y - xhat * mean_yx)


def col_sum(v):
    return jnp.sum(v, axis=0, keepdims=True)


class Steps:
    def __init__(self, *streams):
        self.streams, self.done = streams, [0] * len(streams)

    def start(self):
        for stream in self.streams:
            stream.start(0)

    def advance(self):
        for n, stream in enumerate(self.streams):
            if self.done[n] < stream.steps:
                stream.finish(self.done[n])
                stream.start(self.done[n] + 1)
                self.done[n] += 1

    def busy(self):
        return any(done < stream.steps for done, stream in zip(self.done, self.streams))


def block_kernel(
    dp, lengths, time, tok_h, cot_h, qkv_h, out_wh, up_h, dn_h, ada_h, gain1_i, gain2_i, bias_i, downb_i, adab_i,
    freq, inverse,
    out_h, gtok_h, gmlp_h, gatt_h, rows_h, adaw_h, totals_o,
    tok, cot, qkv_s, out_s, w_s, n2, act, pre, gml, br_own, br_par, ml_own, ml_par, gn_own, gn_par, gn1_par,
    gmid, dk, dv, gproj, qt, kt, q, k, v, att, normed, stat, cos_s, sin_s, bound, mod, small, small_par,
    box1, box2, inbox1, inbox2, vec_own, vec_par, row_own, rows_s, sums,
    load_sem, y_send, y_recv, c_send, c_recv, d_send, d_recv, o_sem,
):
    length, model = tok.shape
    local = out_wh.shape[0]
    hidden = up_h.shape[1]
    cond = freq.shape[1]
    width = 2 * local
    heads = width // HEAD_DIM
    chunks = length // ROWS
    tensor, here_dp = lax.axis_index("tensor"), lax.axis_index("dp")
    core = lax.rem(tensor, 2)
    other_core, other_y = flip(tensor, 0), flip(tensor, 1)
    bits = dp.bit_length() - 1
    scale = 1.0 / math.sqrt(HEAD_DIM)
    vt = gproj.at[pl.ds(2 * width, width)]

    barrier = pltpu.get_barrier_semaphore()
    for peer in [{"tensor": other_core}, {"tensor": other_y}] + [{"dp": flip(here_dp, b)} for b in range(bits)]:
        pl.semaphore_signal(barrier, inc=1, device_id=peer, device_id_type=MESH)

    mine_rows = pl.ds(pl.multiple_of(core * length, 16), length)
    moves = (
        (ada_h, act.at[pl.ds(0, ada_h.shape[0]), pl.ds(0, model)]),
        (tok_h.at[mine_rows], tok),
        (qkv_h, qkv_s.at[:, pl.ds(0, local)]),
        (out_wh, out_s.at[pl.ds(0, local)]),
        (up_h, w_s.at[pl.ds(0, model)]),
        (dn_h, w_s.at[pl.ds(2 * model, hidden)]),
        (cot_h.at[mine_rows], cot),
    )
    loads = [pltpu.make_async_copy(source, target, load_sem.at[n]) for n, (source, target) in enumerate(moves)]
    for load in loads:
        load.start()

    def rows_of(i):
        return pl.ds(pl.multiple_of(i * ROWS, ROWS), ROWS)

    def to_y(source, target, n):
        return pltpu.make_async_remote_copy(
            src_ref=source, dst_ref=target, send_sem=y_send.at[n], recv_sem=y_recv.at[n],
            device_id={"tensor": other_y}, device_id_type=MESH,
        )

    def to_core(source, target, n):
        return pltpu.make_async_remote_copy(
            src_ref=source, dst_ref=target, send_sem=c_send.at[n], recv_sem=c_recv.at[n],
            device_id={"tensor": other_core}, device_id_type=MESH,
        )

    def br_copy(i):
        return to_y(br_own.at[rows_of(i)], br_par.at[rows_of(i)], i)

    def gn_copy(i):
        return to_y(gn_own.at[rows_of(i)], gn_par.at[rows_of(i)], chunks + i)

    def ml_copy(i):
        return to_y(ml_own.at[rows_of(i)], ml_par.at[rows_of(i)], 2 * chunks + i)

    def gn1_copy(i):
        return to_y(n2.at[rows_of(i)], gn1_par.at[rows_of(i)], 3 * chunks + i)

    def vec_copy(n):
        return to_y(vec_own.at[n], vec_par.at[n], 4 * chunks + n)

    for n, ref in enumerate((gain1_i, gain2_i, bias_i, downb_i)):
        small[n : n + 1, : ref.shape[0]] = ref[...].astype(F32).reshape(1, ref.shape[0])
    small[4:10, :] = adab_i[...].astype(F32)
    shares = [
        to_core(qkv_h, qkv_s.at[:, pl.ds(local, local)], 0),
        to_core(out_wh, out_s.at[pl.ds(local, local)], 1),
        to_core(small, small_par, 2),
        to_core(up_h, w_s.at[pl.ds(model, model)], 3),
        to_core(dn_h, w_s.at[pl.ds(2 * model + hidden, hidden)], 4),
    ]
    pl.semaphore_wait(barrier, 2 + bits)
    for share in shares:
        share.start()

    gain1, gain2, downb = small[0:1, :], small[1:2, :], small[3:4, :]
    when = time[core].astype(F32)
    angle = jnp.broadcast_to(freq[...] * when, (8, cond))
    lane = lax.broadcasted_iota(jnp.int32, (8, cond), 1)
    feats = jnp.where(lane < cond // 2, jnp.cos(angle), jnp.sin(angle))
    high = feats.astype(BF16)
    rest = feats - high.astype(F32)
    middle_part = rest.astype(BF16)
    low_part = (rest - middle_part.astype(F32)).astype(BF16)
    sums[...] = jnp.zeros_like(sums)
    vec_own[...] = jnp.zeros_like(vec_own)
    row_own[...] = jnp.zeros_like(row_own)
    row_own[11:12, :cond] = feats[0:1, :]
    place = lax.broadcasted_iota(jnp.int32, (8, length), 1)
    start, begin, end = jnp.int32(0), jnp.zeros((8, length), jnp.int32), jnp.zeros((8, length), jnp.int32)
    for n in range(lengths.shape[1]):
        size = lengths[core, n]
        end = end + jnp.where(place >= start, size, 0)
        start = start + size
        begin = begin + jnp.where(place >= start, size, 0)
    bound[0:8, :] = begin
    bound[8:16, :] = end
    turns = inverse[...] * (place - begin)[0:1, :].astype(F32)
    cos_s[...] = jnp.cos(turns)
    sin_s[...] = jnp.sin(turns)
    loads[0].wait()
    for j in range(6):
        ada = act[j * cond : (j + 1) * cond, :model]
        vec = mm(high, ada) + mm(middle_part, ada) + mm(low_part, ada)
        mod[j : j + 1, :] = vec[0:1, :] + small[4 + j : 5 + j, :]
    for n in (1, 2):
        loads[n].wait()
    shares[0].wait()

    def project(i):
        r = rows_of(i)
        xhat, _ = norm_parts(tok[r, :].astype(F32))
        x1 = (xhat * gain1 * (1.0 + mod[1:2, :]) + mod[0:1, :]).astype(BF16)
        normed[r, :] = x1
        c, s = cos_s[:, r], sin_s[:, r]
        for part, (t_o, r_o) in enumerate(((qt, q), (kt, k), (vt, v))):
            turned = mm(qkv_s[part], x1, NT)
            if part < 2:
                pieces = []
                for h in range(heads):
                    a = turned[h * HEAD_DIM : h * HEAD_DIM + HALF]
                    b = turned[h * HEAD_DIM + HALF : (h + 1) * HEAD_DIM]
                    pieces += [a * c - b * s, b * c + a * s]
                turned = jnp.concatenate(pieces, axis=0)
            if part == 0:
                turned = turned * scale
            t_o[:, r] = turned.astype(BF16)
            r_o[r, :] = turned.T.astype(BF16)

    def allowed_keys(r, keys):
        place = lax.broadcasted_iota(jnp.int32, (keys.size, ROWS), 0) + keys.start
        return (place >= bound[0:1, r]) & (place < bound[8:9, r])

    def attend(i, keys):
        r = rows_of(i)
        allowed = allowed_keys(r, keys)
        for h in range(heads):
            pair = slice((h // 2) * 2 * HEAD_DIM, (h // 2 + 1) * 2 * HEAD_DIM)
            mine = slice(h * HEAD_DIM, (h + 1) * HEAD_DIM)
            scores = mm(k[keys, pair], only_half(qt[mine, r], h % 2))
            scores = jnp.where(allowed, scores, -1000000000.0)
            top = jnp.max(scores, axis=0, keepdims=True)
            terms = jnp.exp(scores - top)
            inv = 1.0 / jnp.sum(terms, axis=0, keepdims=True)
            att[mine, r] = (mm(vt[mine, keys], terms.astype(BF16)) * inv).astype(BF16)
            stat[h : h + 1, r] = top
            stat[8 + h : 9 + h, r] = inv
        br_own[r, :] = mm(att[:, r], out_s[...], TN).astype(BF16)
        br_copy(i).start()

    reach = min(length, ROWS + LONGEST)
    first_keys, last_keys = pl.ds(0, reach), pl.ds(length - reach, reach)

    pl.loop(0, reach // ROWS)(project)
    loads[3].wait()
    shares[1].wait()
    attend(0, first_keys)
    pl.loop(reach // ROWS, chunks)(project)

    @pl.loop(1, chunks - 1)
    def _(i):
        attend(i, pl.ds(0, length))

    attend(chunks - 1, last_keys)

    for n in (4, 5, 6):
        loads[n].wait()
    for n in (2, 3, 4):
        shares[n].wait()

    @pl.loop(0, chunks)
    def _(i):
        r = rows_of(i)
        br_copy(i).wait_recv()
        middle = tok[r, :].astype(F32) + mod[2:3, :] * (br_own[r, :].astype(F32) + br_par[r, :].astype(F32))
        xhat, _ = norm_parts(middle)
        x2 = (xhat * gain2 * (1.0 + mod[4:5, :]) + mod[3:4, :]).astype(BF16)
        n2[r, :] = x2
        grad_out = cot[r, :].astype(F32)
        g = (mod[5:6, :] * grad_out).astype(BF16)
        gml[r, :] = g
        part = jnp.zeros((ROWS, model), F32)
        grad = jnp.zeros((ROWS, model), F32)
        for n in range(2):
            up, down = w_s.at[pl.ds(n * model, model)], w_s.at[pl.ds(2 * model + n * hidden, hidden)]
            cols = slice(n * hidden, (n + 1) * hidden)
            z = mm(x2, up[...]) + (small_par if n else small)[2:3, :hidden]
            square = z * z
            t = jnp.tanh(GELU_A * z * (1.0 + GELU_B * square))
            a = (0.5 * z * (1.0 + t)).astype(BF16)
            act[r, cols] = a
            slope = 0.5 * (1.0 + t) + (0.5 * GELU_A) * z * (1.0 - t * t) * (1.0 + 3.0 * GELU_B * square)
            part = part + mm(a, down[...])
            p = (mm(g, down[...], NT) * slope).astype(BF16)
            pre[r, cols] = p
            sums[n : n + 1, :hidden] += col_sum(p.astype(F32))
            grad = grad + mm(p, up[...], NT)
        ml_own[r, :] = part.astype(BF16)
        gn_own[r, :] = grad.astype(BF16)
        vec_own[0, 0:1, :] += col_sum(grad_out * part)
        sums[2:3, :] += col_sum(grad_out)
        gn_copy(i).start()

    vec_copy(0).start()

    def up_grad(j, n):
        cols = pl.ds(pl.multiple_of(j * ROWS, ROWS), ROWS)
        return mm(n2[:, cols], pre[:, n * hidden : (n + 1) * hidden], TN)

    def down_grad(j, n):
        cols = pl.ds(pl.multiple_of(n * hidden + j * ROWS, ROWS), ROWS)
        return mm(act[:, cols], gml[...], TN)

    outbox = w_s.at[pl.ds(2 * model, model + hidden)]

    @pl.loop(0, model // ROWS)
    def _(j):
        outbox[rows_of(j), :] = up_grad(j, 1).astype(BF16)

    up_copy = to_core(outbox.at[pl.ds(0, model)], box1.at[pl.ds(0, model)], 5)
    up_copy.start()

    @pl.loop(0, hidden // ROWS)
    def _(j):
        outbox[pl.ds(pl.multiple_of(model + j * ROWS, ROWS), ROWS), :] = down_grad(j, 1).astype(BF16)

    down_copy = to_core(outbox.at[pl.ds(model, hidden)], box1.at[pl.ds(model, hidden)], 6)
    down_copy.start()
    up_copy.wait()

    @pl.loop(0, model // ROWS)
    def _(j):
        r = rows_of(j)
        w_s[r, :] = (up_grad(j, 0) + box1[r, :].astype(F32)).astype(BF16)

    order = list(range(bits))
    turned_order = order[1:2] + order[:1] + order[2:]
    orders = (order, turned_order)
    used = [0]

    def streams(total, base, rows, count, shift, inbox, inbase, final):
        made = []
        for n in range(count):
            size = rows // count
            made.append(
                Reduce(total, base + n * size, size, inbox, inbase, orders[(n + shift) % 2], final, d_send, d_recv, used[0])
            )
            inbase = made[-1].inend
            used[0] += made[-1].steps + 1
        return made, inbase

    red_up, inbase = streams(w_s, 0, model, 2, 0, inbox1, 0, gmlp_h)
    for stream in red_up:
        stream.start(0)
    down_copy.wait()

    @pl.loop(0, hidden // ROWS)
    def _(j):
        r = pl.ds(pl.multiple_of(model + j * ROWS, ROWS), ROWS)
        w_s[r, :] = (down_grad(j, 0) + box1[r, :].astype(F32)).astype(BF16)

    red_down, _ = streams(w_s, model, hidden, 2, 0, inbox1, inbase, gmlp_h)
    for stream in red_down:
        stream.start(0)
    mlp_sums = Steps(*red_up, *red_down)

    dk[...] = jnp.zeros_like(dk)
    dv[...] = jnp.zeros_like(dv)

    @pl.loop(0, chunks)
    def _(i):
        r = rows_of(i)
        gn_copy(i).wait_recv()

        @pl.when(i == chunks - 1)
        def _():
            for n in range(chunks - 1):
                ml_copy(n).start()

        branch = br_own[r, :].astype(F32) + br_par[r, :].astype(F32)
        xhat, rstd = norm_parts(tok[r, :].astype(F32) + mod[2:3, :] * branch)
        gn = gn_own[r, :].astype(F32) + gn_par[r, :].astype(F32)
        g = cot[r, :].astype(F32) + norm_back(gn, xhat, rstd, (1.0 + mod[4:5, :]) * gain2)
        gmid[r, :] = g
        sums[3:4, :] += col_sum(gn)
        sums[4:5, :] += col_sum(gn * xhat)
        sums[5:6, :] += col_sum(g * branch)
        gb = (mod[2:3, :] * g).astype(BF16)
        gml[r, :] = gb
        do_t = mm(out_s[...], gb, NT).astype(BF16)
        do = mm(gb, out_s[...], NT).astype(BF16)
        allowed = allowed_keys(r, pl.ds(0, length))
        lane = lax.broadcasted_iota(jnp.int32, (ROWS, 2 * HEAD_DIM), 1)
        c, s = cos_s[:, r], sin_s[:, r]
        for p in range(heads // 2):
            pair = slice(p * 2 * HEAD_DIM, (p + 1) * 2 * HEAD_DIM)
            dk_sum, dv_sum = dk[:, pair], dv[:, pair]
            for n in range(2):
                h = 2 * p + n
                mine = slice(h * HEAD_DIM, (h + 1) * HEAD_DIM)
                scores = mm(k[:, pair], only_half(qt[mine, r], n))
                probs = jnp.where(allowed, jnp.exp(scores - stat[h : h + 1, r]), 0.0) * stat[8 + h : 9 + h, r]
                grad_p = mm(v[:, pair], only_half(do_t[mine, :], n))
                centre = col_sum(probs * grad_p)
                grad_s = (probs * (grad_p - centre)).astype(BF16)
                dq = mm(kt[mine, :], grad_s) * scale
                ua, ub = dq[:HALF], dq[HALF:]
                gproj[h * HEAD_DIM : h * HEAD_DIM + HALF, r] = (ua * c + ub * s).astype(BF16)
                gproj[h * HEAD_DIM + HALF : (h + 1) * HEAD_DIM, r] = (ub * c - ua * s).astype(BF16)
                here = (lane >= HEAD_DIM) if n else (lane < HEAD_DIM)
                none = jnp.zeros((ROWS, 2 * HEAD_DIM), BF16)
                dk_sum = dk_sum + mm(grad_s, jnp.where(here, q[r, pair], none))
                dv_sum = dv_sum + mm(probs.astype(BF16), jnp.where(here, do[:, pair], none))
            dk[:, pair] = dk_sum
            dv[:, pair] = dv_sum
        for step, n in enumerate((chunks - 3, chunks - 2)):

            @pl.when(i == n)
            def _():
                for stream in mlp_sums.streams:
                    stream.finish(step)
                    stream.start(step + 1)

    mlp_sums.done = [2] * len(mlp_sums.streams)

    vec_copy(0).wait()
    row_own[0:1, :] = sums[3:4, :]
    row_own[1:2, :] = sums[4:5, :] * gain2
    row_own[2:3, :] = sums[5:6, :]
    row_own[3:4, :] = vec_own[0, 0:1, :] + vec_par[0, 0:1, :] + sums[2:3, :] * downb
    row_own[4:5, :] = mod[5:6, :] * sums[2:3, :]
    row_own[5:6, :] = (1.0 + mod[4:5, :]) * sums[4:5, :]
    row_own[6:7, :] = jnp.where(core == 0, sums[0:1, :], sums[1:2, :])
    row_own[7:8, :] = jnp.where(core == 0, sums[1:2, :], sums[0:1, :])
    for n in range(chunks):
        br_copy(n).wait_send()
        gn_copy(n).wait_send()

    @pl.loop(0, chunks)
    def _(i):
        r = rows_of(i)
        c, s = cos_s[:, r], sin_s[:, r]
        turned = dk[r, :].T
        pieces = []
        for h in range(heads):
            ua = turned[h * HEAD_DIM : h * HEAD_DIM + HALF]
            ub = turned[h * HEAD_DIM + HALF : (h + 1) * HEAD_DIM]
            pieces += [ua * c + ub * s, ub * c - ua * s]
        gproj[width : 2 * width, r] = jnp.concatenate(pieces, axis=0).astype(BF16)
        gproj[2 * width :, r] = dv[r, :].T.astype(BF16)

    sent2 = w_s.at[pl.ds(2 * model, 4 * local)]
    gatt = w_s.at[pl.ds(2 * model + 4 * local, 4 * local)]

    def att_grads(n):
        for part in range(3):
            rows = slice((2 * part + n) * local, (2 * part + n + 1) * local)
            yield mm(gproj[rows, :], normed[...])
        yield mm(att[n * local : (n + 1) * local, :], gml[...])

    for part, piece in enumerate(att_grads(1)):
        sent2[part * local : (part + 1) * local, :] = piece.astype(BF16)
    att_copy = to_core(sent2, box2, 7)
    att_copy.start()
    mlp_sums.advance()

    for part, piece in enumerate(att_grads(0)):
        gatt[part * local : (part + 1) * local, :] = piece.astype(BF16)
    att_copy.wait()
    for part in range(4):
        rows = slice(part * local, (part + 1) * local)
        gatt[rows, :] = (gatt[rows, :].astype(F32) + box2[rows, :].astype(F32)).astype(BF16)
    red_att, _ = streams(gatt, 0, 4 * local, 2, 0, inbox2, 0, gatt_h)
    att_sums = Steps(*red_att)
    att_sums.start()

    @pl.loop(0, chunks)
    def _(i):
        r = rows_of(i)
        gn = jnp.zeros((ROWS, model), F32)
        for part in range(3):
            gn = gn + mm(gproj[part * width : (part + 1) * width, r], qkv_s[part], TN)
        n2[r, :] = gn.astype(BF16)
        xhat, _ = norm_parts(tok[r, :].astype(F32))
        vec_own[1, 0:1, :] += col_sum(gn)
        vec_own[1, 1:2, :] += col_sum(gn * xhat)

    vec_copy(1).start()
    for n in range(chunks):
        gn1_copy(n).start()
    ml_copy(chunks - 1).start()
    slot_rows = Gather(rows_h, dp, d_send, d_recv, used[0])
    row_steps = Steps(slot_rows)

    out_copies = []

    def hand_over(source, target, i, n):
        rows = pl.ds(pl.multiple_of(core * length + i * ROWS, 16), ROWS)
        keep = pltpu.make_async_copy(source, target.at[rows], o_sem.at[n])
        give = to_core(source, target.at[rows], 8 + n)
        keep.start()
        give.start()
        out_copies.append((keep, give))

    def output_chunk(i):
        r = slice(i * ROWS, (i + 1) * ROWS)
        ml_copy(i).wait()
        middle = tok[r, :].astype(F32) + mod[2:3, :] * (br_own[r, :].astype(F32) + br_par[r, :].astype(F32))
        total = ml_own[r, :].astype(F32) + ml_par[r, :].astype(F32) + downb
        act[r, :model] = (middle + mod[5:6, :] * total).astype(BF16)
        hand_over(act.at[r, :model], out_h, i, i)

    def token_chunk(i):
        r = slice(i * ROWS, (i + 1) * ROWS)
        gn1_copy(i).wait()
        xhat, rstd = norm_parts(tok[r, :].astype(F32))
        gn = n2[r, :].astype(F32) + gn1_par[r, :].astype(F32)
        g = gmid[r, :] + norm_back(gn, xhat, rstd, (1.0 + mod[1:2, :]) * gain1)
        act[r, model : 2 * model] = g.astype(BF16)
        hand_over(act.at[r, model : 2 * model], gtok_h, i, chunks + i)

    att_sums.advance()
    vec_copy(1).wait()
    shift_a = vec_own[1, 0:1, :] + vec_par[1, 0:1, :]
    scale_a = vec_own[1, 1:2, :] + vec_par[1, 1:2, :]
    row_own[8:9, :] = shift_a
    row_own[9:10, :] = scale_a * gain1
    row_own[10:11, :] = (1.0 + mod[1:2, :]) * scale_a
    slot_rows.own(row_own, load_sem.at[1])
    slot_rows.start(0)
    output_chunk(0)
    att_sums.advance()
    output_chunk(1)
    mlp_sums.advance()
    att_sums.advance()
    row_steps.advance()
    for i in range(2, chunks - 1):
        output_chunk(i)
    mlp_sums.advance()
    att_sums.advance()
    row_steps.advance()
    token_chunk(0)
    att_sums.advance()
    row_steps.advance()
    token_chunk(1)
    while row_steps.busy():
        row_steps.advance()

    slots = 2 * dp
    group = min(slots, GROUP)
    totals_o[...] = jnp.zeros_like(totals_o)
    picks = ((1, 0), (1, 1), (0, 2), (0, 0), (0, 1), (0, 3))
    for first_slot in range(0, slots, group):
        take = pltpu.make_async_copy(rows_h.at[pl.ds(first_slot, group)], rows_s, load_sem.at[0])
        take.start()
        take.wait()

        def pick(n, row):
            return jnp.concatenate([rows_s[g, 8 * n + row : 8 * n + row + 1, :] for g in range(group)], axis=0)

        feat = pick(1, 3)[:, :cond]
        for j, (n, row) in enumerate(picks):
            vecs = pick(n, row)
            totals_o[j : j + 1, :] += col_sum(vecs)
            outer = lax.dot_general(feat, vecs, TN, precision=PRECISE, preferred_element_type=F32)
            rows = slice(j * cond, (j + 1) * cond)
            for side, ref in enumerate((dk, dv)):
                cut = outer[:, side * width : (side + 1) * width]
                ref[rows, :] = cut if first_slot == 0 else ref[rows, :] + cut
        totals_o[6:7, :] += col_sum(pick(1, 2))
        totals_o[7:8, :] += col_sum(pick(0, 5))
        totals_o[8:9, :] += col_sum(pick(0, 4))
        totals_o[9:10, :] += jnp.where(core == 0, col_sum(pick(0, 6)), col_sum(pick(0, 7)))
    puts = [
        pltpu.make_async_copy(
            ref.at[pl.ds(0, 6 * cond)], adaw_h.at[:, pl.ds(side * width, width)], load_sem.at[2 + side]
        )
        for side, ref in enumerate((dk, dv))
    ]
    for put in puts:
        put.start()

    att_sums.advance()
    for i in range(2, chunks):
        token_chunk(i)
    output_chunk(chunks - 1)
    while mlp_sums.busy() or att_sums.busy():
        mlp_sums.advance()
        att_sums.advance()
    for put in puts:
        put.wait()
    for keep, give in out_copies:
        keep.wait()
        give.wait()


def block_call(dp, lengths, time, hbm, small):
    tokens, _, qkv_w, out_w, up_w, down_w, ada = hbm
    slot_count, model = time.shape[0], tokens.shape[1]
    length = tokens.shape[0] // slot_count
    hidden, local = up_w.shape[1], out_w.shape[0]
    width = 2 * local
    chunks = length // ROWS
    slots = slot_count * dp
    sems = 7 * (2 * dp.bit_length()) + dp.bit_length()
    any_spec, vmem_spec = pl.BlockSpec(memory_space=pl.ANY), pl.BlockSpec(memory_space=pltpu.VMEM)
    smem_spec = pl.BlockSpec(memory_space=pltpu.SMEM)
    inbox_rows = 2 * inbox_need(dp, model // 2) + 2 * inbox_need(dp, hidden // 2)
    inbox2_rows = 2 * inbox_need(dp, width)
    dma = pltpu.SemaphoreType.DMA

    def low(*shape):
        return pltpu.VMEM(shape, BF16)

    def full(*shape):
        return pltpu.VMEM(shape, F32)

    tokens_like = low(length, model)
    return pl.pallas_call(
        functools.partial(block_kernel, dp),
        in_specs=[smem_spec] * 2 + [any_spec] * len(hbm) + [vmem_spec] * len(small),
        out_specs=[any_spec] * 6 + [vmem_spec],
        out_shape=[
            jax.ShapeDtypeStruct(tokens.shape, BF16),
            jax.ShapeDtypeStruct(tokens.shape, BF16),
            jax.ShapeDtypeStruct((model + hidden, model), BF16),
            jax.ShapeDtypeStruct((4 * local, model), BF16),
            jax.ShapeDtypeStruct((slots, 16, model), F32),
            jax.ShapeDtypeStruct(ada.shape, F32),
            jax.ShapeDtypeStruct((16, model), F32),
        ],
        scratch_shapes=[
            tokens_like, tokens_like, low(3, width, model), low(width, model), low(2 * (model + hidden), model),
            tokens_like, low(length, 2 * hidden), low(length, 2 * hidden), tokens_like,
            tokens_like, tokens_like, tokens_like, tokens_like, tokens_like, tokens_like, tokens_like,
            full(length, model), full(length, width), full(length, width), low(3 * width, length),
            low(width, length), low(width, length), low(length, width), low(length, width), low(length, width),
            low(width, length), tokens_like, full(16, length), full(HALF, length), full(HALF, length),
            pltpu.VMEM((16, length), jnp.int32), full(8, model), full(16, model), full(16, model),
            low(model + hidden, model), low(4 * local, model), low(inbox_rows, model),
            low(inbox2_rows, model), full(2, 8, model), full(2, 8, model), full(16, model),
            full(min(slots, GROUP), 16, model), full(8, model),
            dma((7,)), dma((4 * chunks + 2,)), dma((4 * chunks + 2,)), dma((8 + 2 * chunks,)), dma((8 + 2 * chunks,)),
            dma((sems,)), dma((sems,)), dma((2 * chunks,)),
        ],
        compiler_params=pltpu.CompilerParams(
            collective_id=0, has_side_effects=True, vmem_limit_bytes=VMEM_LIMIT
        ),
        cost_estimate=pl.CostEstimate(flops=80_000_000_000, bytes_accessed=40_000_000, transcendentals=0),
        name="transformer_block",
    )(lengths, time, *hbm, *small)


def inbox_need(dp, rows):
    need = 0
    for _ in range(dp.bit_length() - 1):
        if rows % 32 == 0:
            rows //= 2
        need += rows
    return need


def finish_kernel(totals, *refs):
    *refs, adab_o, gain1_o, gain2_o, downb_o, upb_o = refs
    half = len(refs) // 2
    for source, target in zip(refs[:half], refs[half:]):
        target[...] = source[...].astype(target.dtype)
    adab_o[...] = totals[0:6, :]
    for n, ref in enumerate((gain1_o, gain2_o, downb_o, upb_o)):
        ref[...] = totals[6 + n : 7 + n, : ref.shape[0]].reshape(ref.shape[0])


def finish_call(totals, output, grad_tok, adaw, g_mlp, g_att, hidden, local):
    steps = 4
    model = output.shape[1]

    def rows(count, start=0):
        return pl.BlockSpec((count // steps, model), lambda i: (start * steps // count + i, 0))

    def vector(count):
        return pl.BlockSpec((count,), lambda i: (0,))

    whole = [a.shape[0] for a in (output, grad_tok, adaw)]
    parts = ((model, 0), (hidden, model), (3 * local, 0), (local, 3 * local))
    vectors = (model, model, model, hidden)
    return pl.pallas_call(
        finish_kernel,
        grid=(steps,),
        in_specs=[pl.BlockSpec(totals.shape, lambda i: (0, 0))]
        + [rows(count) for count in whole]
        + [rows(*part) for part in parts],
        out_specs=[rows(count) for count in whole]
        + [rows(count) for count, _ in parts]
        + [pl.BlockSpec((6, model), lambda i: (0, 0))]
        + [vector(count) for count in vectors],
        out_shape=[jax.ShapeDtypeStruct(a.shape, a.dtype) for a in (output, grad_tok, adaw)]
        + [jax.ShapeDtypeStruct((count, model), F32) for count, _ in parts]
        + [jax.ShapeDtypeStruct((6, model), F32)]
        + [jax.ShapeDtypeStruct((count,), F32) for count in vectors],
        compiler_params=pltpu.CompilerParams(vmem_limit_bytes=VMEM_LIMIT),
        name="grads_to_float32",
    )(totals, output, grad_tok, adaw, g_mlp, g_mlp, g_att, g_att)


def per_device(
    dp, tokens, lengths, time, qkv_weight, out_weight, up_weight, up_bias, down_weight, down_bias,
    gain_attn, gain_mlp, ada_weight, ada_bias, cotangent,
):
    model, local = tokens.shape[1], out_weight.shape[0]
    cond = ada_weight.shape[0]
    qkv = jnp.transpose(qkv_weight, (1, 2, 0))
    ada = jnp.transpose(ada_weight, (1, 0, 2)).reshape(6 * cond, model)
    half = cond // 2
    freq = np.exp(np.arange(half) * (-math.log(10000.0) / half)).astype(np.float32)
    freq = jnp.asarray(np.concatenate([freq, freq])[None])
    inverse = jnp.asarray(np.exp(np.arange(HALF) * (-2.0 * math.log(10000.0) / HEAD_DIM)).astype(np.float32)[:, None])
    output, grad_tok, g_mlp, g_att, _, g_ada, totals = block_call(
        dp, lengths, time, [tokens, cotangent, qkv, out_weight, up_weight, down_weight, ada],
        [gain_attn, gain_mlp, up_bias, down_bias, ada_bias, freq, inverse],
    )
    output, grad_tok, g_ada, g_up, g_down, g_qkv, g_out, g_adab, g_gain1, g_gain2, g_downb, g_upb = finish_call(
        totals, output, grad_tok, g_ada, g_mlp, g_att, up_bias.shape[0], local
    )
    return (
        output,
        grad_tok,
        jnp.transpose(g_qkv.reshape(3, local, model), (2, 0, 1)),
        g_out,
        g_up,
        g_upb,
        g_down,
        g_downb,
        g_gain1,
        g_gain2,
        jnp.transpose(g_ada.reshape(6, cond, model), (1, 0, 2)),
        g_adab,
    )


def solution(mesh):
    in_specs = (
        P("dp", None), P("dp", None), P("dp"), P(None, None, "tensor"), P("tensor", None), P(None, "tensor"),
        P("tensor"), P("tensor", None), P(), P(), P(), P(), P(), P("dp", None),
    )
    out_specs = (
        P("dp", None), P("dp", None), P(None, None, "tensor"), P("tensor", None), P(None, "tensor"), P("tensor"),
        P("tensor", None), P(), P(), P(), P(), P(),
    )
    return jax.shard_map(
        functools.partial(per_device, mesh.shape["dp"]),
        mesh=mesh, in_specs=in_specs, out_specs=out_specs, check_vma=False,
    )
```
